32 devices in a mesh: dp: 16 (over z, y, x), mp: 2 (over core).
Axes of the slice: x: 2, y: 2, z: 4, core: 2. Of those that a mesh axis runs over, the one named last changes fastest.
Arguments:
- tokens: bfloat16 [32768, 768], P(('dp', 'mp')), may hold values from -6 to 6
- norm1_gain: float32 [768], replicated, may hold values from 0.1 to 1.9
- norm1_shift: float32 [768], replicated, may hold values from -3 to 3
- w_query: bfloat16 [768, 768], P('dp', 'mp'), may hold values from -0.21875 to 0.21875
- w_key: bfloat16 [768, 768], P('dp', 'mp'), may hold values from -0.21875 to 0.21875
- w_value: bfloat16 [768, 768], P('dp', 'mp'), may hold values from -0.21875 to 0.21875
- w_out: bfloat16 [768, 768], P('dp', 'mp'), may hold values from -3.5 to 3.5
- fmap_query: bfloat16 [12, 64, 64], P('mp'), may hold values from -0.75 to 0.75
- fmap_key: bfloat16 [12, 64, 64], P('mp'), may hold values from -0.75 to 0.75
- norm2_gain: float32 [768], replicated, may hold values from 0.1 to 1.9
- norm2_shift: float32 [768], replicated, may hold values from -3 to 3
- w_fc: bfloat16 [768, 3072], P('dp', 'mp'), may hold values from -0.21875 to 0.21875
- w_down: bfloat16 [768, 3072], P('dp', 'mp'), may hold values from -0.109375 to 0.109375
- lengths: int32 [16, 16], P('dp'), may hold values from 0 to 1536, as said below
- cotangent: bfloat16 [32768, 768], P(('dp', 'mp')), may hold values from -6 to 6
Outputs:
- mixed: bfloat16 [32768, 768], P(('dp', 'mp'))
- grad_tokens: bfloat16 [32768, 768], P(('dp', 'mp'))
- grad_norm1_gain: float32 [768], replicated
- grad_norm1_shift: float32 [768], replicated
- grad_w_query: float32 [768, 768], P('dp', 'mp')
- grad_w_key: float32 [768, 768], P('dp', 'mp')
- grad_w_value: float32 [768, 768], P('dp', 'mp')
- grad_w_out: float32 [768, 768], P('dp', 'mp')
- grad_fmap_query: float32 [12, 64, 64], P('mp')
- grad_fmap_key: float32 [12, 64, 64], P('mp')
- grad_norm2_gain: float32 [768], replicated
- grad_norm2_shift: float32 [768], replicated
- grad_w_fc: float32 [768, 3072], P('dp', 'mp')
- grad_w_down: float32 [768, 3072], P('dp', 'mp')
The draws below stay inside these ranges and needn't reach their ends.
Inputs may be any that keep to these rules, and one draw needn't show every extreme that they name: Row b holds the lengths of the sequences packed one after another from the first row of bin b, followed by zeros; they sum to at most 2048, and rows after that sum are padding. Each nonzero length is at least 128. In every bin one sequence covers both rows 1023 and 1024.
All inputs are finite; a program needn't handle non-finite values.
Results may differ from the reference program's by a relative error of at most 0.015.
Values may be sent and summed in bfloat16 or wider, within the bound.
No kernel may reach another device: no remote copies, remote signals or barrier semaphores. Data moves between devices by JAX's collectives and lax.ppermute only.
A program may use at most 192 MiB of HBM per device.

```python
import jax
import jax.numpy as jnp
from jax import lax

D = 768
HEADS = 12
HEAD_DIM = 64
FF = 3072
BIN = 2048
SLOTS = 16
TOKENS = 32768
N_DP = 16


def draw_lengths(key, part):
    key = jax.random.fold_in(key, 11)
    first_key, long_key, rest_key, order_key, pick_key = jax.random.split(key, 5)
    unit = BIN // 16
    first = jax.random.randint(first_key, (N_DP,), unit, 3 * unit + 1)
    longest = jax.random.randint(long_key, (N_DP,), BIN // 2 + unit // 4, 3 * BIN // 4 + 1)
    chosen = jax.random.randint(pick_key, (), 0, N_DP)
    longest = jnp.where(jnp.arange(N_DP) == chosen, 3 * BIN // 4, longest)
    budget = BIN - first - longest
    extra = jax.random.randint(rest_key, (N_DP, SLOTS - 2), unit, 4 * unit + 1)
    running = jnp.cumsum(extra, axis=1)
    extra = jnp.where(running <= budget[:, None], extra, 0)
    swapped = jax.random.randint(order_key, (N_DP,), 0, 2) == 1
    leading = jnp.where(swapped, longest, first)
    trailing = jnp.where(swapped, first, longest)
    return jnp.concatenate([leading[:, None], trailing[:, None], extra], axis=1).astype(jnp.int32)


def block_scale(rng, dims, cuts, least, top_value):
    def one(position, parts):
        heights = jax.random.uniform(jax.random.fold_in(jax.random.fold_in(rng, 6), position), (parts,), jnp.float32, least / len(cuts), top_value / len(cuts))
        return jnp.repeat(jnp.exp(heights), dims[position] // parts).reshape((-1,) + (1,) * (len(dims) - position - 1))

    level = one(*cuts[0])
    for cut in cuts[1:]:
        level = level * one(*cut)
    return level


def noise(stream_key, shape, scale, most, cuts=(), kind=jnp.bfloat16):
    array = jax.random.normal(stream_key, shape, jnp.float32) * scale
    if len(cuts) > 0:
        array = block_scale(stream_key, shape, cuts, -0.22, 0.18) * array
    return jnp.clip(array, min=-most, max=most).astype(kind)


def setup_inputs(seed: int = 0) -> dict:
    key_list = jax.random.split(jax.random.key(seed), 16)
    tokens = noise(key_list[0], (TOKENS, D), 1.0, 6.0, ((0, 32),))
    norm1_gain = jnp.clip(1.0 + 0.18 * jax.random.normal(key_list[1], (D,), jnp.float32), 0.1, 1.9)
    norm1_shift = noise(key_list[2], (D,), 0.5, 3.0, (), jnp.float32)
    w_query = noise(key_list[3], (D, D), D ** -0.5, 0.21875, ((0, 16), (1, 2)))
    w_key = noise(key_list[4], (D, D), D ** -0.5, 0.21875, ((0, 16), (1, 2)))
    w_value = noise(key_list[5], (D, D), D ** -0.5, 0.21875, ((0, 16), (1, 2)))
    w_out = noise(key_list[6], (D, D), (max(D // 256, 1)) ** -0.5, 3.5, ((0, 16), (1, 2)))
    fmap_query = noise(key_list[7], (HEADS, HEAD_DIM, HEAD_DIM), HEAD_DIM ** -0.5, 0.75, ((0, 2),))
    fmap_key = noise(key_list[8], (HEADS, HEAD_DIM, HEAD_DIM), HEAD_DIM ** -0.5, 0.75, ((0, 2),))
    norm2_gain = jnp.clip(1.0 + 0.18 * jax.random.normal(key_list[9], (D,), jnp.float32), 0.1, 1.9)
    norm2_shift = noise(key_list[10], (D,), 0.5, 3.0, (), jnp.float32)
    w_fc = noise(key_list[11], (D, FF), D ** -0.5, 0.21875, ((0, 16), (1, 2)))
    w_down = noise(key_list[12], (D, FF), FF ** -0.5, 0.109375, ((0, 16), (1, 2)))
    lengths = draw_lengths(jax.random.fold_in(key_list[15], 71), 0)
    cotangent = noise(key_list[14], (TOKENS, D), 1.0, 6.0, ((0, 32),))
    return {"tokens": tokens, "norm1_gain": norm1_gain, "norm1_shift": norm1_shift, "w_query": w_query, "w_key": w_key, "w_value": w_value, "w_out": w_out, "fmap_query": fmap_query, "fmap_key": fmap_key, "norm2_gain": norm2_gain, "norm2_shift": norm2_shift, "w_fc": w_fc, "w_down": w_down, "lengths": lengths, "cotangent": cotangent}


HIGH = lax.Precision.HIGHEST
EPS = 1e-05

@jax.custom_vjp
def low(v):
    return lax.optimization_barrier(v.astype(jnp.bfloat16)).astype(jnp.float32)

@jax.custom_vjp
def low_back(v):
    return v

def low_keep(v):
    return (low(v), None)

def low_pass(kept, grad):
    return (grad,)

def back_keep(v):
    return (v, None)

def back_low(kept, grad):
    return (low(grad),)
low.defvjp(low_keep, low_pass)
low_back.defvjp(back_keep, back_low)

def layer_norm(rows, gain, shift):
    center = rows - lax.optimization_barrier(jnp.mean(rows, axis=-1, keepdims=True))
    spread = lax.optimization_barrier(jnp.mean(center * center, axis=-1, keepdims=True))
    return center * lax.rsqrt(spread + EPS) * gain + shift

def features(logits):
    return jnp.concatenate([jax.nn.softmax(logits, axis=-1), jax.nn.softmax(-logits, axis=-1)], axis=-1)

def gelu_tanh(inner):
    return jax.nn.gelu(inner, approximate=True)

def segment_rows(counts, total):
    ends = jnp.cumsum(counts).astype(jnp.int32)
    places = jnp.arange(total, dtype=jnp.int32)
    segment = lax.optimization_barrier(jnp.sum((ends[None, :] <= places[:, None]).astype(jnp.int32), axis=1))
    living = places < ends[-1]
    return (segment, living)

def full_core(phi_q, phi_k, values, segment, living):
    places = jnp.arange(segment.shape[0], dtype=jnp.int32)
    mask = (segment[:, None] == segment[None, :]) & (places[None, :] <= places[:, None]) & living[:, None]
    scores = jnp.dot(phi_q, phi_k.T, precision=HIGH)
    weights = jnp.where(mask, scores, jnp.zeros_like(scores))
    numer = jnp.dot(weights, values, precision=HIGH)
    padding = jnp.where(living, 0.0, 1.0).astype(scores.dtype)
    denom = lax.optimization_barrier(jnp.sum(weights, axis=1)) + padding
    return numer / denom[:, None]

def bin_forward(params, rows_in, counts):
    gain1, shift1, w_query, w_key, w_value, w_out, fmap_query, fmap_key, gain2, shift2, w_fc, w_down = params
    total = rows_in.shape[0]
    heads = fmap_query.shape[0]
    width = fmap_query.shape[1]
    segment, living = segment_rows(counts, total)
    normed1 = low(layer_norm(rows_in, gain1, shift1))

    def project(matrix):
        return low(low_back(jnp.dot(normed1, matrix, precision=HIGH)))
    query = project(w_query)
    keyed = project(w_key)
    valued = project(w_value)
    query_logits = low_back(jnp.einsum('rhd,hde->hre', query.reshape(total, heads, width), fmap_query, precision=HIGH))
    key_logits = low_back(jnp.einsum('rhd,hde->hre', keyed.reshape(total, heads, width), fmap_key, precision=HIGH))
    value_heads = valued.reshape(total, heads, width).transpose(1, 0, 2)

    def one_head(members):
        return full_core(features(members[0]), features(members[1]), members[2], segment, living)
    attended = lax.map(one_head, (query_logits, key_logits, value_heads))
    attended = low(attended.transpose(1, 0, 2).reshape(total, heads * width))
    branch = low_back(jnp.dot(attended, w_out.T, precision=HIGH))
    hidden_state = rows_in + branch
    normed2 = low(layer_norm(hidden_state, gain2, shift2))
    inner = low_back(jnp.dot(normed2, w_fc, precision=HIGH))
    activated = low(gelu_tanh(inner))
    feed = low_back(jnp.dot(activated, w_down.T, precision=HIGH))
    return hidden_state + feed

def layer(params, rows_all, lengths):
    bins = lengths.shape[0]
    stacked = rows_all.reshape(bins, rows_all.shape[0] // bins, rows_all.shape[1])

    def one_bin(members):
        return bin_forward(params, members[0], members[1])
    result = lax.map(jax.checkpoint(one_bin), (stacked, lengths))
    return result.reshape(rows_all.shape)

def reference(tokens, norm1_gain, norm1_shift, w_query, w_key, w_value, w_out, fmap_query, fmap_key, norm2_gain, norm2_shift, w_fc, w_down, lengths, cotangent):
    params = tuple((member.astype(jnp.float32) for member in (norm1_gain, norm1_shift, w_query, w_key, w_value, w_out, fmap_query, fmap_key, norm2_gain, norm2_shift, w_fc, w_down)))
    inputs = tokens.astype(jnp.float32)

    def whole(params_in, rows_in):
        return layer(params_in, rows_in, lengths)
    mixed, backward = jax.vjp(whole, params, inputs)
    grads, grad_rows = backward(cotangent.astype(jnp.float32))
    return (mixed.astype(jnp.bfloat16), grad_rows.astype(jnp.bfloat16), grads[0], grads[1], grads[2], grads[3], grads[4], grads[5], grads[6], grads[7], grads[8], grads[9], grads[10], grads[11])
```

```python
import functools

import jax
import jax.numpy as jnp
from jax import lax
from jax.experimental import pallas as pl
from jax.experimental.pallas import tpu as pltpu
from jax.sharding import PartitionSpec as P

EPS = 1e-05
CHUNK = 256
EXT = 80
LOW = jnp.bfloat16
F32 = jnp.float32
VMEM = 56 * 1024 * 1024
GELU_C = 0.7978845608028654
GELU_A = 0.044715


def nn(a, b):
    return lax.dot_general(a, b, (((1,), (0,)), ((), ())), preferred_element_type=F32)


def nt(a, b):
    return lax.dot_general(a, b, (((1,), (1,)), ((), ())), preferred_element_type=F32)


def tn(a, b):
    return lax.dot_general(a, b, (((0,), (0,)), ((), ())), preferred_element_type=F32)


def norm_parts(rows):
    center = rows - jnp.mean(rows, axis=-1, keepdims=True)
    spread = jnp.mean(center * center, axis=-1, keepdims=True)
    rstd = lax.rsqrt(spread + EPS)
    return center * rstd, rstd


def norm_back(grad, xhat, rstd, gain):
    e = grad * gain
    return rstd * (
        e - jnp.mean(e, axis=-1, keepdims=True) - xhat * jnp.mean(e * xhat, axis=-1, keepdims=True)
    )


def softmax_pair(logits):
    high = jnp.max(logits, axis=0, keepdims=True)
    least = jnp.min(logits, axis=0, keepdims=True)
    pos = jnp.exp(logits - high)
    neg = jnp.exp(least - logits)
    pos = pos * (1.0 / jnp.sum(pos, axis=0, keepdims=True))
    neg = neg * (1.0 / jnp.sum(neg, axis=0, keepdims=True))
    return jnp.concatenate([pos, neg], axis=0).astype(LOW)


def softmax_pair_back(phi, grad):
    width = phi.shape[0] // 2
    pos = phi[:width].astype(F32)
    neg = phi[width:].astype(F32)
    gp = grad[:width]
    gn = grad[width:]
    gp = gp - jnp.sum(pos * gp, axis=0, keepdims=True)
    gn = gn - jnp.sum(neg * gn, axis=0, keepdims=True)
    return pos * gp - neg * gn


def project_kernel(
    kept,
    tokens,
    gain,
    shift,
    w_own,
    w_oth,
    fq,
    fk,
    aux,
    normed_t,
    q_t,
    k_t,
    v_nat,
    v_ext,
    phi_q,
    phi_k,
    phi_k_nat,
    prefix,
    final,
    v_sum,
    state,
):
    step = pl.program_id(0)
    width = v_ext.shape[1] - 16
    xhat, unused = norm_parts(tokens[...].astype(F32))
    normed = (xhat * gain[...] + shift[...]).astype(LOW)
    normed_t[...] = normed.T
    written = aux[1:2, :].astype(LOW)
    rows = normed.shape[0]
    tail = jnp.where(lax.broadcasted_iota(jnp.int32, (16, rows), 0) == 0, 1.0, 0.0).astype(LOW)

    @pl.when(step == 0)
    def _():
        state[...] = jnp.zeros_like(state)
        v_sum[...] = jnp.zeros_like(v_sum)

    prefix[0] = state[...]
    keep = kept[step]
    for side, weights in enumerate((w_own, w_oth)):
        made = nn(normed, weights[...]).astype(LOW)
        part = made.shape[1] // 3
        v_nat[:, side * part : (side + 1) * part] = made[:, 2 * part :]
        v_sum[:, side * part : (side + 1) * part] += jnp.sum(
            made[:, 2 * part :].astype(F32), axis=0, keepdims=True
        )
        for pair in range(part // (2 * width)):
            at = side * part + pair * 2 * width
            index = at // (2 * width)
            lanes = slice(pair * 2 * width, (pair + 1) * 2 * width)
            q = made[:, :part][:, lanes].T
            k = made[:, part : 2 * part][:, lanes].T
            v = made[:, 2 * part :][:, lanes].T
            q_t[at : at + 2 * width, :] = q
            k_t[at : at + 2 * width, :] = k
            q_logits = nn(fq[index], q)
            k_logits = nn(fk[index], k)
            for one in range(2):
                head = 2 * index + one
                inside = slice(one * width, (one + 1) * width)
                feat_q = softmax_pair(q_logits[inside])
                feat_k = softmax_pair(k_logits[inside])
                phi_q[head] = feat_q
                phi_k[head] = feat_k
                phi_k_nat[:, head * 2 * width : (head + 1) * 2 * width] = feat_k.T
                value = jnp.concatenate([v[inside], tail], axis=0)
                v_ext[head] = value
                state[head] = keep * state[head] + nt(value, feat_k * written)
    final[...] = state[...]


def project(tokens, gain, shift, w_own, w_oth, fq, fk, aux, kept, heads, width):
    rows, dim = tokens.shape
    count = rows // CHUNK
    feat = 2 * width
    outs = (
        jax.ShapeDtypeStruct((dim, rows), LOW),
        jax.ShapeDtypeStruct((heads * width, rows), LOW),
        jax.ShapeDtypeStruct((heads * width, rows), LOW),
        jax.ShapeDtypeStruct((rows, heads * width), LOW),
        jax.ShapeDtypeStruct((heads, EXT, rows), LOW),
        jax.ShapeDtypeStruct((heads, feat, rows), LOW),
        jax.ShapeDtypeStruct((heads, feat, rows), LOW),
        jax.ShapeDtypeStruct((rows, heads * feat), LOW),
        jax.ShapeDtypeStruct((count, heads, EXT, feat), F32),
        jax.ShapeDtypeStruct((heads, EXT, feat), F32),
        jax.ShapeDtypeStruct((1, heads * width), F32),
    )
    whole = lambda a: pl.BlockSpec(a.shape, lambda c, *_: (0,) * a.ndim)
    return pl.pallas_call(
        project_kernel,
        grid_spec=pltpu.PrefetchScalarGridSpec(
            num_scalar_prefetch=1,
            grid=(count,),
            in_specs=[
                pl.BlockSpec((CHUNK, dim), lambda c, *_: (c, 0)),
                whole(gain),
                whole(shift),
                whole(w_own),
                whole(w_oth),
                whole(fq),
                whole(fk),
                pl.BlockSpec((8, CHUNK), lambda c, *_: (0, c)),
            ],
            out_specs=[
                pl.BlockSpec((dim, CHUNK), lambda c, *_: (0, c)),
                pl.BlockSpec((heads * width, CHUNK), lambda c, *_: (0, c)),
                pl.BlockSpec((heads * width, CHUNK), lambda c, *_: (0, c)),
                pl.BlockSpec((CHUNK, heads * width), lambda c, *_: (c, 0)),
                pl.BlockSpec((heads, EXT, CHUNK), lambda c, *_: (0, 0, c)),
                pl.BlockSpec((heads, feat, CHUNK), lambda c, *_: (0, 0, c)),
                pl.BlockSpec((heads, feat, CHUNK), lambda c, *_: (0, 0, c)),
                pl.BlockSpec((CHUNK, heads * feat), lambda c, *_: (c, 0)),
                pl.BlockSpec((1, heads, EXT, feat), lambda c, *_: (c, 0, 0, 0)),
                pl.BlockSpec((heads, EXT, feat), lambda c, *_: (0, 0, 0)),
                pl.BlockSpec((1, heads * width), lambda c, *_: (0, 0)),
            ],
            scratch_shapes=[pltpu.VMEM((heads, EXT, feat), F32)],
        ),
        out_shape=outs,
        compiler_params=pltpu.CompilerParams(vmem_limit_bytes=VMEM),
        cost_estimate=pl.CostEstimate(
            flops=2 * rows * dim * 3 * heads * width * 3, bytes_accessed=20 << 20, transcendentals=0
        ),
        name="project",
    )(kept, tokens, gain, shift, w_own, w_oth, fq, fk, aux)


def attend_kernel(
    carry,
    tokens,
    gain,
    shift,
    w_own,
    w_oth,
    aux,
    mask,
    phi_q,
    phi_k_nat,
    v_ext,
    prefix,
    entering,
    center,
    att_t,
    att_c,
    denom,
    hidden,
    normed,
    normed_t,
):
    step = pl.program_id(0)
    heads, feat, unused = phi_q.shape
    width = feat // 2
    reach = aux[0:1, :]
    padding = aux[3:4, :]
    keep = carry[step]
    for head in range(heads):
        pq = phi_q[head]
        scores = nn(phi_k_nat[:, head * feat : (head + 1) * feat], pq)
        weights = scores.astype(LOW) * mask[0]
        state = (prefix[0, head] + keep * entering[head]).astype(LOW)
        numer = nn(v_ext[head], weights) + reach * nn(state, pq)
        below = numer[width : width + 1] + padding
        denom[head : head + 1, :] = below
        place = slice(head * width, (head + 1) * width)
        att = numer[:width] * (1.0 / below)
        att_t[place, :] = att.astype(LOW)
        att_c[place, :] = (att - center[place, :]).astype(LOW)
    att = att_t[...].T
    part = w_own.shape[1]
    branch = nt(att[:, :part], w_own[...]) + nt(att[:, part:], w_oth[...])
    total = tokens[...].astype(F32) + branch
    hidden[...] = total
    xhat, unused = norm_parts(total)
    low = (xhat * gain[...] + shift[...]).astype(LOW)
    normed[...] = low
    normed_t[...] = low.T


def attend(tokens, gain, shift, w_own, w_oth, aux, mask, phi_q, phi_k_nat, v_ext, prefix, entering, center, carry):
    rows, dim = tokens.shape
    count = rows // CHUNK
    heads, feat, unused = phi_q.shape
    width = feat // 2
    outs = (
        jax.ShapeDtypeStruct((heads * width, rows), LOW),
        jax.ShapeDtypeStruct((heads * width, rows), LOW),
        jax.ShapeDtypeStruct((16, rows), F32),
        jax.ShapeDtypeStruct((rows, dim), F32),
        jax.ShapeDtypeStruct((rows, dim), LOW),
        jax.ShapeDtypeStruct((dim, rows), LOW),
    )
    whole = lambda a: pl.BlockSpec(a.shape, lambda c, *_: (0,) * a.ndim)
    return pl.pallas_call(
        attend_kernel,
        grid_spec=pltpu.PrefetchScalarGridSpec(
            num_scalar_prefetch=1,
            grid=(count,),
            in_specs=[
                pl.BlockSpec((CHUNK, dim), lambda c, *_: (c, 0)),
                whole(gain),
                whole(shift),
                whole(w_own),
                whole(w_oth),
                pl.BlockSpec((8, CHUNK), lambda c, *_: (0, c)),
                pl.BlockSpec((1, CHUNK, CHUNK), lambda c, *_: (c, 0, 0)),
                pl.BlockSpec((heads, feat, CHUNK), lambda c, *_: (0, 0, c)),
                pl.BlockSpec((CHUNK, heads * feat), lambda c, *_: (c, 0)),
                pl.BlockSpec((heads, EXT, CHUNK), lambda c, *_: (0, 0, c)),
                pl.BlockSpec((1, heads, EXT, feat), lambda c, *_: (c, 0, 0, 0)),
                whole(entering),
                whole(center),
            ],
            out_specs=[
                pl.BlockSpec((heads * width, CHUNK), lambda c, *_: (0, c)),
                pl.BlockSpec((heads * width, CHUNK), lambda c, *_: (0, c)),
                pl.BlockSpec((16, CHUNK), lambda c, *_: (0, c)),
                pl.BlockSpec((CHUNK, dim), lambda c, *_: (c, 0)),
                pl.BlockSpec((CHUNK, dim), lambda c, *_: (c, 0)),
                pl.BlockSpec((dim, CHUNK), lambda c, *_: (0, c)),
            ],
        ),
        out_shape=outs,
        compiler_params=pltpu.CompilerParams(vmem_limit_bytes=VMEM),
        cost_estimate=pl.CostEstimate(
            flops=2 * rows * dim * heads * width * 6, bytes_accessed=20 << 20, transcendentals=0
        ),
        name="attend",
    )(carry, tokens, gain, shift, w_own, w_oth, aux, mask, phi_q, phi_k_nat, v_ext, prefix, entering, center)


def feed_kernel(
    normed,
    normed_t,
    cot,
    cot_t,
    fc_own,
    fc_oth,
    down_own,
    down_oth,
    feed,
    grad_normed,
    d_fc_own,
    d_fc_oth,
    d_down_own,
    d_down_oth,
):
    step = pl.program_id(0)

    acts = []
    grads = []
    for fc, down, d_fc, d_down in (
        (fc_own, down_own, d_fc_own, d_down_own),
        (fc_oth, down_oth, d_fc_oth, d_down_oth),
    ):
        u = nn(normed[...], fc[...])
        square = u * u
        t = jnp.tanh(u * (GELU_C + (GELU_C * GELU_A) * square))
        half = 0.5 + 0.5 * t
        act = (u * half).astype(LOW)
        slope = half + (0.5 * u) * (1.0 - t * t) * (GELU_C + (3.0 * GELU_C * GELU_A) * square)
        d_down[...] = nn(cot_t[...], act).astype(LOW)
        grad = (nn(cot[...], down[...]) * slope).astype(LOW)
        d_fc[...] = nn(normed_t[...], grad).astype(LOW)
        acts.append(act)
        grads.append(grad)
    more = nt(
        jnp.concatenate(acts, axis=1), jnp.concatenate([down_own[...], down_oth[...]], axis=1)
    )
    more_grad = nt(
        jnp.concatenate(grads, axis=1), jnp.concatenate([fc_own[...], fc_oth[...]], axis=1)
    )

    @pl.when(step == 0)
    def _():
        feed[...] = more
        grad_normed[...] = more_grad

    @pl.when(step > 0)
    def _():
        feed[...] += more
        grad_normed[...] += more_grad


def feed_forward(normed, normed_t, cot, cot_t, fc_own, fc_oth, down_own, down_oth):
    rows, dim = normed.shape
    units = fc_own.shape[1]
    tile = 256
    whole = lambda a: pl.BlockSpec(a.shape, lambda j: (0,) * a.ndim)
    tiled = pl.BlockSpec((dim, tile), lambda j: (0, j))
    total = pl.BlockSpec((rows, dim), lambda j: (0, 0))
    grad = jax.ShapeDtypeStruct((dim, units), LOW)
    return pl.pallas_call(
        feed_kernel,
        grid=(units // tile,),
        in_specs=[whole(normed), whole(normed_t), whole(cot), whole(cot_t)] + [tiled] * 4,
        out_specs=[total, total] + [tiled] * 4,
        out_shape=(
            jax.ShapeDtypeStruct((rows, dim), F32),
            jax.ShapeDtypeStruct((rows, dim), F32),
            grad,
            grad,
            grad,
            grad,
        ),
        compiler_params=pltpu.CompilerParams(vmem_limit_bytes=VMEM),
        cost_estimate=pl.CostEstimate(
            flops=2 * 6 * rows * dim * 2 * units, bytes_accessed=24 << 20, transcendentals=0
        ),
        name="feed",
    )(normed, normed_t, cot, cot_t, fc_own, fc_oth, down_own, down_oth)


def middle_kernel(
    hidden,
    feed_a,
    feed_b,
    gn_a,
    gn_b,
    cot,
    gain,
    w_own,
    w_oth,
    att_t,
    att_c,
    denom,
    phi_q,
    aux,
    mixed,
    grad_hidden,
    d_gain,
    d_shift,
    g_ext,
    leaving,
    d_out_own,
    d_out_oth,
    branch_t,
    att_all,
    state,
):
    step = pl.program_id(0)
    count = pl.num_programs(0)
    rows = hidden.shape[0]
    heads, feat, unused = phi_q.shape
    width = feat // 2
    hid = hidden[...]
    mixed[...] = (hid + (feed_a[...] + feed_b[...])).astype(LOW)
    xhat, rstd = norm_parts(hid)
    grad = gn_a[...] + gn_b[...]
    back = cot[...].astype(F32) + norm_back(grad, xhat, rstd, gain[...])
    grad_hidden[...] = back
    gain_part = jnp.sum(grad * xhat, axis=0, keepdims=True)
    shift_part = jnp.sum(grad, axis=0, keepdims=True)

    @pl.when(step == 0)
    def _():
        d_gain[...] = gain_part
        d_shift[...] = shift_part
        state[...] = jnp.zeros_like(state)

    @pl.when(step > 0)
    def _():
        d_gain[...] += gain_part
        d_shift[...] += shift_part

    low = back.astype(LOW)
    place = pl.ds(pl.multiple_of(step * rows, rows), rows)
    branch_t[:, place] = low.T
    att_all[:, place] = att_t[...]
    reach = aux[2:3, :].astype(LOW)
    part = w_own.shape[1]
    first = lax.broadcasted_iota(jnp.int32, (16, rows), 0) == 0
    for side, weights in enumerate((w_own, w_oth)):
        grad_att = nn(low, weights[...])
        for pair in range(part // (2 * width)):
            turned = grad_att[:, pair * 2 * width : (pair + 1) * 2 * width].T
            for one in range(2):
                head = side * (part // width) + pair * 2 + one
                ga = turned[one * width : (one + 1) * width]
                inverse = 1.0 / denom[head : head + 1, :]
                at = att_c[head * width : (head + 1) * width, :].astype(F32)
                gd = -jnp.sum(ga * at, axis=0, keepdims=True) * inverse
                ext = jnp.concatenate(
                    [(ga * inverse).astype(LOW), jnp.where(first, gd, 0.0).astype(LOW)], axis=0
                )
                g_ext[head] = ext
                state[head] += nt(ext * reach, phi_q[head])
    leaving[...] = state[...].astype(LOW)

    @pl.when(step == count - 1)
    def _():
        d_out_own[...] = nt(branch_t[...], att_all[:part, :]).astype(LOW)
        d_out_oth[...] = nt(branch_t[...], att_all[part:, :]).astype(LOW)


def middle(hidden, feed_a, feed_b, gn_a, gn_b, cot, gain, w_own, w_oth, att_t, att_c, denom, phi_q, aux):
    rows, dim = hidden.shape
    count = rows // CHUNK
    heads, feat, unused = phi_q.shape
    width = feat // 2
    part = w_own.shape[1]
    whole = lambda a: pl.BlockSpec(a.shape, lambda c: (0,) * a.ndim)
    rowed = pl.BlockSpec((CHUNK, dim), lambda c: (c, 0))
    fixed = lambda *shape: pl.BlockSpec(shape, lambda c: (0,) * len(shape))
    return pl.pallas_call(
        middle_kernel,
        grid=(count,),
        in_specs=[rowed] * 6
        + [
            whole(gain),
            whole(w_own),
            whole(w_oth),
            pl.BlockSpec((heads * width, CHUNK), lambda c: (0, c)),
            pl.BlockSpec((heads * width, CHUNK), lambda c: (0, c)),
            pl.BlockSpec((16, CHUNK), lambda c: (0, c)),
            pl.BlockSpec((heads, feat, CHUNK), lambda c: (0, 0, c)),
            pl.BlockSpec((8, CHUNK), lambda c: (0, c)),
        ],
        out_specs=[
            rowed,
            rowed,
            fixed(1, dim),
            fixed(1, dim),
            pl.BlockSpec((heads, EXT, CHUNK), lambda c: (0, 0, c)),
            fixed(heads, EXT, feat),
            fixed(dim, part),
            fixed(dim, part),
        ],
        out_shape=(
            jax.ShapeDtypeStruct((rows, dim), LOW),
            jax.ShapeDtypeStruct((rows, dim), F32),
            jax.ShapeDtypeStruct((1, dim), F32),
            jax.ShapeDtypeStruct((1, dim), F32),
            jax.ShapeDtypeStruct((heads, EXT, rows), LOW),
            jax.ShapeDtypeStruct((heads, EXT, feat), LOW),
            jax.ShapeDtypeStruct((dim, part), LOW),
            jax.ShapeDtypeStruct((dim, part), LOW),
        ),
        scratch_shapes=[
            pltpu.VMEM((dim, rows), LOW),
            pltpu.VMEM((heads * width, rows), LOW),
            pltpu.VMEM((heads, EXT, feat), F32),
        ],
        compiler_params=pltpu.CompilerParams(vmem_limit_bytes=VMEM),
        cost_estimate=pl.CostEstimate(
            flops=2 * rows * dim * heads * width * 3, bytes_accessed=24 << 20, transcendentals=0
        ),
        name="middle",
    )(hidden, feed_a, feed_b, gn_a, gn_b, cot, gain, w_own, w_oth, att_t, att_c, denom, phi_q, aux)


def attend_back_kernel(
    carry,
    kept,
    aux,
    mask,
    phi_q,
    phi_k,
    phi_k_nat,
    v_nat,
    v_ext,
    g_ext,
    prefix,
    entering,
    arriving,
    q_t,
    k_t,
    fq,
    fk,
    center,
    center_row,
    gq_t,
    gk_t,
    gv_t,
    d_fq,
    d_fk,
    state,
):
    step = pl.program_id(0)
    count = pl.num_programs(0)
    heads, feat, rows = phi_q.shape
    width = feat // 2
    chunk = count - 1 - step
    keep_in = carry[chunk]
    keep = kept[chunk]
    reach = aux[0:1, :].astype(LOW)
    written = aux[1:2, :].astype(LOW)

    @pl.when(step == 0)
    def _():
        state[...] = arriving[...].astype(F32)
        d_fq[...] = jnp.zeros_like(d_fq)
        d_fk[...] = jnp.zeros_like(d_fk)

    for pair in range(heads // 2):
        logit_grads = ([], [])
        lanes = slice(pair * feat, (pair + 1) * feat)
        v_pair = (v_nat[:, lanes].astype(F32) - center_row[:, lanes]).astype(LOW)
        for one in range(2):
            head = 2 * pair + one
            pq = phi_q[head]
            pk = phi_k[head]
            scores = nn(phi_k_nat[:, head * feat : (head + 1) * feat], pq)
            weights = scores.astype(LOW) * mask[0]
            ext = g_ext[head]
            numer = ext[:width]
            blank = jnp.zeros_like(numer)
            padded = jnp.concatenate([numer, blank] if one == 0 else [blank, numer], axis=0)
            gw = nn(v_pair, padded)
            gw = (gw + ext[width : width + 1].astype(F32)).astype(LOW) * mask[0]
            middle_v = center[head * width : (head + 1) * width, :]
            before = prefix[0, head] + keep_in * entering[head]
            before = jnp.concatenate(
                [before[:width] - middle_v * before[width : width + 1], before[width:]], axis=0
            ).astype(LOW)
            value = v_ext[head]
            value = jnp.concatenate(
                [(value[:width].astype(F32) - middle_v).astype(LOW), value[width:]], axis=0
            )
            after = state[head].astype(LOW)
            reached = ext * reach
            g_phi_q = nn(pk, gw) + tn(before, reached)
            g_phi_k = nt(pq, gw) + tn(after, value * written)
            g_value = nt(numer, weights) + nn(after[:width], pk * written)
            gv_t[head * width : (head + 1) * width, :] = g_value.astype(LOW)
            state[head] = keep * state[head] + nt(reached, pq)
            logit_grads[0].append(softmax_pair_back(pq, g_phi_q).astype(LOW))
            logit_grads[1].append(softmax_pair_back(pk, g_phi_k).astype(LOW))
        place = slice(pair * feat, (pair + 1) * feat)
        for grads, fmap, source, grad_out, d_fmap in (
            (logit_grads[0], fq, q_t, gq_t, d_fq),
            (logit_grads[1], fk, k_t, gk_t, d_fk),
        ):
            both = jnp.concatenate(grads, axis=0)
            grad_out[place, :] = nn(fmap[pair], both).astype(LOW)
            d_fmap[pair] += nt(source[place, :], both)


def attend_back(
    aux, mask, phi_q, phi_k, phi_k_nat, v_nat, v_ext, g_ext, prefix, entering, arriving, q_t, k_t, fq, fk, center, center_row, carry, kept
):
    heads, feat, rows = phi_q.shape
    width = feat // 2
    count = rows // CHUNK
    whole = lambda a: pl.BlockSpec(a.shape, lambda c, *_: (0,) * a.ndim)
    lanes = lambda size: pl.BlockSpec((size, CHUNK), lambda c, *_: (0, count - 1 - c))
    headed = lambda size: pl.BlockSpec((heads, size, CHUNK), lambda c, *_: (0, 0, count - 1 - c))
    natural = lambda size: pl.BlockSpec((CHUNK, size), lambda c, *_: (count - 1 - c, 0))
    fixed = lambda *shape: pl.BlockSpec(shape, lambda c, *_: (0,) * len(shape))
    grad = jax.ShapeDtypeStruct((heads * width, rows), LOW)
    grad_map = jax.ShapeDtypeStruct((heads // 2, feat, feat), F32)
    return pl.pallas_call(
        attend_back_kernel,
        grid_spec=pltpu.PrefetchScalarGridSpec(
            num_scalar_prefetch=2,
            grid=(count,),
            in_specs=[
                lanes(8),
                pl.BlockSpec((1, CHUNK, CHUNK), lambda c, *_: (count - 1 - c, 0, 0)),
                headed(feat),
                headed(feat),
                natural(heads * feat),
                natural(heads * width),
                headed(EXT),
                headed(EXT),
                pl.BlockSpec((1, heads, EXT, feat), lambda c, *_: (count - 1 - c, 0, 0, 0)),
                whole(entering),
                whole(arriving),
                lanes(heads * width),
                lanes(heads * width),
                whole(fq),
                whole(fk),
                whole(center),
                whole(center_row),
            ],
            out_specs=[
                lanes(heads * width),
                lanes(heads * width),
                lanes(heads * width),
                fixed(heads // 2, feat, feat),
                fixed(heads // 2, feat, feat),
            ],
            scratch_shapes=[pltpu.VMEM((heads, EXT, feat), F32)],
        ),
        out_shape=(grad, grad, grad, grad_map, grad_map),
        compiler_params=pltpu.CompilerParams(vmem_limit_bytes=VMEM),
        cost_estimate=pl.CostEstimate(
            flops=2 * rows * heads * CHUNK * feat * 10, bytes_accessed=24 << 20, transcendentals=0
        ),
        name="attend_back",
    )(carry, kept, aux, mask, phi_q, phi_k, phi_k_nat, v_nat, v_ext, g_ext, prefix, entering, arriving, q_t, k_t, fq, fk, center, center_row)


def weight_kernel(normed_t, gq_t, gk_t, gv_t, out):
    part = out.shape[1] // 3
    for place, grad in enumerate((gq_t, gk_t, gv_t)):
        out[:, place * part : (place + 1) * part] = nt(normed_t[...], grad[...]).astype(LOW)


def weight_grads(normed_t, gq_t, gk_t, gv_t):
    dim, rows = normed_t.shape
    part = gq_t.shape[0] // 2
    spec = pl.BlockSpec((part, rows), lambda s: (s, 0))
    return pl.pallas_call(
        weight_kernel,
        grid=(2,),
        in_specs=[pl.BlockSpec((dim, rows), lambda s: (0, 0)), spec, spec, spec],
        out_specs=pl.BlockSpec((dim, 3 * part), lambda s: (0, s)),
        out_shape=jax.ShapeDtypeStruct((dim, 6 * part), LOW),
        compiler_params=pltpu.CompilerParams(vmem_limit_bytes=VMEM),
        cost_estimate=pl.CostEstimate(
            flops=2 * 6 * part * dim * rows, bytes_accessed=10 << 20, transcendentals=0
        ),
        name="weight_grads",
    )(normed_t, gq_t, gk_t, gv_t)


def first_kernel(tokens, gain, grad_hidden, w_own, w_oth, gq_t, gk_t, gv_t, out, d_gain, d_shift):
    step = pl.program_id(0)
    part = w_own.shape[1] // 3
    total = None
    for side, weights in enumerate((w_own, w_oth)):
        place = slice(side * part, (side + 1) * part)
        stacked = jnp.concatenate([gq_t[place, :], gk_t[place, :], gv_t[place, :]], axis=0)
        term = nn(weights[...], stacked)
        total = term if total is None else total + term
    grad = total.T
    xhat, rstd = norm_parts(tokens[...].astype(F32))
    out[...] = (grad_hidden[...] + norm_back(grad, xhat, rstd, gain[...])).astype(LOW)
    gain_part = jnp.sum(grad * xhat, axis=0, keepdims=True)
    shift_part = jnp.sum(grad, axis=0, keepdims=True)

    @pl.when(step == 0)
    def _():
        d_gain[...] = gain_part
        d_shift[...] = shift_part

    @pl.when(step > 0)
    def _():
        d_gain[...] += gain_part
        d_shift[...] += shift_part


def first_back(tokens, gain, grad_hidden, w_own, w_oth, gq_t, gk_t, gv_t):
    rows, dim = tokens.shape
    size = gq_t.shape[0]
    whole = lambda a: pl.BlockSpec(a.shape, lambda c: (0,) * a.ndim)
    rowed = pl.BlockSpec((CHUNK, dim), lambda c: (c, 0))
    lanes = pl.BlockSpec((size, CHUNK), lambda c: (0, c))
    fixed = pl.BlockSpec((1, dim), lambda c: (0, 0))
    return pl.pallas_call(
        first_kernel,
        grid=(rows // CHUNK,),
        in_specs=[rowed, whole(gain), rowed, whole(w_own), whole(w_oth), lanes, lanes, lanes],
        out_specs=[rowed, fixed, fixed],
        out_shape=(
            jax.ShapeDtypeStruct((rows, dim), LOW),
            jax.ShapeDtypeStruct((1, dim), F32),
            jax.ShapeDtypeStruct((1, dim), F32),
        ),
        compiler_params=pltpu.CompilerParams(vmem_limit_bytes=VMEM),
        cost_estimate=pl.CostEstimate(
            flops=2 * 3 * size * dim * rows, bytes_accessed=14 << 20, transcendentals=0
        ),
        name="first_back",
    )(tokens, gain, grad_hidden, w_own, w_oth, gq_t, gk_t, gv_t)


SWAP = [(0, 1), (1, 0)]


def swap(piece):
    return lax.ppermute(piece, "mp", SWAP)


def flip(piece, bit, size):
    return lax.ppermute(piece, "dp", [(i, i ^ bit) for i in range(size)])


def turn(piece, by, size):
    return lax.ppermute(piece, "dp", [(i, (i + by) % size) for i in range(size)])


def other_order(state):
    half = state.shape[0] // 2
    return jnp.concatenate([state[half:], state[:half]], axis=0)


def ordered(mine, theirs, bit, axis):
    low = jnp.where(bit == 0, mine, theirs)
    high = jnp.where(bit == 0, theirs, mine)
    return jnp.stack([low, high], axis=axis)


def gather(shard, size):
    rows, columns = shard.shape
    if size % 4:
        own = lax.all_gather(shard, "dp", axis=0, tiled=True)
        return own, swap(own)
    place = lax.axis_index("dp")
    deep = size // 4
    x, y, z = place % 2, (place // 2) % 2, place // 4
    pieces = [shard] + [turn(shard, 4 * s, size) for s in range(1, deep)]
    ring = jnp.concatenate([pieces[deep - 1 - s] for s in range(deep)] * 2, axis=0)
    line = lax.dynamic_slice_in_dim(ring, (deep - 1 - z) * rows, deep * rows, 0)
    half = columns // 2
    a = line[:, :half].reshape(deep, rows, half)
    b = line[:, half:].reshape(deep, rows, half)
    a = ordered(a, flip(a, 1, size), x, 1)
    b = ordered(b, flip(b, 2, size), y, 1)
    a = ordered(a, flip(a, 2, size), y, 1)
    b = ordered(b, flip(b, 1, size), x, 2)
    own = jnp.concatenate(
        [a.reshape(size * rows, half), b.reshape(size * rows, half)], axis=1
    )
    return own, swap(own)


def scatter(own, other, size):
    got = own.astype(F32) + swap(other).astype(F32)
    rows = own.shape[0] // size
    columns = own.shape[1]
    if size % 4:
        return lax.psum_scatter(got, "dp", scatter_dimension=0, tiled=True)
    place = lax.axis_index("dp")
    deep = size // 4
    x, y, z = place % 2, (place // 2) % 2, place // 4
    half = columns // 2
    got = got.astype(LOW).reshape(deep, 2, 2, rows, columns)

    def fold(value, axis, bit, step):
        keep = lax.dynamic_index_in_dim(value, bit, axis, False)
        send = lax.dynamic_index_in_dim(value, 1 - bit, axis, False)
        return (keep.astype(F32) + flip(send, step, size).astype(F32)).astype(LOW)

    a = fold(got[..., :half], 2, x, 1)
    b = fold(got[..., half:], 1, y, 2)
    a = fold(a, 1, y, 2)
    b = fold(b, 1, x, 1)
    line = jnp.concatenate([a, b], axis=-1)
    total = lax.dynamic_index_in_dim(line, z, 0, False).astype(F32)
    for s in range(1, deep):
        send = lax.dynamic_index_in_dim(line, (z + s) % deep, 0, False)
        total = total + turn(send, 4 * s, size).astype(F32)
    return total


def block_pairs(fmap):
    heads, width, unused = fmap.shape
    pairs = fmap.reshape(heads // 2, 2, width, width)
    blank = jnp.zeros_like(pairs[:, 0])
    return jnp.concatenate(
        [
            jnp.concatenate([pairs[:, 0], blank], axis=2),
            jnp.concatenate([blank, pairs[:, 1]], axis=2),
        ],
        axis=1,
    )


def unblock_pairs(pairs):
    width = pairs.shape[1] // 2
    both = jnp.stack([pairs[:, :width, :width], pairs[:, width:, width:]], axis=1)
    return both.reshape(-1, width, width)


def per_device(
    size,
    tokens,
    norm1_gain,
    norm1_shift,
    w_query,
    w_key,
    w_value,
    w_out,
    fmap_query,
    fmap_key,
    norm2_gain,
    norm2_shift,
    w_fc,
    w_down,
    lengths,
    cotangent,
):
    rows, dim = tokens.shape
    heads = 2 * fmap_query.shape[0]
    width = fmap_query.shape[1]
    part = w_query.shape[1]
    slots = lengths.shape[1]
    count = rows // CHUNK
    core = lax.axis_index("mp")

    ends = jnp.cumsum(lengths[0])
    places = core * rows - 1 + jnp.arange(rows + 1, dtype=jnp.int32)
    numbers = jnp.sum((ends[None, :] <= places[:, None]).astype(jnp.int32), axis=1)
    numbers = jnp.where(places < 0, -1, numbers)
    segment = numbers[1:]
    living = places[1:] < ends[-1]
    blocks = segment.reshape(count, CHUNK)
    last = blocks[:, -1]
    before = jnp.concatenate([numbers[:1], last[:-1]])
    kept = (last == before).astype(F32)
    carry = (before == numbers[0]).astype(F32)
    reach = (blocks == before[:, None]).reshape(rows) & living
    written = (blocks == last[:, None]).reshape(rows)
    reach_in = (segment == numbers[0]) & living
    aux = jnp.stack([reach, written, reach_in, ~living] + [jnp.zeros_like(living)] * 4).astype(F32)
    order = jnp.arange(CHUNK, dtype=jnp.int32)
    mask = (
        (blocks[:, :, None] == blocks[:, None, :])
        & (order[:, None] <= order[None, :])
        & living.reshape(count, 1, CHUNK)
    ).astype(LOW)

    fq = block_pairs(jnp.concatenate([fmap_query, swap(fmap_query)], axis=0))
    fk = block_pairs(jnp.concatenate([fmap_key, swap(fmap_key)], axis=0))
    gain1, shift1 = norm1_gain[None, :], norm1_shift[None, :]
    gain2, shift2 = norm2_gain[None, :], norm2_shift[None, :]

    qkv_own, qkv_oth = gather(jnp.concatenate([w_query, w_key, w_value], axis=1), size)
    out_own, out_oth = gather(w_out, size)
    split = w_fc.shape[1] // 2
    groups = []
    for g in range(2):
        cut = slice(g * split, (g + 1) * split)
        own, oth = gather(jnp.concatenate([w_fc[:, cut], w_down[:, cut]], axis=1), size)
        groups.append((own[:, :split], oth[:, :split], own[:, split:], oth[:, split:]))

    normed1_t, q_t, k_t, v_nat, v_ext, phi_q, phi_k, phi_k_nat, prefix, final, v_sum = project(
        tokens,
        gain1,
        shift1,
        qkv_own,
        qkv_oth,
        fq.swapaxes(1, 2),
        fk.swapaxes(1, 2),
        aux,
        kept,
        heads,
        width,
    )
    entering = other_order(lax.ppermute(final, "mp", [(0, 1)]))
    center = (v_sum[0] + other_order(swap(v_sum[0]))) * (1.0 / (2 * rows))
    att_t, att_c, denom, hidden, normed2, normed2_t = attend(
        tokens, gain2, shift2, out_own, out_oth, aux, mask, phi_q, phi_k_nat, v_ext, prefix, entering, center[:, None], carry
    )
    cot_t = cotangent.T
    parts = []
    for fc_own, fc_oth, down_own, down_oth in groups:
        parts.append(
            feed_forward(normed2, normed2_t, cotangent, cot_t, fc_own, fc_oth, down_own, down_oth)
        )
    mixed, grad_hidden, d_gain2, d_shift2, g_ext, leaving, d_out_own, d_out_oth = middle(
        hidden,
        parts[0][0],
        parts[1][0],
        parts[0][1],
        parts[1][1],
        cotangent,
        gain2,
        out_own,
        out_oth,
        att_t,
        att_c,
        denom,
        phi_q,
        aux,
    )
    arriving = other_order(lax.ppermute(leaving, "mp", [(1, 0)]))
    gq_t, gk_t, gv_t, d_fq, d_fk = attend_back(
        aux,
        mask,
        phi_q,
        phi_k,
        phi_k_nat,
        v_nat,
        v_ext,
        g_ext,
        prefix,
        entering,
        arriving,
        q_t,
        k_t,
        fq,
        fk,
        center[:, None],
        center[None, :],
        carry,
        kept,
    )
    d_qkv = weight_grads(normed1_t, gq_t, gk_t, gv_t)
    grad_tokens, d_gain1, d_shift1 = first_back(
        tokens, gain1, grad_hidden, qkv_own, qkv_oth, gq_t, gk_t, gv_t
    )

    sums = []
    for members in parts:
        sums.append(
            scatter(
                jnp.concatenate([members[2], members[4]], axis=1),
                jnp.concatenate([members[3], members[5]], axis=1),
                size,
            )
        )
    grad_fc = jnp.concatenate([member[:, :split] for member in sums], axis=1)
    grad_down = jnp.concatenate([member[:, split:] for member in sums], axis=1)
    grad_out = scatter(d_out_own, d_out_oth, size)
    grad_qkv = scatter(d_qkv[:, : 3 * part], d_qkv[:, 3 * part :], size)
    d_fq = unblock_pairs(d_fq)
    d_fk = unblock_pairs(d_fk)
    local = heads // 2
    d_fq = d_fq[:local] + swap(d_fq[local:])
    d_fk = d_fk[:local] + swap(d_fk[local:])
    d_fq, d_fk = lax.psum((d_fq, d_fk), "dp")
    d_gain1, d_shift1, d_gain2, d_shift2 = lax.psum(
        (d_gain1[0], d_shift1[0], d_gain2[0], d_shift2[0]), ("dp", "mp")
    )
    return (
        mixed,
        grad_tokens,
        d_gain1,
        d_shift1,
        grad_qkv[:, :part],
        grad_qkv[:, part : 2 * part],
        grad_qkv[:, 2 * part :],
        grad_out,
        d_fq,
        d_fk,
        d_gain2,
        d_shift2,
        grad_fc,
        grad_down,
    )


def solution(mesh):
    placed = (
        P(("dp", "mp"), None),
        P(),
        P(),
        P("dp", "mp"),
        P("dp", "mp"),
        P("dp", "mp"),
        P("dp", "mp"),
        P("mp", None, None),
        P("mp", None, None),
        P(),
        P(),
        P("dp", "mp"),
        P("dp", "mp"),
        P("dp", None),
        P(("dp", "mp"), None),
    )
    return jax.shard_map(
        functools.partial(per_device, mesh.shape["dp"]),
        mesh=mesh,
        in_specs=placed,
        out_specs=(
            P(("dp", "mp"), None),
            P(("dp", "mp"), None),
            P(),
            P(),
            P("dp", "mp"),
            P("dp", "mp"),
            P("dp", "mp"),
            P("dp", "mp"),
            P("mp", None, None),
            P("mp", None, None),
            P(),
            P(),
            P("dp", "mp"),
            P("dp", "mp"),
        ),
        check_vma=False,
    )
```

```python
import functools

import jax
import jax.numpy as jnp
from jax import lax
from jax.experimental import pallas as pl
from jax.experimental.pallas import tpu as pltpu
from jax.sharding import PartitionSpec as P

EPS = 1e-05
CHUNK = 256
EXT = 80
LOW = jnp.bfloat16
F32 = jnp.float32
MIB = 1024 * 1024
PACE = 3_000_000_000
GELU_C = 0.7978845608028654
GELU_A = 0.044715


def nn(a, b):
    return lax.dot_general(a, b, (((1,), (0,)), ((), ())), preferred_element_type=F32)


def nt(a, b):
    return lax.dot_general(a, b, (((1,), (1,)), ((), ())), preferred_element_type=F32)


def tn(a, b):
    return lax.dot_general(a, b, (((0,), (0,)), ((), ())), preferred_element_type=F32)


def norm_parts(rows):
    center = rows - jnp.mean(rows, axis=-1, keepdims=True)
    spread = jnp.mean(center * center, axis=-1, keepdims=True)
    rstd = lax.rsqrt(spread + EPS)
    return center * rstd, rstd


def norm_back(grad, xhat, rstd, gain):
    e = grad * gain
    return rstd * (
        e - jnp.mean(e, axis=-1, keepdims=True) - xhat * jnp.mean(e * xhat, axis=-1, keepdims=True)
    )


def softmax_pair(logits):
    high = jnp.max(logits, axis=0, keepdims=True)
    least = jnp.min(logits, axis=0, keepdims=True)
    pos = jnp.exp(logits - high)
    neg = jnp.exp(least - logits)
    pos = pos * (1.0 / jnp.sum(pos, axis=0, keepdims=True))
    neg = neg * (1.0 / jnp.sum(neg, axis=0, keepdims=True))
    return jnp.concatenate([pos, neg], axis=0).astype(LOW)


def softmax_pair_back(phi, grad):
    width = phi.shape[0] // 2
    pos = phi[:width].astype(F32)
    neg = phi[width:].astype(F32)
    gp = grad[:width]
    gn = grad[width:]
    gp = gp - jnp.sum(pos * gp, axis=0, keepdims=True)
    gn = gn - jnp.sum(neg * gn, axis=0, keepdims=True)
    return pos * gp - neg * gn


def flat(value):
    return value.reshape(-1, value.shape[-1])


def kept_in_vmem(shape, dtype):
    return pltpu.VMEM(shape, dtype)


def streamed(shape, dtype):
    return pltpu.HBM(shape, dtype)


def apart(*arrays):
    return tuple(pltpu.with_memory_space_constraint(a, pltpu.HBM) for a in arrays)


def pinned(*arrays):
    return tuple(pltpu.with_memory_space_constraint(a, pltpu.VMEM) for a in arrays)


def whole(array):
    return pl.BlockSpec(
        array.shape, lambda *_: (0,) * array.ndim, pipeline_mode=pl.Buffered(1)
    )


def fixed(*shape):
    return pl.BlockSpec(shape, lambda *_: (0,) * len(shape))


STAYS = pl.BlockSpec(memory_space=pltpu.VMEM)


def at(step, size):
    return pl.ds(pl.multiple_of(step * size, size), size)


def call(kernel, name, grid, in_specs, out_specs, out_shape, scratch, limit, micros, args, scalars=0, alias=None):
    return pl.pallas_call(
        kernel,
        grid_spec=pltpu.PrefetchScalarGridSpec(
            num_scalar_prefetch=scalars,
            grid=grid,
            in_specs=in_specs,
            out_specs=out_specs,
            scratch_shapes=scratch,
        ),
        out_shape=out_shape,
        input_output_aliases=alias or {},
        compiler_params=pltpu.CompilerParams(vmem_limit_bytes=limit * MIB),
        cost_estimate=pl.CostEstimate(flops=micros * PACE, bytes_accessed=1024, transcendentals=0),
        name=name,
    )(*args)


def prepare_kernel(
    tokens, cot, norms, fq_own, fq_oth, fk_own, fk_oth, normed, normed_t, held_cot, cot_t, maps
):
    step = pl.program_id(0)
    rows = at(step, CHUNK)
    xhat, unused = norm_parts(tokens[...].astype(F32))
    low = (xhat * norms[0:1, :] + norms[1:2, :]).astype(LOW)
    normed[rows, :] = low
    normed_t[...] = low.T
    held_cot[rows, :] = cot[...]
    cot_t[:, rows] = cot[...].T

    @pl.when(step == 0)
    def _():
        half, width, unused = fq_own.shape
        blank = jnp.zeros((width, width), F32)
        for kind, (own, oth) in enumerate(((fq_own, fq_oth), (fk_own, fk_oth))):
            for pair in range(half):
                source = own if pair < half // 2 else oth
                first = 2 * pair % half
                block = jnp.concatenate(
                    [
                        jnp.concatenate([source[first].astype(F32), blank], axis=1),
                        jnp.concatenate([blank, source[first + 1].astype(F32)], axis=1),
                    ],
                    axis=0,
                )
                maps[2 * kind, pair] = block.astype(LOW)
                maps[2 * kind + 1, pair] = block.T.astype(LOW)


def prepare(tokens, cot, norms, fq_own, fq_oth, fk_own, fk_oth):
    rows, dim = tokens.shape
    half, width, unused = fq_own.shape
    block = pl.BlockSpec((CHUNK, dim), lambda c: (c, 0))
    natural = kept_in_vmem((rows, dim), LOW)
    turned = kept_in_vmem((dim, rows), LOW)
    return call(
        prepare_kernel,
        "prepare",
        (rows // CHUNK,),
        [block, block] + [whole(a) for a in (norms, fq_own, fq_oth, fk_own, fk_oth)],
        [STAYS, pl.BlockSpec((dim, CHUNK), lambda c: (0, c))] + [STAYS] * 3,
        (natural, streamed((dim, rows), LOW), natural, turned, kept_in_vmem((4, half, 2 * width, 2 * width), LOW)),
        [],
        8,
        5,
        (*apart(tokens, cot), norms, fq_own, fq_oth, fk_own, fk_oth),
    )


def project_kernel(
    kept,
    normed,
    wa_own,
    wb_own,
    wa_oth,
    wb_oth,
    maps,
    aux,
    q_t,
    k_t,
    v_nat,
    v_ext,
    phi_q,
    phi_k,
    phi_k_nat,
    prefix,
    final,
    state,
):
    step = pl.program_id(0)
    heads, feat, unused = phi_q.shape
    width = feat // 2
    rows = at(step, CHUNK)
    normed_now = normed[rows, :]
    written = aux[1:2, rows].astype(LOW)
    tail = jnp.where(lax.broadcasted_iota(jnp.int32, (16, CHUNK), 0) == 0, 1.0, 0.0).astype(LOW)

    @pl.when(step == 0)
    def _():
        state[...] = jnp.zeros_like(state)

    prefix[0] = state[:heads]
    keep = kept[step]
    for side, (wa, wb) in enumerate(((wa_own, wb_own), (wa_oth, wb_oth))):
        made = jnp.concatenate([nn(normed_now, wa[...]), nn(normed_now, wb[...])], axis=1).astype(LOW)
        part = made.shape[1] // 3
        values = made[:, 2 * part :]
        v_nat[:, side * part : (side + 1) * part] = values
        for pair in range(part // feat):
            place = side * part + pair * feat
            index = place // feat
            lanes = slice(pair * feat, (pair + 1) * feat)
            q = made[:, :part][:, lanes].T
            k = made[:, part : 2 * part][:, lanes].T
            v = values[:, lanes].T
            state[heads, index : index + 1, :] += jnp.sum(
                values[:, lanes].astype(F32), axis=0, keepdims=True
            )
            q_t[place : place + feat, :] = q
            k_t[place : place + feat, :] = k
            q_logits = nn(maps[1, index], q)
            k_logits = nn(maps[3, index], k)
            for one in range(2):
                head = 2 * index + one
                inside = slice(one * width, (one + 1) * width)
                feat_q = softmax_pair(q_logits[inside])
                feat_k = softmax_pair(k_logits[inside])
                phi_q[head, :, rows] = feat_q
                phi_k[head] = feat_k
                phi_k_nat[rows, head * feat : (head + 1) * feat] = feat_k.T
                value = jnp.concatenate([v[inside], tail], axis=0)
                v_ext[head, :, rows] = value
                state[head] = keep * state[head] + nt(value, feat_k * written)
    final[...] = state[...]


def project(normed, wa_own, wb_own, wa_oth, wb_oth, maps, aux, kept, heads, width):
    rows, dim = normed.shape
    count = rows // CHUNK
    feat = 2 * width
    return call(
        project_kernel,
        "project",
        (count,),
        [STAYS] + [whole(a) for a in (wa_own, wb_own, wa_oth, wb_oth)] + [STAYS, whole(aux)],
        [
            pl.BlockSpec((heads * width, CHUNK), lambda c, *_: (0, c)),
            pl.BlockSpec((heads * width, CHUNK), lambda c, *_: (0, c)),
            pl.BlockSpec((CHUNK, heads * width), lambda c, *_: (c, 0)),
            STAYS,
            STAYS,
            pl.BlockSpec((heads, feat, CHUNK), lambda c, *_: (0, 0, c)),
            STAYS,
            pl.BlockSpec((1, heads, EXT, feat), lambda c, *_: (c, 0, 0, 0)),
            fixed(heads + 1, EXT, feat),
        ],
        (
            streamed((heads * width, rows), LOW),
            streamed((heads * width, rows), LOW),
            streamed((rows, heads * width), LOW),
            kept_in_vmem((heads, EXT, rows), LOW),
            kept_in_vmem((heads, feat, rows), LOW),
            streamed((heads, feat, rows), LOW),
            kept_in_vmem((rows, heads * feat), LOW),
            streamed((count, heads, EXT, feat), F32),
            streamed((heads + 1, EXT, feat), F32),
        ),
        [pltpu.VMEM((heads + 1, EXT, feat), F32)],
        16,
        14,
        (kept, *pinned(normed), wa_own, wb_own, wa_oth, wb_oth, *pinned(maps), aux),
        scalars=1,
    )


def center_of(final, entering, pair, rows):
    heads, unused, feat = final.shape
    other = (pair + (heads - 1) // 4) % ((heads - 1) // 2)
    total = final[heads - 1, pair : pair + 1, :] + entering[heads - 1, other : other + 1, :]
    return jnp.broadcast_to(total * (1.0 / rows), (feat, feat))


def attend_kernel(
    carry,
    aux,
    mask,
    phi_q,
    phi_k_nat,
    v_ext,
    prefix,
    final,
    entering,
    att_t,
    att_c,
    denom,
):
    step = pl.program_id(0)
    heads, feat, unused = phi_q.shape
    width = feat // 2
    rows = at(step, CHUNK)
    reach = aux[0:1, rows]
    padding = aux[3:4, rows]
    keep = carry[step]
    mask_now = mask[0]
    for head in range(heads):
        if head % 2 == 0:
            center = center_of(final, entering, head // 2, 2 * att_t.shape[1]).T
        pq = phi_q[head, :, rows]
        scores = nn(phi_k_nat[rows, head * feat : (head + 1) * feat], pq)
        weights = scores.astype(LOW) * mask_now
        state = (prefix[0, head] + keep * entering[(head + heads // 2) % heads]).astype(LOW)
        numer = nn(v_ext[head, :, rows], weights) + reach * nn(state, pq)
        below = numer[width : width + 1] + padding
        denom[head : head + 1, rows] = below
        place = slice(head * width, (head + 1) * width)
        att = numer[:width] * (1.0 / below)
        att_t[place, rows] = att.astype(LOW)
        near = center[head % 2 * width : (head % 2 + 1) * width, :]
        att_c[place, :] = (att - jnp.concatenate([near] * (CHUNK // feat), axis=1)).astype(LOW)


def attend(aux, mask, phi_q, phi_k_nat, v_ext, prefix, final, entering, carry):
    heads, feat, rows = phi_q.shape
    width = feat // 2
    turned = kept_in_vmem((heads * width, rows), LOW)
    return call(
        attend_kernel,
        "attend",
        (rows // CHUNK,),
        [whole(aux), pl.BlockSpec((1, CHUNK, CHUNK), lambda c, *_: (c, 0, 0))]
        + [STAYS] * 3
        + [pl.BlockSpec((1, heads, EXT, feat), lambda c, *_: (c, 0, 0, 0))]
        + [whole(final), whole(entering)],
        [STAYS, pl.BlockSpec((heads * width, CHUNK), lambda c, *_: (0, c)), STAYS],
        (turned, streamed((heads * width, rows), LOW), kept_in_vmem((16, rows), F32)),
        [],
        8,
        14,
        (carry, aux, *apart(mask), *pinned(phi_q, phi_k_nat, v_ext), *apart(prefix, final, entering)),
        scalars=1,
    )


def mix_kernel(spots, tokens, norms, w_own, w_oth, att_t, hidden, normed, normed_t):
    step = pl.program_id(0)
    rows = at(step, CHUNK)
    att = att_t[:, rows].T
    part = w_own.shape[-1]
    total = tokens[...].astype(F32)
    total = total + nt(att[:, :part], flat(w_own[...])) + nt(att[:, part:], flat(w_oth[...]))
    hidden[...] = total
    xhat, unused = norm_parts(total)
    low = (xhat * norms[2:3, :] + norms[3:4, :]).astype(LOW)
    normed[rows, :] = low
    normed_t[:, rows] = low.T


def gathered(array, width, index, side):
    return pl.BlockSpec(
        (array.shape[0], 1, array.shape[2], width),
        lambda c, spots: (0, spots[3] if side == 0 else 1 - spots[3], 0, index),
        pipeline_mode=pl.Buffered(1),
    )


def mix(spots, tokens, norms, early, units, att_t):
    rows, dim = tokens.shape
    part = att_t.shape[0] // 2
    weights = [gathered(early, part, 2 * units // part, side) for side in (0, 1)]
    block = pl.BlockSpec((CHUNK, dim), lambda c, *_: (c, 0))
    return call(
        mix_kernel,
        "mix",
        (rows // CHUNK,),
        [block, whole(norms)] + weights + [STAYS],
        [block, STAYS, STAYS],
        (
            streamed((rows, dim), F32),
            kept_in_vmem((rows, dim), LOW),
            kept_in_vmem((dim, rows), LOW),
        ),
        [],
        10,
        7,
        (spots, *apart(tokens), norms, *apart(early, early), *pinned(att_t)),
        scalars=1,
    )


def feed_kernel(first, sides, spots, normed, normed_t, cot, cot_t, *refs):
    feed, grad_normed = refs[-2 - sides : -sides]
    for side in range(sides):
        fc = flat(refs[2 * side][...])
        down = flat(refs[2 * side + 1][...])
        d_weights = refs[len(refs) - sides + side]
        units = fc.shape[1]
        u = nn(normed[...], fc)
        square = u * u
        t = jnp.tanh(u * (GELU_C + (GELU_C * GELU_A) * square))
        half = 0.5 + 0.5 * t
        act = (u * half).astype(LOW)
        slope = half + (0.5 * u) * (1.0 - t * t) * (GELU_C + (3.0 * GELU_C * GELU_A) * square)
        d_weights[:, units:] = nn(cot_t[...], act).astype(LOW)
        grad = (nn(cot[...], down) * slope).astype(LOW)
        d_weights[:, :units] = nn(normed_t[...], grad).astype(LOW)
        if first and side == 0:
            feed[...] = nt(act, down)
            grad_normed[...] = nt(grad, fc)
        else:
            feed[...] += nt(act, down)
            grad_normed[...] += nt(grad, fc)


def feed_forward(spots, normed, normed_t, cot, cot_t, weights, specs, units, sums):
    rows, dim = normed.shape
    sides = len(weights) // 2
    total = kept_in_vmem((rows, dim), F32)
    return call(
        functools.partial(feed_kernel, sums is None, sides),
        "feed",
        (1,),
        [STAYS] * 4 + specs + ([] if sums is None else [STAYS] * 2),
        [STAYS] * 2 + [fixed(dim, 2 * units)] * sides,
        (total, total) + (jax.ShapeDtypeStruct((dim, 2 * units), LOW),) * sides,
        [],
        24,
        9 * sides,
        (
            spots,
            *pinned(normed, normed_t, cot, cot_t),
            *weights,
            *(() if sums is None else pinned(*sums)),
        ),
        scalars=1,
        alias=None if sums is None else {5 + 2 * sides: 0, 6 + 2 * sides: 1},
    )


def middle_kernel(
    spots,
    hidden,
    feed,
    grad_normed,
    cot,
    norms,
    w_own,
    w_oth,
    att_t,
    att_c,
    denom,
    phi_q,
    aux,
    mixed,
    grad_hidden,
    d_gain,
    d_shift,
    g_ext,
    leaving,
    d_own,
    d_oth,
    branch_t,
    state,
):
    step = pl.program_id(0)
    count = pl.num_programs(0)
    heads, feat, unused = phi_q.shape
    width = feat // 2
    rows = at(step, CHUNK)
    hid = hidden[...]
    mixed[...] = (hid + feed[rows, :]).astype(LOW)
    xhat, rstd = norm_parts(hid)
    grad = grad_normed[rows, :]
    back = cot[rows, :].astype(F32) + norm_back(grad, xhat, rstd, norms[2:3, :])
    grad_hidden[...] = back

    @pl.when(step == 0)
    def _():
        d_gain[...] = jnp.zeros_like(d_gain)
        d_shift[...] = jnp.zeros_like(d_shift)
        state[...] = jnp.zeros_like(state)

    d_gain[...] += jnp.sum(grad * xhat, axis=0, keepdims=True)
    d_shift[...] += jnp.sum(grad, axis=0, keepdims=True)
    low = back.astype(LOW)
    branch_t[:, rows] = low.T
    reach = aux[2:3, rows].astype(LOW)
    first = lax.broadcasted_iota(jnp.int32, (16, CHUNK), 0) == 0
    pair = 0
    for weights in (w_own, w_oth):
        grad_att = nn(low, flat(weights[...]))
        for inner in range(weights.shape[-1] // feat):
            turned = grad_att[:, inner * feat : (inner + 1) * feat].T
            for one in range(2):
                head = 2 * pair + one
                ga = turned[one * width : (one + 1) * width]
                inverse = 1.0 / denom[head : head + 1, rows]
                centered = att_c[head * width : (head + 1) * width, :].astype(F32)
                gd = -jnp.sum(ga * centered, axis=0, keepdims=True) * inverse
                ext = jnp.concatenate(
                    [(ga * inverse).astype(LOW), jnp.where(first, gd, 0.0).astype(LOW)], axis=0
                )
                g_ext[head, :, rows] = ext
                state[head] += nt(ext * reach, phi_q[head, :, rows])
            pair += 1
    leaving[...] = state[...].astype(LOW)

    @pl.when(step == count - 1)
    def _():
        start = 0
        for out in (d_own, d_oth):
            size = out.shape[1]
            out[...] = nt(branch_t[...], att_t[start : start + size, :]).astype(LOW)
            start += size


def middle(spots, hidden, feed, grad_normed, cot, norms, early, units, att_t, att_c, denom, phi_q, aux):
    rows, dim = hidden.shape
    heads, feat, unused = phi_q.shape
    width = feat // 2
    part = heads * width // 2
    block = pl.BlockSpec((CHUNK, dim), lambda c, *_: (c, 0))
    weights = [gathered(early, part, 2 * units // part, side) for side in (0, 1)]
    return call(
        middle_kernel,
        "middle",
        (rows // CHUNK,),
        [block]
        + [STAYS] * 3
        + [whole(norms)]
        + weights
        + [STAYS, pl.BlockSpec((heads * width, CHUNK), lambda c, *_: (0, c)), STAYS, STAYS]
        + [whole(aux)],
        [block, block, fixed(1, dim), fixed(1, dim), STAYS, fixed(heads, EXT, feat)]
        + [fixed(dim, part)] * 2,
        (
            streamed((rows, dim), LOW),
            streamed((rows, dim), F32),
            streamed((1, dim), F32),
            streamed((1, dim), F32),
            kept_in_vmem((heads, EXT, rows), LOW),
            streamed((heads, EXT, feat), LOW),
        )
        + (jax.ShapeDtypeStruct((dim, part), LOW),) * 2,
        [pltpu.VMEM((dim, rows), LOW), pltpu.VMEM((heads, EXT, feat), F32)],
        20,
        13,
        (
            spots,
            *apart(hidden),
            *pinned(feed, grad_normed, cot),
            norms,
            *apart(early, early),
            *pinned(att_t),
            *apart(att_c),
            *pinned(denom, phi_q),
            aux,
        ),
        scalars=1,
    )


def attend_back_kernel(
    side,
    carry,
    kept,
    aux,
    mask,
    phi_q,
    phi_k,
    phi_k_nat,
    v_nat,
    v_ext,
    g_ext,
    prefix,
    final,
    entering,
    arriving,
    q_t,
    k_t,
    maps,
    grads,
    d_maps,
    state,
    d_fq,
    d_fk,
):
    step = pl.program_id(0)
    count = pl.num_programs(0)
    heads, feat, unused = phi_q.shape
    width = feat // 2
    part = heads * width // 2
    half = heads // 2
    chunk = count - 1 - step
    rows = at(chunk, CHUNK)
    keep_in = carry[chunk]
    keep = kept[chunk]
    reach = aux[0:1, rows].astype(LOW)
    written = aux[1:2, rows].astype(LOW)
    mask_now = mask[0]

    @pl.when(step == 0)
    def _():
        for head in range(half):
            state[head] = arriving[(1 - side) * half + head].astype(F32)
        d_fq[...] = jnp.zeros_like(d_fq)
        d_fk[...] = jnp.zeros_like(d_fk)

    for local in range(half // 2):
        pair = side * half // 2 + local
        logit_grads = ([], [])
        value_grads = []
        lanes = slice(local * feat, (local + 1) * feat)
        center = center_of(final, entering, pair, 2 * phi_q.shape[2])
        v_pair = (v_nat[:, lanes].astype(F32) - center[:1]).astype(LOW)
        center = center.T
        for one in range(2):
            head = 2 * pair + one
            kept_head = 2 * local + one
            pq = phi_q[head, :, rows]
            pk = phi_k[kept_head]
            scores = nn(phi_k_nat[rows, head * feat : (head + 1) * feat], pq)
            weights = scores.astype(LOW) * mask_now
            ext = g_ext[head, :, rows]
            numer = ext[:width]
            blank = jnp.zeros_like(numer)
            padded = jnp.concatenate([numer, blank] if one == 0 else [blank, numer], axis=0)
            gw = nn(v_pair, padded)
            gw = (gw + ext[width : width + 1].astype(F32)).astype(LOW) * mask_now
            middle_v = center[one * width : (one + 1) * width, :]
            before = prefix[0, kept_head] + keep_in * entering[(head + heads // 2) % heads]
            before = jnp.concatenate(
                [before[:width] - middle_v * before[width : width + 1], before[width:]], axis=0
            ).astype(LOW)
            value = v_ext[head, :, rows]
            value = jnp.concatenate(
                [
                    (
                        value[:width].astype(F32) - jnp.concatenate([middle_v] * (CHUNK // feat), axis=1)
                    ).astype(LOW),
                    value[width:],
                ],
                axis=0,
            )
            after = state[kept_head].astype(LOW)
            reached = ext * reach
            g_phi_q = nn(pk, gw) + tn(before, reached)
            g_phi_k = nt(pq, gw) + tn(after, value * written)
            g_value = nt(numer, weights) + nn(after[:width], pk * written)
            value_grads.append(g_value.astype(LOW))
            state[kept_head] = keep * state[kept_head] + nt(reached, pq)
            logit_grads[0].append(softmax_pair_back(pq, g_phi_q).astype(LOW))
            logit_grads[1].append(softmax_pair_back(pk, g_phi_k).astype(LOW))
        place = slice(local * feat, (local + 1) * feat)
        base = local * feat
        for index, (both, kind, source, d_fmap) in enumerate(
            ((logit_grads[0], 0, q_t, d_fq), (logit_grads[1], 2, k_t, d_fk))
        ):
            both = jnp.concatenate(both, axis=0)
            start = base + index * part
            grads[start : start + feat, rows] = nn(maps[kind, pair], both).astype(LOW)
            d_fmap[local] += nt(source[place, :], both)
        start = base + 2 * part
        grads[start : start + feat, rows] = jnp.concatenate(value_grads, axis=0)

    @pl.when(step == count - 1)
    def _():
        first = lax.broadcasted_iota(jnp.int32, (width, feat), 1) < width
        for kind, source in enumerate((d_fq, d_fk)):
            for local in range(half // 2):
                block = source[local]
                d_maps[kind, local] = jnp.where(first, block[:width], block[width:])


def attend_back(
    side, aux, mask, phi_q, phi_k, phi_k_nat, v_nat, v_ext, g_ext, prefix, final, entering, arriving, q_t, k_t, maps, carry, kept
):
    heads, feat, rows = phi_q.shape
    width = feat // 2
    half = heads // 2
    count = rows // CHUNK
    lanes = pl.BlockSpec((half * width, CHUNK), lambda c, *_: (side, count - 1 - c))
    return call(
        functools.partial(attend_back_kernel, side),
        "attend_back",
        (rows // CHUNK,),
        [
            whole(aux),
            pl.BlockSpec((1, CHUNK, CHUNK), lambda c, *_: (count - 1 - c, 0, 0)),
            STAYS,
            pl.BlockSpec((half, feat, CHUNK), lambda c, *_: (side, 0, count - 1 - c)),
            STAYS,
            pl.BlockSpec((CHUNK, half * width), lambda c, *_: (count - 1 - c, side)),
            STAYS,
            STAYS,
            pl.BlockSpec((1, half, EXT, feat), lambda c, *_: (count - 1 - c, side, 0, 0)),
            whole(final),
            whole(entering),
            whole(arriving),
            lanes,
            lanes,
            STAYS,
        ],
        [STAYS, fixed(2, half // 2, width, feat)],
        (kept_in_vmem((3 * half * width, rows), LOW), streamed((2, half // 2, width, feat), F32)),
        [pltpu.VMEM((half, EXT, feat), F32)] + [pltpu.VMEM((half // 2, feat, feat), F32)] * 2,
        10,
        14,
        (
            carry,
            kept,
            aux,
            *apart(mask),
            *pinned(phi_q),
            *apart(phi_k),
            *pinned(phi_k_nat),
            *apart(v_nat),
            *pinned(v_ext, g_ext),
            *apart(prefix, final, entering, arriving, q_t, k_t),
            *pinned(maps),
        ),
        scalars=2,
    )


def weight_kernel(normed_t, grads, out):
    out[...] = nt(normed_t[...], grads[...]).astype(LOW)


def weight_grads(normed_t, grads):
    dim, rows = normed_t.shape
    size = grads.shape[0]
    return call(
        weight_kernel,
        "weight_grads",
        (1,),
        [whole(normed_t), STAYS],
        fixed(dim, size),
        jax.ShapeDtypeStruct((dim, size), LOW),
        [],
        8,
        4,
        (*apart(normed_t), *pinned(grads)),
    )


def first_kernel(tokens, norms, grad_hidden, wa_own, wb_own, wa_oth, wb_oth, grads_own, grads_oth, out, d_gain, d_shift):
    step = pl.program_id(0)
    rows = at(step, CHUNK)
    total = None
    for wa, wb, grads in ((wa_own, wb_own, grads_own), (wa_oth, wb_oth, grads_oth)):
        cut = wa.shape[1]
        term = nn(wa[...], grads[:cut, rows]) + nn(wb[...], grads[cut:, rows])
        total = term if total is None else total + term
    grad = total.T
    xhat, rstd = norm_parts(tokens[...].astype(F32))
    out[...] = (grad_hidden[...] + norm_back(grad, xhat, rstd, norms[0:1, :])).astype(LOW)

    @pl.when(step == 0)
    def _():
        d_gain[...] = jnp.zeros_like(d_gain)
        d_shift[...] = jnp.zeros_like(d_shift)

    d_gain[...] += jnp.sum(grad * xhat, axis=0, keepdims=True)
    d_shift[...] += jnp.sum(grad, axis=0, keepdims=True)


def first_back(tokens, norms, grad_hidden, weights, grads):
    rows, dim = tokens.shape
    block = pl.BlockSpec((CHUNK, dim), lambda c: (c, 0))
    return call(
        first_kernel,
        "first_back",
        (rows // CHUNK,),
        [block, whole(norms), block] + [whole(w) for w in weights] + [STAYS] * 2,
        [block, fixed(1, dim), fixed(1, dim)],
        (
            streamed((rows, dim), LOW),
            streamed((1, dim), F32),
            streamed((1, dim), F32),
        ),
        [],
        16,
        9,
        (*apart(tokens), norms, *apart(grad_hidden), *weights, *pinned(*grads)),
    )


SWAP = [(0, 1), (1, 0)]


def swap(piece):
    return lax.ppermute(piece, "mp", SWAP)


def flip(piece, bit, size):
    return lax.ppermute(piece, "dp", [(i, i ^ bit) for i in range(size)])


def turn(piece, by, size):
    return lax.ppermute(piece, "dp", [(i, (i + by) % size) for i in range(size)])


def after(value, *others):
    return lax.optimization_barrier((value, *others))[0]


class Places:
    def __init__(self, size):
        self.size = size
        self.deep = size // 4
        place = lax.axis_index("dp")
        self.spots = jnp.stack([place % 2, (place // 2) % 2, place // 4, lax.axis_index("mp")])

    def flip(self, value, axis):
        return flip(value, 1 if axis == "x" else 2, self.size)


def line_kernel(cut, spots, *refs):
    deep = len(refs) - 2
    for s in range(deep):
        spot = lax.rem(spots[2] + deep - s, deep)
        refs[-2][spot] = refs[s][:, :cut]
        refs[-1][spot] = refs[s][:, cut:]


def gather_line(shard, cut, at, *others):
    pieces = [shard] + [turn(shard, 4 * s, at.size) for s in range(1, at.deep)]
    if others:
        pieces[1] = after(pieces[1], *others)
    rows, columns = shard.shape
    shapes = [(at.deep, rows, cut), (at.deep, rows, columns - cut)]
    return call(
        functools.partial(line_kernel, cut),
        "line",
        (1,),
        [whole(p) for p in pieces],
        [fixed(*shape) for shape in shapes],
        tuple(jax.ShapeDtypeStruct(shape, LOW) for shape in shapes),
        [],
        6,
        0,
        (at.spots, *pieces),
        scalars=1,
    )


def pair_kernel(axes, dims, spots, *refs):
    for index, (axis, dim) in enumerate(zip(axes, dims)):
        mine, theirs, out = refs[2 * index], refs[2 * index + 1], refs[4 + index]
        bit = spots[0 if axis == "x" else 1]
        for source, place in ((mine, bit), (theirs, 1 - bit)):
            if dim == 1:
                out[:, pl.ds(place, 1)] = source[...][:, None]
            else:
                out[:, :, pl.ds(place, 1)] = source[...][:, :, None]


def first_by(shape):
    tail = (0,) * (len(shape) - 1)
    return pl.BlockSpec((1, *shape[1:]), lambda d, *_: (d, *tail))


def gather_pair(values, axes, at, *others, kind=jax.ShapeDtypeStruct):
    moved = [at.flip(v, axis) for v, axis in zip(values, axes)]
    if others:
        moved[0] = after(moved[0], *others)
    dims = [v.ndim - 2 if axis == "x" else 1 for v, axis in zip(values, axes)]
    shapes = [(*v.shape[:d], 2, *v.shape[d:]) for v, d in zip(values, dims)]
    return call(
        functools.partial(pair_kernel, axes, dims),
        "pair",
        (at.deep,),
        [first_by(v.shape) for v in values for unused in (0, 1)],
        [first_by(shape) for shape in shapes],
        tuple(kind(shape, LOW) for shape in shapes),
        [],
        8,
        0,
        (at.spots, values[0], moved[0], values[1], moved[1]),
        scalars=1,
    )


def first_fold_kernel(axes, cuts, spots, *refs):
    outs = refs[-4:]
    for index, axis in enumerate(axes):
        bit = spots[0 if axis == "x" else 1]
        sent, kept = outs[2 * index : 2 * index + 2]
        start = 0
        for segment, cut in enumerate(cuts):
            pair = refs[2 * segment : 2 * segment + 2]
            columns = slice(0, cut) if index == 0 else slice(cut, pair[0].shape[-1])
            size = columns.stop - columns.start
            for out, place in ((sent, 1 - bit), (kept, bit)):
                if axis == "x":
                    terms = [r[:, :, pl.ds(place, 1), :, columns].astype(F32) for r in pair]
                else:
                    terms = [r[:, pl.ds(place, 1), :, :, columns].astype(F32) for r in pair]
                total = (terms[0] + terms[1]).astype(LOW)
                out[..., start : start + size] = total.reshape(*out.shape[:-1], size)
            start += size


def fold_kernel(axes, spots, *refs):
    for index, axis in enumerate(axes):
        bit = spots[0 if axis == "x" else 1]
        sent, kept = refs[4 + 2 * index : 6 + 2 * index]
        for out, place in ((sent, 1 - bit), (kept, bit)):
            terms = [r[:, pl.ds(place, 1)].astype(F32) for r in refs[2 * index : 2 * index + 2]]
            out[...] = (terms[0] + terms[1]).astype(LOW).reshape(out.shape)


def spread_kernel(spots, a_kept, a_sent, b_kept, b_sent, *outs):
    deep = len(outs)
    cut = a_kept.shape[-1]
    for s, out in enumerate(outs):
        spot = lax.rem(spots[2] + s, deep)
        out[:, :cut] = (a_kept[spot].astype(F32) + a_sent[spot].astype(F32)).astype(LOW)
        out[:, cut:] = (b_kept[spot].astype(F32) + b_sent[spot].astype(F32)).astype(LOW)


class Scatter:
    def __init__(self, segments, at):
        self.at = at
        self.cuts = [cut for own, oth, cut in segments]
        self.cut = sum(self.cuts)
        self.terms = [[own, swap(oth)] for own, oth, cut in segments]
        if at.size % 4 == 0:
            split = lambda v: v.reshape(at.deep, 2, 2, v.shape[0] // at.size, v.shape[1])
            self.terms = [[split(v) for v in pair] for pair in self.terms]

    def wait_for(self, *others):
        self.terms[0][1] = after(self.terms[0][1], *others)

    def fold(self, axes):
        at = self.at
        flats = [v for pair in self.terms for v in pair]
        if at.size % 4:
            return flats[0]
        if self.cuts:
            columns = sum(pair[0].shape[-1] for pair in self.terms)
            head = flats[0].shape[:2]
            rows = flats[0].shape[3]
            lefts = [(*head, rows, self.cut), (*head, rows, columns - self.cut)]
            kernel = functools.partial(first_fold_kernel, axes, tuple(self.cuts))
        else:
            lefts = [(v.shape[0], *v.shape[2:]) for v in flats[::2]]
            kernel = functools.partial(fold_kernel, axes)
        outs = [left for left in lefts for unused in (0, 1)]
        a_sent, a_kept, b_sent, b_kept = call(
            kernel,
            "fold",
            (at.deep,),
            [first_by(v.shape) for v in flats],
            [first_by(left) for left in outs],
            tuple(jax.ShapeDtypeStruct(left, LOW) for left in outs),
            [],
            12,
            0,
            (at.spots, *flats),
            scalars=1,
        )
        self.cuts = []
        self.terms = [[a_kept, at.flip(a_sent, axes[0])], [b_kept, at.flip(b_sent, axes[1])]]
        return a_kept

    def spread(self):
        at = self.at
        if at.size % 4:
            return self.terms[0][0]
        a, b = self.terms
        shape = (a[0].shape[1], self.cut + b[0].shape[-1])
        own, *sends = call(
            spread_kernel,
            "spread",
            (1,),
            [whole(v) for v in (*a, *b)],
            [fixed(*shape)] * at.deep,
            (jax.ShapeDtypeStruct(shape, LOW),) * at.deep,
            [],
            8,
            0,
            (at.spots, *a, *b),
            scalars=1,
        )
        self.parts = [own] + [turn(p, 4 * s, at.size) for s, p in enumerate(sends, 1)]
        return own

    def end(self, *others):
        if self.at.size % 4:
            sums = [own.astype(F32) + moved.astype(F32) for own, moved in self.terms]
            total = [t[:, :cut] for t, cut in zip(sums, self.cuts)] + [t[:, cut:] for t, cut in zip(sums, self.cuts)]
            total = lax.psum_scatter(jnp.concatenate(total, axis=1), "dp", scatter_dimension=0, tiled=True)
        else:
            if others:
                self.parts[1] = after(self.parts[1], *others)
            total = sum(p.astype(F32) for p in self.parts)
        return total


def add_along(value, steps, size):
    for step in steps:
        if step < size:
            value = value.astype(LOW)
            value = value.astype(F32) + flip(value, step, size).astype(F32)
    return value


def per_device(
    size,
    tokens,
    norm1_gain,
    norm1_shift,
    w_query,
    w_key,
    w_value,
    w_out,
    fmap_query,
    fmap_key,
    norm2_gain,
    norm2_shift,
    w_fc,
    w_down,
    lengths,
    cotangent,
):
    rows, dim = tokens.shape
    heads = 2 * fmap_query.shape[0]
    width = fmap_query.shape[1]
    feat = 2 * width
    part = w_query.shape[1]
    count = rows // CHUNK
    core = lax.axis_index("mp")

    ends = jnp.cumsum(lengths[0])
    places = core * rows - 1 + jnp.arange(rows + 1, dtype=jnp.int32)
    numbers = jnp.sum((ends[None, :] <= places[:, None]).astype(jnp.int32), axis=1)
    numbers = jnp.where(places < 0, -1, numbers)
    segment = numbers[1:]
    living = places[1:] < ends[-1]
    blocks = segment.reshape(count, CHUNK)
    last = blocks[:, -1]
    before = jnp.concatenate([numbers[:1], last[:-1]])
    kept = (last == before).astype(F32)
    carry = ((before == numbers[0]) & (core > 0)).astype(F32)
    reach = (blocks == before[:, None]).reshape(rows) & living
    written = (blocks == last[:, None]).reshape(rows)
    reach_in = (segment == numbers[0]) & living
    aux = jnp.stack([reach, written, reach_in, ~living] + [jnp.zeros_like(living)] * 4).astype(F32)
    order = jnp.arange(CHUNK, dtype=jnp.int32)
    mask = (
        (blocks[:, :, None] == blocks[:, None, :])
        & (order[:, None] <= order[None, :])
        & living.reshape(count, 1, CHUNK)
    ).astype(LOW)

    norms = jnp.stack([norm1_gain, norm1_shift, norm2_gain, norm2_shift])

    where = Places(size)
    staged = size % 4 == 0
    units = w_fc.shape[1] // 2
    cut = (3 * part // feat + 1) // 2 * feat
    cut_out = (part // feat + 1) // 2 * feat
    shard_qkv = jnp.concatenate([w_query, w_key, w_value], axis=1)
    shard_early = jnp.concatenate([w_fc[:, :units], w_down[:, :units], w_out], axis=1)
    shard_late = jnp.concatenate([w_fc[:, units:], w_down[:, units:]], axis=1)
    early = lax.all_gather(shard_early, ("dp", "mp"), axis=0)
    early = early.reshape(size, 2, *shard_early.shape)
    if shard_early.shape[0] % 16:
        early = early.swapaxes(0, 1).reshape(1, 2, dim, -1)
    fq_oth, fk_oth = swap(fmap_query), swap(fmap_key)
    ready = lax.optimization_barrier((shard_late, norms, aux, mask, kept, carry, where.spots))
    shard_late, norms, aux, mask, kept, carry, spots = ready
    where.spots = spots
    if staged:
        qkv = gather_line(shard_qkv, cut, where)
        qkv = gather_pair(qkv, "xy", where)
        shard_late, tokens = after(shard_late, qkv[0]), after(tokens, qkv[0])
    normed1, normed1_t, cot, cot_t, maps = prepare(
        tokens, cotangent, norms, fmap_query, fq_oth, fmap_key, fk_oth
    )
    if staged:
        qkv = tuple(map(flat, gather_pair(qkv, "yx", where, maps)))
    else:
        qkv, late = (
            tuple(lax.all_gather(s, "dp", axis=0, tiled=True) for s in shards)
            for shards in (
                (shard_qkv[:, :cut], shard_qkv[:, cut:]),
                (shard_late[:, :units], shard_late[:, units:]),
            )
        )
    qkv = (*qkv, *map(swap, qkv))
    q_t, k_t, v_nat, v_ext, phi_q, phi_k, phi_k_nat, prefix, final = project(
        normed1, *qkv, maps, aux, kept, heads, width
    )
    if staged:
        late = gather_line(shard_late, units, where, final)
        final = after(final, late[0])
    entering = swap(final)
    att_t, att_c, denom = attend(aux, mask, phi_q, phi_k_nat, v_ext, prefix, final, entering, carry)
    if staged:
        late = gather_pair(late, "xy", where, denom)
        att_t = after(att_t, late[0])
    hidden, normed2, normed2_t = mix(spots, tokens, norms, early, units, att_t)
    feed_part = functools.partial(feed_forward, spots, normed2, normed2_t, cot, cot_t)
    early_specs = [[gathered(early, units, index, side) for index in (0, 1)] for side in (0, 1)]
    feed, grad_normed, *d_early_oth = feed_part(apart(early, early), early_specs[1], units, None)
    if staged:
        late = tuple(map(flat, gather_pair(late, "yx", where, d_early_oth[0], kind=streamed)))
        feed = after(feed, late[0])
    feed, grad_normed, *d_early_own = feed_part(
        apart(early, early), early_specs[0], units, (feed, grad_normed)
    )
    sums_early = Scatter([(*d_early_own, *d_early_oth, units)], where)
    late_oth = tuple(map(swap, late))
    feed = after(feed, sums_early.fold("xy"))
    feed, grad_normed, d_late_own, d_late_oth = feed_part(
        (*late, *late_oth), [whole(w) for w in late] * 2, units, (feed, grad_normed)
    )
    sums_early.wait_for(d_late_oth)
    hidden = after(hidden, sums_early.fold("yx"))
    mixed, grad_hidden, d_gain2, d_shift2, g_ext, leaving, d_out_own, d_out_oth = middle(
        spots, hidden, feed, grad_normed, cot, norms, early, units, att_t, att_c, denom, phi_q, aux
    )
    sums_early.wait_for(d_gain2)
    leaving = after(leaving, sums_early.spread())
    arriving = lax.ppermute(leaving, "mp", [(1, 0)])
    sums_late = Scatter([(d_late_own, d_late_oth, units), (d_out_own, d_out_oth, cut_out)], where)
    back = functools.partial(
        attend_back, carry=carry, kept=kept, prefix=prefix, final=final, entering=entering, q_t=q_t, k_t=k_t, maps=maps
    )
    back_inputs = (aux, mask, phi_q, phi_k, phi_k_nat, v_nat, v_ext, g_ext)
    lanes = lambda v: v.reshape(-1, feat)
    grads_oth, maps_oth = back(1, *back_inputs, arriving=arriving)
    sums_late.wait_for(maps_oth)
    grads_oth = after(grads_oth, sums_late.fold("xy"))
    total_early = sums_early.end(maps_oth)
    maps_oth = swap(maps_oth)
    d_qkv_oth = weight_grads(normed1_t, grads_oth)
    arriving = after(arriving, d_qkv_oth, total_early)
    grads_own, maps_own = back(0, *back_inputs, arriving=arriving)
    sums_late.wait_for(maps_own)
    grads_own = after(grads_own, sums_late.fold("yx"))
    map_grads = add_along(lanes(maps_own + maps_oth), [1], size)
    d_qkv_own = weight_grads(normed1_t, grads_own)
    sums_qkv = Scatter([(d_qkv_own, d_qkv_oth, cut)], where)
    grad_hidden = after(grad_hidden, sums_qkv.fold("xy"))
    sums_late.wait_for(d_qkv_own)
    grad_hidden = after(grad_hidden, sums_late.spread())
    map_grads = add_along(after(map_grads, d_qkv_own), [2], size)
    grad_tokens, d_gain1, d_shift1 = first_back(tokens, norms, grad_hidden, qkv, (grads_own, grads_oth))
    sums_qkv.wait_for(d_gain1)
    norm_grads = jnp.concatenate([d_gain1, d_shift1, d_gain2, d_shift2], axis=0)
    norm_grads = lanes(after(norm_grads, sums_qkv.fold("yx")))
    norm_grads = add_along(norm_grads + swap(norm_grads), [1, 2], size)
    small = jnp.concatenate([map_grads, norm_grads], axis=0)
    small = add_along(after(small, sums_qkv.spread()), [4 << i for i in range(size.bit_length() - 3)], size)
    map_grads = small[: map_grads.shape[0]].reshape(2, heads // 4, width, 2, width)
    map_grads = map_grads.swapaxes(2, 3).reshape(2, heads // 2, width, width)
    norm_grads = small[-norm_grads.shape[0] :].reshape(4, dim)
    total_late = sums_late.end()
    grad_qkv = sums_qkv.end()
    cut_late = units + cut_out
    return (
        mixed,
        grad_tokens,
        norm_grads[0],
        norm_grads[1],
        grad_qkv[:, :part],
        grad_qkv[:, part : 2 * part],
        grad_qkv[:, 2 * part :],
        jnp.concatenate([total_late[:, units:cut_late], total_late[:, cut_late + units :]], axis=1),
        map_grads[0],
        map_grads[1],
        norm_grads[2],
        norm_grads[3],
        jnp.concatenate([total_early[:, :units], total_late[:, :units]], axis=1),
        jnp.concatenate([total_early[:, units:], total_late[:, cut_late : cut_late + units]], axis=1),
    )


def solution(mesh):
    placed = (
        P(("dp", "mp"), None),
        P(),
        P(),
        P("dp", "mp"),
        P("dp", "mp"),
        P("dp", "mp"),
        P("dp", "mp"),
        P("mp", None, None),
        P("mp", None, None),
        P(),
        P(),
        P("dp", "mp"),
        P("dp", "mp"),
        P("dp", None),
        P(("dp", "mp"), None),
    )
    return jax.shard_map(
        functools.partial(per_device, mesh.shape["dp"]),
        mesh=mesh,
        in_specs=placed,
        out_specs=(
            P(("dp", "mp"), None),
            P(("dp", "mp"), None),
            P(),
            P(),
            P("dp", "mp"),
            P("dp", "mp"),
            P("dp", "mp"),
            P("dp", "mp"),
            P("mp", None, None),
            P("mp", None, None),
            P(),
            P(),
            P("dp", "mp"),
            P("dp", "mp"),
        ),
        check_vma=False,
    )
```

```python
import functools

import jax
import jax.numpy as jnp
from jax import lax
from jax.experimental import pallas as pl
from jax.experimental.pallas import tpu as pltpu
from jax.sharding import PartitionSpec as P

EPS = 1e-05
CHUNK = 256
EXT = 80
LOW = jnp.bfloat16
F32 = jnp.float32
MIB = 1024 * 1024
PACE = 3_000_000_000
GELU_C = 0.7978845608028654
GELU_A = 0.044715


def nn(a, b):
    return lax.dot_general(a, b, (((1,), (0,)), ((), ())), preferred_element_type=F32)


def nt(a, b):
    return lax.dot_general(a, b, (((1,), (1,)), ((), ())), preferred_element_type=F32)


def tn(a, b):
    return lax.dot_general(a, b, (((0,), (0,)), ((), ())), preferred_element_type=F32)


def norm_parts(rows):
    center = rows - jnp.mean(rows, axis=-1, keepdims=True)
    spread = jnp.mean(center * center, axis=-1, keepdims=True)
    rstd = lax.rsqrt(spread + EPS)
    return center * rstd, rstd


def norm_back(grad, xhat, rstd, gain):
    e = grad * gain
    return rstd * (
        e - jnp.mean(e, axis=-1, keepdims=True) - xhat * jnp.mean(e * xhat, axis=-1, keepdims=True)
    )


def softmax_pair(logits):
    high = jnp.max(logits, axis=0, keepdims=True)
    least = jnp.min(logits, axis=0, keepdims=True)
    pos = jnp.exp(logits - high)
    neg = jnp.exp(least - logits)
    pos = pos * (1.0 / jnp.sum(pos, axis=0, keepdims=True))
    neg = neg * (1.0 / jnp.sum(neg, axis=0, keepdims=True))
    return jnp.concatenate([pos, neg], axis=0).astype(LOW)


def softmax_pair_back(phi, grad):
    width = phi.shape[0] // 2
    pos = phi[:width].astype(F32)
    neg = phi[width:].astype(F32)
    gp = grad[:width]
    gn = grad[width:]
    gp = gp - jnp.sum(pos * gp, axis=0, keepdims=True)
    gn = gn - jnp.sum(neg * gn, axis=0, keepdims=True)
    return pos * gp - neg * gn


def flat(value):
    return value.reshape(-1, value.shape[-1])


def kept_in_vmem(shape, dtype):
    return pltpu.VMEM(shape, dtype)


def streamed(shape, dtype):
    return pltpu.HBM(shape, dtype)


def apart(*arrays):
    return tuple(pltpu.with_memory_space_constraint(a, pltpu.HBM) for a in arrays)


def pinned(*arrays):
    return tuple(pltpu.with_memory_space_constraint(a, pltpu.VMEM) for a in arrays)


def whole(array):
    return pl.BlockSpec(
        array.shape, lambda *_: (0,) * array.ndim, pipeline_mode=pl.Buffered(1)
    )


def fixed(*shape):
    return pl.BlockSpec(shape, lambda *_: (0,) * len(shape))


STAYS = pl.BlockSpec(memory_space=pltpu.VMEM)


def at(step, size):
    return pl.ds(pl.multiple_of(step * size, size), size)


def call(kernel, name, grid, in_specs, out_specs, out_shape, scratch, limit, micros, args, scalars=0, alias=None):
    return pl.pallas_call(
        kernel,
        grid_spec=pltpu.PrefetchScalarGridSpec(
            num_scalar_prefetch=scalars,
            grid=grid,
            in_specs=in_specs,
            out_specs=out_specs,
            scratch_shapes=scratch,
        ),
        out_shape=out_shape,
        input_output_aliases=alias or {},
        compiler_params=pltpu.CompilerParams(vmem_limit_bytes=limit * MIB),
        cost_estimate=pl.CostEstimate(flops=micros * PACE, bytes_accessed=1024, transcendentals=0),
        name=name,
    )(*args)


def pack_kernel(groups, *refs):
    outs = refs[len(refs) - len(groups) :]
    for out, group in zip(outs, groups):
        start = 0
        for index, first, size in group:
            out[:, start : start + size] = refs[index][:, first : first + size]
            start += size


def pack(arrays, groups):
    rows = arrays[0].shape[0]
    shapes = [(rows, sum(size for unused, first, size in group)) for group in groups]
    return call(
        functools.partial(pack_kernel, groups),
        "pack",
        (1,),
        [whole(a) for a in arrays],
        [fixed(*shape) for shape in shapes],
        tuple(jax.ShapeDtypeStruct(shape, LOW) for shape in shapes),
        [],
        8,
        1,
        apart(*arrays),
    )


def prepare_kernel(
    tokens, cot, norms, fq_own, fq_oth, fk_own, fk_oth, normed, normed_t, held_cot, cot_t, maps
):
    step = pl.program_id(0)
    rows = at(step, CHUNK)
    xhat, unused = norm_parts(tokens[...].astype(F32))
    low = (xhat * norms[0:1, :] + norms[1:2, :]).astype(LOW)
    normed[rows, :] = low
    normed_t[...] = low.T
    held_cot[rows, :] = cot[...]
    cot_t[:, rows] = cot[...].T

    @pl.when(step == 0)
    def _():
        half, width, unused = fq_own.shape
        blank = jnp.zeros((width, width), F32)
        for kind, (own, oth) in enumerate(((fq_own, fq_oth), (fk_own, fk_oth))):
            for pair in range(half):
                source = own if pair < half // 2 else oth
                first = 2 * pair % half
                block = jnp.concatenate(
                    [
                        jnp.concatenate([source[first].astype(F32), blank], axis=1),
                        jnp.concatenate([blank, source[first + 1].astype(F32)], axis=1),
                    ],
                    axis=0,
                )
                maps[2 * kind, pair] = block.astype(LOW)
                maps[2 * kind + 1, pair] = block.T.astype(LOW)


def prepare(tokens, cot, norms, fq_own, fq_oth, fk_own, fk_oth):
    rows, dim = tokens.shape
    half, width, unused = fq_own.shape
    block = pl.BlockSpec((CHUNK, dim), lambda c: (c, 0))
    natural = kept_in_vmem((rows, dim), LOW)
    turned = kept_in_vmem((dim, rows), LOW)
    return call(
        prepare_kernel,
        "prepare",
        (rows // CHUNK,),
        [block, block] + [whole(a) for a in (norms, fq_own, fq_oth, fk_own, fk_oth)],
        [STAYS, pl.BlockSpec((dim, CHUNK), lambda c: (0, c))] + [STAYS] * 3,
        (natural, streamed((dim, rows), LOW), natural, turned, kept_in_vmem((4, half, 2 * width, 2 * width), LOW)),
        [],
        8,
        5,
        (*apart(tokens, cot), norms, fq_own, fq_oth, fk_own, fk_oth),
    )


def project_kernel(
    kept,
    normed,
    wa_own,
    wb_own,
    wa_oth,
    wb_oth,
    maps,
    aux,
    q_t,
    k_t,
    v_nat,
    v_ext,
    phi_q,
    phi_k,
    phi_k_nat,
    prefix,
    final,
    state,
):
    step = pl.program_id(0)
    heads, feat, unused = phi_q.shape
    width = feat // 2
    rows = at(step, CHUNK)
    normed_now = normed[rows, :]
    written = aux[1:2, rows].astype(LOW)
    tail = jnp.where(lax.broadcasted_iota(jnp.int32, (16, CHUNK), 0) == 0, 1.0, 0.0).astype(LOW)

    @pl.when(step == 0)
    def _():
        state[...] = jnp.zeros_like(state)

    prefix[0] = state[:heads]
    keep = kept[step]
    halves = ((wa_own, wb_own), (wa_oth, wb_oth))
    made = [jnp.concatenate([nn(normed_now, w[...]) for w in half], axis=1).astype(LOW) for half in halves]
    part = made[0].shape[1] // 3
    pairs = part // feat
    for side in range(2):
        values = made[side][:, 2 * part :]
        v_nat[:, side * part : (side + 1) * part] = values
        turned = [
            [made[side][:, kind * part + p * feat : kind * part + (p + 1) * feat].T for p in range(pairs)]
            for kind in range(3)
        ]
        indices = [side * pairs + p for p in range(pairs)]
        logits = [
            [nn(maps[2 * kind + 1, index], piece) for index, piece in zip(indices, turned[kind])]
            for kind in range(2)
        ]
        for p, index in enumerate(indices):
            place = slice(index * feat, (index + 1) * feat)
            q_t[place, :] = turned[0][p]
            k_t[place, :] = turned[1][p]
            state[heads, index : index + 1, :] += jnp.sum(
                values[:, p * feat : (p + 1) * feat].astype(F32), axis=0, keepdims=True
            )
        inside = [slice(one * width, (one + 1) * width) for one in range(2)]
        feats_q = [softmax_pair(piece[lines]) for piece in logits[0] for lines in inside]
        feats_k = [softmax_pair(piece[lines]) for piece in logits[1] for lines in inside]
        extended = [jnp.concatenate([piece[lines], tail], axis=0) for piece in turned[2] for lines in inside]
        more = [nt(value, feat_k * written) for value, feat_k in zip(extended, feats_k)]
        for local in range(2 * pairs):
            head = 2 * side * pairs + local
            phi_q[head, :, rows] = feats_q[local]
            phi_k[head] = feats_k[local]
            phi_k_nat[rows, head * feat : (head + 1) * feat] = feats_k[local].T
            v_ext[head, :, rows] = extended[local]
            state[head] = keep * state[head] + more[local]
    final[...] = state[...]


def project(normed, wa_own, wb_own, wa_oth, wb_oth, maps, aux, kept, heads, width):
    rows, dim = normed.shape
    count = rows // CHUNK
    feat = 2 * width
    return call(
        project_kernel,
        "project",
        (count,),
        [STAYS] + [whole(a) for a in (wa_own, wb_own, wa_oth, wb_oth)] + [STAYS, whole(aux)],
        [
            pl.BlockSpec((heads * width, CHUNK), lambda c, *_: (0, c)),
            pl.BlockSpec((heads * width, CHUNK), lambda c, *_: (0, c)),
            pl.BlockSpec((CHUNK, heads * width), lambda c, *_: (c, 0)),
            STAYS,
            STAYS,
            pl.BlockSpec((heads, feat, CHUNK), lambda c, *_: (0, 0, c)),
            STAYS,
            pl.BlockSpec((1, heads, EXT, feat), lambda c, *_: (c, 0, 0, 0)),
            fixed(heads + 1, EXT, feat),
        ],
        (
            streamed((heads * width, rows), LOW),
            streamed((heads * width, rows), LOW),
            streamed((rows, heads * width), LOW),
            kept_in_vmem((heads, EXT, rows), LOW),
            kept_in_vmem((heads, feat, rows), LOW),
            streamed((heads, feat, rows), LOW),
            kept_in_vmem((rows, heads * feat), LOW),
            streamed((count, heads, EXT, feat), F32),
            streamed((heads + 1, EXT, feat), F32),
        ),
        [pltpu.VMEM((heads + 1, EXT, feat), F32)],
        16,
        14,
        (kept, *pinned(normed), wa_own, wb_own, wa_oth, wb_oth, *pinned(maps), aux),
        scalars=1,
    )


def center_of(final, entering, pair, rows):
    heads, unused, feat = final.shape
    other = (pair + (heads - 1) // 4) % ((heads - 1) // 2)
    total = final[heads - 1, pair : pair + 1, :] + entering[heads - 1, other : other + 1, :]
    return jnp.broadcast_to(total * (1.0 / rows), (feat, feat))


def attend_kernel(
    carry,
    aux,
    mask,
    phi_q,
    phi_k_nat,
    v_ext,
    prefix,
    final,
    entering,
    att_t,
    att_c,
    denom,
):
    step = pl.program_id(0)
    heads, feat, unused = phi_q.shape
    width = feat // 2
    rows = at(step, CHUNK)
    reach = aux[0:1, rows]
    padding = aux[3:4, rows]
    keep = carry[step]
    mask_now = mask[0]
    half = heads // 2
    centers = [center_of(final, entering, pair, 2 * att_t.shape[1]).T for pair in range(half)]
    for side in range(2):
        group = range(side * half, (side + 1) * half)
        pqs = [phi_q[head, :, rows] for head in group]
        states = [(prefix[0, head] + keep * entering[(head + half) % heads]).astype(LOW) for head in group]
        scores = [
            nn(phi_k_nat[rows, head * feat : (head + 1) * feat], pq) for head, pq in zip(group, pqs)
        ]
        inter = [nn(state, pq) for state, pq in zip(states, pqs)]
        weights = [score.astype(LOW) * mask_now for score in scores]
        numers = [
            nn(v_ext[head, :, rows], weight) + reach * more
            for head, weight, more in zip(group, weights, inter)
        ]
        for head, numer in zip(group, numers):
            below = numer[width : width + 1] + padding
            denom[head : head + 1, rows] = below
            place = slice(head * width, (head + 1) * width)
            att = numer[:width] * (1.0 / below)
            att_t[place, rows] = att.astype(LOW)
            near = centers[head // 2][head % 2 * width : (head % 2 + 1) * width, :]
            att_c[place, :] = (att - jnp.concatenate([near] * (CHUNK // feat), axis=1)).astype(LOW)


def attend(aux, mask, phi_q, phi_k_nat, v_ext, prefix, final, entering, carry):
    heads, feat, rows = phi_q.shape
    width = feat // 2
    turned = kept_in_vmem((heads * width, rows), LOW)
    return call(
        attend_kernel,
        "attend",
        (rows // CHUNK,),
        [whole(aux), pl.BlockSpec((1, CHUNK, CHUNK), lambda c, *_: (c, 0, 0))]
        + [STAYS] * 3
        + [pl.BlockSpec((1, heads, EXT, feat), lambda c, *_: (c, 0, 0, 0))]
        + [whole(final), whole(entering)],
        [STAYS, pl.BlockSpec((heads * width, CHUNK), lambda c, *_: (0, c)), STAYS],
        (turned, streamed((heads * width, rows), LOW), kept_in_vmem((16, rows), F32)),
        [],
        8,
        14,
        (carry, aux, *apart(mask), *pinned(phi_q, phi_k_nat, v_ext), *apart(prefix, final, entering)),
        scalars=1,
    )


def mix_kernel(spots, tokens, norms, w_own, w_oth, att_t, hidden, normed, normed_t):
    step = pl.program_id(0)
    rows = at(step, CHUNK)
    att = att_t[:, rows].T
    part = w_own.shape[-1]
    total = tokens[...].astype(F32)
    total = total + nt(att[:, :part], flat(w_own[...])) + nt(att[:, part:], flat(w_oth[...]))
    hidden[...] = total
    xhat, unused = norm_parts(total)
    low = (xhat * norms[2:3, :] + norms[3:4, :]).astype(LOW)
    normed[rows, :] = low
    normed_t[:, rows] = low.T


def gathered(array, width, index, side):
    return pl.BlockSpec(
        (array.shape[0], 1, array.shape[2], width),
        lambda c, spots: (0, spots[3] if side == 0 else 1 - spots[3], 0, index),
        pipeline_mode=pl.Buffered(1),
    )


def mix(spots, tokens, norms, early, units, att_t):
    rows, dim = tokens.shape
    part = att_t.shape[0] // 2
    weights = [gathered(early, part, 2 * units // part, side) for side in (0, 1)]
    block = pl.BlockSpec((CHUNK, dim), lambda c, *_: (c, 0))
    return call(
        mix_kernel,
        "mix",
        (rows // CHUNK,),
        [block, whole(norms)] + weights + [STAYS],
        [block, STAYS, STAYS],
        (
            streamed((rows, dim), F32),
            kept_in_vmem((rows, dim), LOW),
            kept_in_vmem((dim, rows), LOW),
        ),
        [],
        10,
        7,
        (spots, *apart(tokens), norms, *apart(early, early), *pinned(att_t)),
        scalars=1,
    )


def feed_kernel(first, sides, spots, normed, normed_t, cot, cot_t, *refs):
    feed, grad_normed = refs[-2 - sides : -sides]
    for side in range(sides):
        fc = flat(refs[2 * side][...])
        down = flat(refs[2 * side + 1][...])
        d_weights = refs[len(refs) - sides + side]
        units = fc.shape[1]
        u = nn(normed[...], fc)
        square = u * u
        t = jnp.tanh(u * (GELU_C + (GELU_C * GELU_A) * square))
        half = 0.5 + 0.5 * t
        act = (u * half).astype(LOW)
        slope = half + (0.5 * u) * (1.0 - t * t) * (GELU_C + (3.0 * GELU_C * GELU_A) * square)
        d_weights[:, units:] = nn(cot_t[...], act).astype(LOW)
        grad = (nn(cot[...], down) * slope).astype(LOW)
        d_weights[:, :units] = nn(normed_t[...], grad).astype(LOW)
        if first and side == 0:
            feed[...] = nt(act, down)
            grad_normed[...] = nt(grad, fc)
        else:
            feed[...] += nt(act, down)
            grad_normed[...] += nt(grad, fc)


def feed_forward(spots, normed, normed_t, cot, cot_t, weights, specs, units, sums):
    rows, dim = normed.shape
    sides = len(weights) // 2
    total = kept_in_vmem((rows, dim), F32)
    return call(
        functools.partial(feed_kernel, sums is None, sides),
        "feed",
        (1,),
        [STAYS] * 4 + specs + ([] if sums is None else [STAYS] * 2),
        [STAYS] * 2 + [fixed(dim, 2 * units)] * sides,
        (total, total) + (jax.ShapeDtypeStruct((dim, 2 * units), LOW),) * sides,
        [],
        24,
        9 * sides,
        (
            spots,
            *pinned(normed, normed_t, cot, cot_t),
            *weights,
            *(() if sums is None else pinned(*sums)),
        ),
        scalars=1,
        alias=None if sums is None else {5 + 2 * sides: 0, 6 + 2 * sides: 1},
    )


def middle_kernel(
    spots,
    hidden,
    feed,
    grad_normed,
    cot,
    norms,
    w_own,
    w_oth,
    att_t,
    att_c,
    denom,
    phi_q,
    aux,
    mixed,
    grad_hidden,
    d_gain,
    d_shift,
    g_ext,
    leaving,
    d_own,
    d_oth,
    branch_t,
    state,
):
    step = pl.program_id(0)
    count = pl.num_programs(0)
    heads, feat, unused = phi_q.shape
    width = feat // 2
    rows = at(step, CHUNK)
    hid = hidden[...]
    mixed[...] = (hid + feed[rows, :]).astype(LOW)
    xhat, rstd = norm_parts(hid)
    grad = grad_normed[rows, :]
    back = cot[rows, :].astype(F32) + norm_back(grad, xhat, rstd, norms[2:3, :])
    grad_hidden[...] = back

    @pl.when(step == 0)
    def _():
        d_gain[...] = jnp.zeros_like(d_gain)
        d_shift[...] = jnp.zeros_like(d_shift)
        state[...] = jnp.zeros_like(state)

    d_gain[...] += jnp.sum(grad * xhat, axis=0, keepdims=True)
    d_shift[...] += jnp.sum(grad, axis=0, keepdims=True)
    low = back.astype(LOW)
    branch_t[:, rows] = low.T
    reach = aux[2:3, rows].astype(LOW)
    first = lax.broadcasted_iota(jnp.int32, (16, CHUNK), 0) == 0
    grad_att = [nn(low, flat(weights[...])) for weights in (w_own, w_oth)]
    turned = [
        piece[:, inner * feat : (inner + 1) * feat].T
        for piece in grad_att
        for inner in range(piece.shape[1] // feat)
    ]
    exts = []
    for head in range(heads):
        ga = turned[head // 2][head % 2 * width : (head % 2 + 1) * width]
        inverse = 1.0 / denom[head : head + 1, rows]
        centered = att_c[head * width : (head + 1) * width, :].astype(F32)
        gd = -jnp.sum(ga * centered, axis=0, keepdims=True) * inverse
        exts.append(
            jnp.concatenate([(ga * inverse).astype(LOW), jnp.where(first, gd, 0.0).astype(LOW)], axis=0)
        )
    more = [nt(ext * reach, phi_q[head, :, rows]) for head, ext in enumerate(exts)]
    for head in range(heads):
        g_ext[head, :, rows] = exts[head]
        state[head] += more[head]
    leaving[...] = state[...].astype(LOW)

    @pl.when(step == count - 1)
    def _():
        start = 0
        for out in (d_own, d_oth):
            size = out.shape[1]
            out[...] = nt(branch_t[...], att_t[start : start + size, :]).astype(LOW)
            start += size


def middle(spots, hidden, feed, grad_normed, cot, norms, early, units, att_t, att_c, denom, phi_q, aux):
    rows, dim = hidden.shape
    heads, feat, unused = phi_q.shape
    width = feat // 2
    part = heads * width // 2
    block = pl.BlockSpec((CHUNK, dim), lambda c, *_: (c, 0))
    weights = [gathered(early, part, 2 * units // part, side) for side in (0, 1)]
    return call(
        middle_kernel,
        "middle",
        (rows // CHUNK,),
        [block]
        + [STAYS] * 3
        + [whole(norms)]
        + weights
        + [STAYS, pl.BlockSpec((heads * width, CHUNK), lambda c, *_: (0, c)), STAYS, STAYS]
        + [whole(aux)],
        [block, block, fixed(1, dim), fixed(1, dim), STAYS, fixed(heads, EXT, feat)]
        + [fixed(dim, part)] * 2,
        (
            streamed((rows, dim), LOW),
            streamed((rows, dim), F32),
            jax.ShapeDtypeStruct((1, dim), F32),
            jax.ShapeDtypeStruct((1, dim), F32),
            kept_in_vmem((heads, EXT, rows), LOW),
            streamed((heads, EXT, feat), LOW),
        )
        + (jax.ShapeDtypeStruct((dim, part), LOW),) * 2,
        [pltpu.VMEM((dim, rows), LOW), pltpu.VMEM((heads, EXT, feat), F32)],
        20,
        13,
        (
            spots,
            *apart(hidden),
            *pinned(feed, grad_normed, cot),
            norms,
            *apart(early, early),
            *pinned(att_t),
            *apart(att_c),
            *pinned(denom, phi_q),
            aux,
        ),
        scalars=1,
    )


def attend_back_kernel(
    side,
    carry,
    kept,
    aux,
    mask,
    phi_q,
    phi_k,
    phi_k_nat,
    v_nat,
    v_ext,
    g_ext,
    prefix,
    final,
    entering,
    arriving,
    q_t,
    k_t,
    maps,
    grads,
    d_maps,
    state,
    d_fq,
    d_fk,
):
    step = pl.program_id(0)
    count = pl.num_programs(0)
    heads, feat, unused = phi_q.shape
    width = feat // 2
    part = heads * width // 2
    half = heads // 2
    chunk = count - 1 - step
    rows = at(chunk, CHUNK)
    keep_in = carry[chunk]
    keep = kept[chunk]
    reach = aux[0:1, rows].astype(LOW)
    written = aux[1:2, rows].astype(LOW)
    mask_now = mask[0]

    @pl.when(step == 0)
    def _():
        for head in range(half):
            state[head] = arriving[(1 - side) * half + head].astype(F32)
        d_fq[...] = jnp.zeros_like(d_fq)
        d_fk[...] = jnp.zeros_like(d_fk)

    locals_ = range(half)
    pairs = range(half // 2)
    centers = [center_of(final, entering, side * half // 2 + p, 2 * phi_q.shape[2]) for p in pairs]
    v_pairs = [
        (v_nat[:, p * feat : (p + 1) * feat].astype(F32) - centers[p][:1]).astype(LOW) for p in pairs
    ]
    columns = [center.T for center in centers]
    nears = [columns[n // 2][n % 2 * width : (n % 2 + 1) * width, :] for n in locals_]
    pqs = [phi_q[side * half + n, :, rows] for n in locals_]
    pks = [phi_k[n] for n in locals_]
    exts = [g_ext[side * half + n, :, rows] for n in locals_]
    scores = [
        nn(phi_k_nat[rows, (side * half + n) * feat : (side * half + n + 1) * feat], pqs[n]) for n in locals_
    ]
    blank = jnp.zeros((width, CHUNK), LOW)
    gws = []
    for n in locals_:
        numer = exts[n][:width]
        padded = jnp.concatenate([numer, blank] if n % 2 == 0 else [blank, numer], axis=0)
        gws.append(nn(v_pairs[n // 2], padded))
    weights = [score.astype(LOW) * mask_now for score in scores]
    gws = [
        (gw + ext[width : width + 1].astype(F32)).astype(LOW) * mask_now for gw, ext in zip(gws, exts)
    ]
    befores, values, afters, reached = [], [], [], []
    for n in locals_:
        before = prefix[0, n] + keep_in * entering[(1 - side) * half + n]
        befores.append(
            jnp.concatenate([before[:width] - nears[n] * before[width : width + 1], before[width:]], axis=0).astype(LOW)
        )
        value = v_ext[side * half + n, :, rows]
        near = jnp.concatenate([nears[n]] * (CHUNK // feat), axis=1)
        value = jnp.concatenate([(value[:width].astype(F32) - near).astype(LOW), value[width:]], axis=0)
        values.append(value * written)
        afters.append(state[n].astype(LOW))
        reached.append(exts[n] * reach)
    g_phi_q = [nn(pks[n], gws[n]) + tn(befores[n], reached[n]) for n in locals_]
    g_phi_k = [nt(pqs[n], gws[n]) + tn(afters[n], values[n]) for n in locals_]
    g_values = [
        nt(exts[n][:width], weights[n]) + nn(afters[n][:width], pks[n] * written) for n in locals_
    ]
    more = [nt(reached[n], pqs[n]) for n in locals_]
    grads_q = [softmax_pair_back(pqs[n], g_phi_q[n]).astype(LOW) for n in locals_]
    grads_k = [softmax_pair_back(pks[n], g_phi_k[n]).astype(LOW) for n in locals_]
    for n in locals_:
        state[n] = keep * state[n] + more[n]
    both = [[jnp.concatenate(g[2 * p : 2 * p + 2], axis=0) for p in pairs] for g in (grads_q, grads_k)]
    through = [[nn(maps[2 * kind, side * half // 2 + p], both[kind][p]) for p in pairs] for kind in range(2)]
    onto = [
        [nt(source[p * feat : (p + 1) * feat, :], both[kind][p]) for p in pairs]
        for kind, source in enumerate((q_t, k_t))
    ]
    for p in pairs:
        for kind in range(2):
            start = kind * part + p * feat
            grads[start : start + feat, rows] = through[kind][p].astype(LOW)
        start = 2 * part + p * feat
        grads[start : start + feat, rows] = jnp.concatenate(g_values[2 * p : 2 * p + 2], axis=0).astype(LOW)
        d_fq[p] += onto[0][p]
        d_fk[p] += onto[1][p]

    @pl.when(step == count - 1)
    def _():
        first = lax.broadcasted_iota(jnp.int32, (width, feat), 1) < width
        for kind, source in enumerate((d_fq, d_fk)):
            for local in range(half // 2):
                block = source[local]
                d_maps[kind, local] = jnp.where(first, block[:width], block[width:])


def attend_back(
    side, aux, mask, phi_q, phi_k, phi_k_nat, v_nat, v_ext, g_ext, prefix, final, entering, arriving, q_t, k_t, maps, carry, kept
):
    heads, feat, rows = phi_q.shape
    width = feat // 2
    half = heads // 2
    count = rows // CHUNK
    lanes = pl.BlockSpec((half * width, CHUNK), lambda c, *_: (side, count - 1 - c))
    return call(
        functools.partial(attend_back_kernel, side),
        "attend_back",
        (rows // CHUNK,),
        [
            whole(aux),
            pl.BlockSpec((1, CHUNK, CHUNK), lambda c, *_: (count - 1 - c, 0, 0)),
            STAYS,
            pl.BlockSpec((half, feat, CHUNK), lambda c, *_: (side, 0, count - 1 - c)),
            STAYS,
            pl.BlockSpec((CHUNK, half * width), lambda c, *_: (count - 1 - c, side)),
            STAYS,
            STAYS,
            pl.BlockSpec((1, half, EXT, feat), lambda c, *_: (count - 1 - c, side, 0, 0)),
            whole(final),
            whole(entering),
            whole(arriving),
            lanes,
            lanes,
            STAYS,
        ],
        [STAYS, fixed(2, half // 2, width, feat)],
        (kept_in_vmem((3 * half * width, rows), LOW), streamed((2, half // 2, width, feat), F32)),
        [pltpu.VMEM((half, EXT, feat), F32)] + [pltpu.VMEM((half // 2, feat, feat), F32)] * 2,
        10,
        14,
        (
            carry,
            kept,
            aux,
            *apart(mask),
            *pinned(phi_q),
            *apart(phi_k),
            *pinned(phi_k_nat),
            *apart(v_nat),
            *pinned(v_ext, g_ext),
            *apart(prefix, final, entering, arriving, q_t, k_t),
            *pinned(maps),
        ),
        scalars=2,
    )


def weight_kernel(normed_t, grads, out):
    out[...] = nt(normed_t[...], grads[...]).astype(LOW)


def weight_grads(normed_t, grads):
    dim, rows = normed_t.shape
    size = grads.shape[0]
    return call(
        weight_kernel,
        "weight_grads",
        (1,),
        [whole(normed_t), STAYS],
        fixed(dim, size),
        jax.ShapeDtypeStruct((dim, size), LOW),
        [],
        8,
        0,
        (*apart(normed_t), *pinned(grads)),
    )


def first_kernel(tokens, norms, grad_hidden, wa_own, wb_own, wa_oth, wb_oth, grads_own, grads_oth, out, d_gain, d_shift):
    step = pl.program_id(0)
    rows = at(step, CHUNK)
    total = None
    for wa, wb, grads in ((wa_own, wb_own, grads_own), (wa_oth, wb_oth, grads_oth)):
        cut = wa.shape[1]
        term = nn(wa[...], grads[:cut, rows]) + nn(wb[...], grads[cut:, rows])
        total = term if total is None else total + term
    grad = total.T
    xhat, rstd = norm_parts(tokens[...].astype(F32))
    out[...] = (grad_hidden[...] + norm_back(grad, xhat, rstd, norms[0:1, :])).astype(LOW)

    @pl.when(step == 0)
    def _():
        d_gain[...] = jnp.zeros_like(d_gain)
        d_shift[...] = jnp.zeros_like(d_shift)

    d_gain[...] += jnp.sum(grad * xhat, axis=0, keepdims=True)
    d_shift[...] += jnp.sum(grad, axis=0, keepdims=True)


def first_back(tokens, norms, grad_hidden, weights, grads):
    rows, dim = tokens.shape
    block = pl.BlockSpec((CHUNK, dim), lambda c: (c, 0))
    return call(
        first_kernel,
        "first_back",
        (rows // CHUNK,),
        [block, whole(norms), block] + [whole(w) for w in weights] + [STAYS] * 2,
        [block, fixed(1, dim), fixed(1, dim)],
        (
            streamed((rows, dim), LOW),
            jax.ShapeDtypeStruct((1, dim), F32),
            jax.ShapeDtypeStruct((1, dim), F32),
        ),
        [],
        16,
        9,
        (*apart(tokens), norms, *apart(grad_hidden), *weights, *pinned(*grads)),
    )


SWAP = [(0, 1), (1, 0)]


def swap(piece):
    return lax.ppermute(piece, "mp", SWAP)


def flip(piece, bit, size):
    return lax.ppermute(piece, "dp", [(i, i ^ bit) for i in range(size)])


def turn(piece, by, size):
    return lax.ppermute(piece, "dp", [(i, (i + by) % size) for i in range(size)])


def after(value, *others):
    return lax.optimization_barrier((value, *others))[0]


class Places:
    def __init__(self, size, staged):
        self.size = size
        self.deep = size // 4
        self.staged = staged
        place = lax.axis_index("dp")
        self.spots = jnp.stack([place % 2, (place // 2) % 2, place // 4, lax.axis_index("mp")])

    def flip(self, value, axis):
        return flip(value, 1 if axis == "x" else 2, self.size)


def line_kernel(cut, spots, *refs):
    deep = len(refs) - 2
    for s in range(deep):
        spot = lax.rem(spots[2] + deep - s, deep)
        refs[-2][spot] = refs[s][:, :cut]
        refs[-1][spot] = refs[s][:, cut:]


def gather_line(shard, cut, at, *others):
    pieces = [shard] + [turn(shard, 4 * s, at.size) for s in range(1, at.deep)]
    if others:
        pieces[1] = after(pieces[1], *others)
    rows, columns = shard.shape
    shapes = [(at.deep, rows, cut), (at.deep, rows, columns - cut)]
    return call(
        functools.partial(line_kernel, cut),
        "line",
        (1,),
        [whole(p) for p in pieces],
        [fixed(*shape) for shape in shapes],
        tuple(jax.ShapeDtypeStruct(shape, LOW) for shape in shapes),
        [],
        6,
        0,
        (at.spots, *pieces),
        scalars=1,
    )


def pair_kernel(axes, dims, spots, *refs):
    for index, (axis, dim) in enumerate(zip(axes, dims)):
        mine, theirs, out = refs[2 * index], refs[2 * index + 1], refs[4 + index]
        bit = spots[0 if axis == "x" else 1]
        for source, place in ((mine, bit), (theirs, 1 - bit)):
            if dim == 1:
                out[:, pl.ds(place, 1)] = source[...][:, None]
            else:
                out[:, :, pl.ds(place, 1)] = source[...][:, :, None]


def first_by(shape):
    tail = (0,) * (len(shape) - 1)
    return pl.BlockSpec((1, *shape[1:]), lambda d, *_: (jnp.minimum(d, shape[0] - 1), *tail))


def gather_pair(values, axes, at, *others, kind=jax.ShapeDtypeStruct):
    moved = [at.flip(v, axis) for v, axis in zip(values, axes)]
    if others:
        moved[0] = after(moved[0], *others)
    dims = [v.ndim - 2 if axis == "x" else 1 for v, axis in zip(values, axes)]
    shapes = [(*v.shape[:d], 2, *v.shape[d:]) for v, d in zip(values, dims)]
    return call(
        functools.partial(pair_kernel, axes, dims),
        "pair",
        (at.deep,),
        [first_by(v.shape) for v in values for unused in (0, 1)],
        [first_by(shape) for shape in shapes],
        tuple(kind(shape, LOW) for shape in shapes),
        [],
        8,
        0,
        (at.spots, values[0], moved[0], values[1], moved[1]),
        scalars=1,
    )


def first_fold_kernel(axes, cuts, deep, spots, *refs):
    outs = refs[-4:]
    step = pl.program_id(0)
    if len(refs) == 5 + 2 * len(cuts):
        rider = refs[-5]
        rows = outs[0].shape[2]

        @pl.when(step == deep)
        def _():
            for index in range(rider.shape[0] // rows):
                group, place = divmod(index, 2)
                outs[0][0, place, :, group * 128 : (group + 1) * 128] = rider[index * rows : (index + 1) * rows, :]

        @pl.when(step < deep)
        def _():
            first_fold_step(axes, cuts, spots, refs, outs)

    else:
        first_fold_step(axes, cuts, spots, refs, outs)


def first_fold_step(axes, cuts, spots, refs, outs):
    for index, axis in enumerate(axes):
        bit = spots[0 if axis == "x" else 1]
        sent, kept = outs[2 * index : 2 * index + 2]
        start = 0
        for segment, cut in enumerate(cuts):
            pair = refs[2 * segment : 2 * segment + 2]
            columns = slice(0, cut) if index == 0 else slice(cut, pair[0].shape[-1])
            size = columns.stop - columns.start
            for out, place in ((sent, 1 - bit), (kept, bit)):
                if axis == "x":
                    terms = [r[:, :, pl.ds(place, 1), :, columns].astype(F32) for r in pair]
                else:
                    terms = [r[:, pl.ds(place, 1), :, :, columns].astype(F32) for r in pair]
                total = (terms[0] + terms[1]).astype(LOW)
                out[..., start : start + size] = total.reshape(*out.shape[:-1], size)
            start += size


def fold_kernel(axes, spots, *refs):
    for index, axis in enumerate(axes):
        bit = spots[0 if axis == "x" else 1]
        sent, kept = refs[4 + 2 * index : 6 + 2 * index]
        for out, place in ((sent, 1 - bit), (kept, bit)):
            terms = [r[:, pl.ds(place, 1)].astype(F32) for r in refs[2 * index : 2 * index + 2]]
            out[...] = (terms[0] + terms[1]).astype(LOW).reshape(out.shape)


def spread_kernel(spots, a_kept, a_sent, b_kept, b_sent, *outs):
    deep = len(outs)
    cut = a_kept.shape[-1]
    for s, out in enumerate(outs):
        spot = lax.rem(spots[2] + s, deep)
        out[:, :cut] = (a_kept[spot].astype(F32) + a_sent[spot].astype(F32)).astype(LOW)
        out[:, cut:] = (b_kept[spot].astype(F32) + b_sent[spot].astype(F32)).astype(LOW)


class Scatter:
    def __init__(self, segments, at):
        self.at = at
        self.cuts = [cut for own, oth, cut in segments]
        self.cut = sum(self.cuts)
        self.terms = [[own, swap(oth)] for own, oth, cut in segments]
        if at.staged:
            split = lambda v: v.reshape(at.deep, 2, 2, v.shape[0] // at.size, v.shape[1])
            self.terms = [[split(v) for v in pair] for pair in self.terms]

    def wait_for(self, *others):
        self.terms[0][1] = after(self.terms[0][1], *others)

    def fold(self, axes, rider=None):
        at = self.at
        flats = [v for pair in self.terms for v in pair]
        if not at.staged:
            return flats[0]
        if self.cuts:
            columns = sum(pair[0].shape[-1] for pair in self.terms)
            head = flats[0].shape[:2]
            rows = flats[0].shape[3]
            lefts = [(*head, rows, self.cut), (*head, rows, columns - self.cut)]
            kernel = functools.partial(first_fold_kernel, axes, tuple(self.cuts), at.deep)
        else:
            lefts = [(v.shape[0], *v.shape[2:]) for v in flats[::2]]
            kernel = functools.partial(fold_kernel, axes)
        outs = [left for left in lefts for unused in (0, 1)]
        extra = []
        steps = at.deep
        if rider is not None:
            extra = [rider]
            steps += 1
            outs[0] = (steps, *outs[0][1:])
        a_sent, a_kept, b_sent, b_kept = call(
            kernel,
            "fold",
            (steps,),
            [first_by(v.shape) for v in flats] + [whole(v) for v in extra],
            [first_by(left) for left in outs],
            tuple(jax.ShapeDtypeStruct(left, LOW) for left in outs),
            [],
            12,
            0,
            (at.spots, *flats, *extra),
            scalars=1,
        )
        self.cuts = []
        self.terms = [[a_kept, at.flip(a_sent, axes[0])], [b_kept, at.flip(b_sent, axes[1])]]
        return a_kept

    def spread(self):
        at = self.at
        if not at.staged:
            return self.terms[0][0]
        a, b = self.terms
        shape = (a[0].shape[1], self.cut + b[0].shape[-1])
        own, *sends = call(
            spread_kernel,
            "spread",
            (1,),
            [whole(v) for v in (*a, *b)],
            [fixed(*shape)] * at.deep,
            (jax.ShapeDtypeStruct(shape, LOW),) * at.deep,
            [],
            8,
            0,
            (at.spots, *a, *b),
            scalars=1,
        )
        self.parts = [own] + [turn(p, 4 * s, at.size) for s, p in enumerate(sends, 1)]
        return own

    def end(self, *others):
        if not self.at.staged:
            sums = [own.astype(F32) + moved.astype(F32) for own, moved in self.terms]
            total = [t[:, :cut] for t, cut in zip(sums, self.cuts)] + [t[:, cut:] for t, cut in zip(sums, self.cuts)]
            total = lax.psum_scatter(jnp.concatenate(total, axis=1), "dp", scatter_dimension=0, tiled=True)
        else:
            if others:
                self.parts[1] = after(self.parts[1], *others)
            total = sum(p.astype(F32) for p in self.parts)
        return total


def ride_kernel(deep, spots, *refs):
    a_kept, a_moved, b_kept, b_moved, gain1, shift1, gain2, shift2, maps, early = refs[:10]
    late = refs[10 : 10 + deep]
    a_sent, a_left, b_sent, b_left, norm_low, maps_low, g_fc, g_down, g_out = refs[10 + deep :]
    rows = a_left.shape[1]
    units = early.shape[1] // 2
    total = late[0][...].astype(F32)
    for part in late[1:]:
        total = total + part[...].astype(F32)
    rest = total.shape[1] - 2 * units
    cut = units + (rest // 128 + 1) // 2 * 128
    g_fc[:, :units] = early[:, :units]
    g_down[:, :units] = early[:, units:]
    g_fc[:, units:] = total[:, :units]
    g_down[:, units:] = total[:, cut : cut + units]
    g_out[:, : cut - units] = total[:, units:cut]
    g_out[:, cut - units :] = total[:, cut + units :]
    blank = jnp.zeros((4, gain1.shape[1]), F32)
    norm_now = jnp.concatenate([gain1[...], shift1[...], gain2[...], shift2[...], blank], axis=0)
    norm_low[...] = jnp.concatenate([norm_now, jnp.zeros_like(norm_now)], axis=0).astype(LOW)
    for index in range(maps.shape[0] // rows):
        group, place = divmod(index, 2)
        moved = a_moved[deep, place, :, group * 128 : (group + 1) * 128].astype(F32)
        here = slice(index * rows, (index + 1) * rows)
        maps_low[here, :] = (maps[here, :].astype(F32) + moved).astype(LOW)
    for kept, moved, sent, left, bit in (
        (a_kept, a_moved, a_sent, a_left, spots[1]),
        (b_kept, b_moved, b_sent, b_left, spots[0]),
    ):
        columns = left.shape[2]
        for out, place in ((sent, 1 - bit), (left, bit)):
            terms = [r[:deep, pl.ds(place, 1)].astype(F32) for r in (kept, moved)]
            total = (terms[0] + terms[1]).astype(LOW)
            if out is left:
                out[...] = total.reshape(deep, rows, columns)
            else:
                out[: deep * rows] = total.reshape(deep * rows, columns)
        rest = norm_now[:, columns:]
        rest = jnp.concatenate([rest, jnp.zeros((8, columns - rest.shape[1]), F32)], axis=1)
        sent[deep * rows :] = jnp.concatenate([norm_now[:, :columns], rest], axis=0).astype(LOW)


def last_spread_kernel(spots, a_kept, a_moved, b_kept, b_moved, norm, norm_far, maps, maps_moved, *outs):
    *parts, maps_low = outs
    deep, rows, cut = a_kept.shape
    dim = norm.shape[1]
    maps_low[...] = (maps[...].astype(F32) + maps_moved[...].astype(F32)).astype(LOW)
    near = []
    for moved in (b_moved, a_moved):
        columns = moved.shape[1]
        tail = moved[deep * rows :].astype(F32)
        near.append(jnp.concatenate([tail[:8], tail[8:, : dim - columns]], axis=1))
    plane = (norm[...].astype(F32)[:8] + near[0]) + (near[1] + norm_far[...].astype(F32)[:8])
    tail = jnp.concatenate([plane[:, i : i + 128] for i in range(0, dim, 128)], axis=0)
    for s, out in enumerate(parts):
        spot = lax.rem(spots[2] + s, deep)
        place = pl.ds(pl.multiple_of(spot * rows, rows), rows)
        rest = out.shape[1] - 128
        out[:, :cut] = (a_kept[spot].astype(F32) + a_moved[place].astype(F32)).astype(LOW)
        out[:, cut:rest] = (b_kept[spot].astype(F32) + b_moved[place].astype(F32)).astype(LOW)
        out[:, rest:] = tail.astype(LOW)


def finish_kernel(spots, *refs):
    deep = len(refs) - 9
    parts = refs[:deep]
    maps, maps_moved, g_query, g_key, g_value, norms, map_q, map_k, held = refs[deep:]
    rows, part = g_query.shape
    total = None
    for s, ref in enumerate(parts):
        value = ref[...].astype(F32)
        held[lax.rem(spots[2] + deep - s, deep)] = value[:, 3 * part :]
        total = value if total is None else total + value
    for index, out in enumerate((g_query, g_key, g_value)):
        out[...] = total[:, index * part : (index + 1) * part]
    together = held[0]
    for spot in range(1, deep):
        together = together + held[spot]
    for index in range(rows // 8):
        norms[:, index * 128 : (index + 1) * 128] = together[index * 8 : (index + 1) * 8]
    width = map_q.shape[1]
    both = maps[...].astype(F32) + maps_moved[...].astype(F32)
    heads = map_q.shape[0]
    for kind, out in enumerate((map_q, map_k)):
        for pair in range(heads // 2):
            start = (kind * heads // 2 + pair) * width
            block = both[start : start + width]
            out[2 * pair] = block[:, :width]
            out[2 * pair + 1] = block[:, width:]


def finish_last(sums, norm, map_grads, early, late, part, heads, width, at):
    small = lambda shape, kind: jax.ShapeDtypeStruct(shape, kind)
    (a_kept, a_moved), (b_kept, b_moved) = sums.terms
    deep, unused, rows, cut = a_kept.shape
    rest = b_kept.shape[3]
    dim = norm[0].shape[1]
    units = early.shape[1]
    ins = (a_kept, a_moved, b_kept, b_moved, *norm, map_grads, early, *late)
    outs = (
        small((deep * rows + 16, cut), LOW),
        small((deep, rows, cut), LOW),
        small((deep * rows + 16, rest), LOW),
        small((deep, rows, rest), LOW),
        small((16, dim), LOW),
        small(map_grads.shape, LOW),
        small((rows, units), F32),
        small((rows, units), F32),
        small((rows, part), F32),
    )

    def run(kernel, name, ins, outs, scratch):
        return call(
            kernel,
            name,
            (1,),
            [whole(v) for v in ins],
            [fixed(*out.shape) for out in outs],
            outs,
            scratch,
            12,
            0,
            (at.spots, *ins),
            scalars=1,
        )

    kernel = functools.partial(ride_kernel, deep)
    a_sent, a_kept, b_sent, b_kept, norm_low, maps, *done = run(kernel, "ride", ins, outs, [])
    across = [(i, i ^ 3) for i in range(at.size)]
    ins = (
        a_kept,
        at.flip(a_sent, "y"),
        b_kept,
        at.flip(b_sent, "x"),
        norm_low,
        lax.ppermute(norm_low, "dp", across),
        maps,
        flip(maps, 4 << (at.size.bit_length() - 4), at.size),
    )
    ins = lax.optimization_barrier(ins)
    outs = (small((rows, cut + rest + 128), LOW),) * deep + (small(map_grads.shape, LOW),)
    own, *sends, maps = run(last_spread_kernel, "last_spread", ins, outs, [])
    ins = (own, *(turn(p, 4 * s, at.size) for s, p in enumerate(sends, 1)), maps, at.flip(maps, "y"))
    ins = lax.optimization_barrier(ins)
    outs = (
        (small((rows, part), F32),) * 3
        + (small((8, dim), F32),)
        + (small((heads // 2, width, width), F32),) * 2
    )
    return done, run(finish_kernel, "finish", ins, outs, [pltpu.VMEM((deep, rows, 128), F32)])


def add_along(value, steps, size):
    for step in steps:
        if step < size:
            value = value.astype(LOW)
            value = value.astype(F32) + flip(value, step, size).astype(F32)
    return value


def per_device(
    size,
    tokens,
    norm1_gain,
    norm1_shift,
    w_query,
    w_key,
    w_value,
    w_out,
    fmap_query,
    fmap_key,
    norm2_gain,
    norm2_shift,
    w_fc,
    w_down,
    lengths,
    cotangent,
):
    rows, dim = tokens.shape
    heads = 2 * fmap_query.shape[0]
    width = fmap_query.shape[1]
    feat = 2 * width
    part = w_query.shape[1]
    count = rows // CHUNK
    core = lax.axis_index("mp")
    staged = size % 4 == 0 and dim // size % 16 == 0
    where = Places(size, staged)
    units = w_fc.shape[1] // 2
    cut = (3 * part // feat + 1) // 2 * feat
    cut_out = (part // feat + 1) // 2 * feat
    shard_qkv, shard_early, shard_late = pack(
        (w_query, w_key, w_value, w_out, w_fc, w_down),
        (
            ((0, 0, part), (1, 0, part), (2, 0, part)),
            ((4, 0, units), (5, 0, units), (3, 0, part)),
            ((4, units, units), (5, units, units)),
        ),
    )
    early = lax.all_gather(shard_early, ("dp", "mp"), axis=0)
    early = early.reshape(size, 2, *shard_early.shape)
    if shard_early.shape[0] % 16:
        early = early.swapaxes(0, 1).reshape(1, 2, dim, -1)
    fq_oth, fk_oth = swap(fmap_query), swap(fmap_key)
    if staged:
        qkv = gather_line(shard_qkv, cut, where)
        lengths = after(lengths, qkv[0])

    ends = jnp.cumsum(lengths[0])
    places = core * rows - 1 + jnp.arange(rows + 1, dtype=jnp.int32)
    numbers = jnp.sum((ends[None, :] <= places[:, None]).astype(jnp.int32), axis=1)
    numbers = jnp.where(places < 0, -1, numbers)
    segment = numbers[1:]
    living = places[1:] < ends[-1]
    blocks = segment.reshape(count, CHUNK)
    last = blocks[:, -1]
    before = jnp.concatenate([numbers[:1], last[:-1]])
    kept = (last == before).astype(F32)
    carry = ((before == numbers[0]) & (core > 0)).astype(F32)
    reach = (blocks == before[:, None]).reshape(rows) & living
    written = (blocks == last[:, None]).reshape(rows)
    reach_in = (segment == numbers[0]) & living
    aux = jnp.stack([reach, written, reach_in, ~living] + [jnp.zeros_like(living)] * 4).astype(F32)
    order = jnp.arange(CHUNK, dtype=jnp.int32)
    mask = (
        (blocks[:, :, None] == blocks[:, None, :])
        & (order[:, None] <= order[None, :])
        & living.reshape(count, 1, CHUNK)
    ).astype(LOW)

    norms = jnp.stack([norm1_gain, norm1_shift, norm2_gain, norm2_shift])

    shard_late, norms, aux, mask, kept, carry = lax.optimization_barrier(
        (shard_late, norms, aux, mask, kept, carry)
    )
    spots = where.spots
    if staged:
        qkv = gather_pair(qkv, "xy", where)
        shard_late, tokens = after(shard_late, qkv[0]), after(tokens, qkv[0], mask)
    normed1, normed1_t, cot, cot_t, maps = prepare(
        tokens, cotangent, norms, fmap_query, fq_oth, fmap_key, fk_oth
    )
    if staged:
        qkv = tuple(map(flat, gather_pair(qkv, "yx", where, maps)))
    else:
        qkv, late = (
            tuple(lax.all_gather(s, "dp", axis=0, tiled=True) for s in shards)
            for shards in (
                (shard_qkv[:, :cut], shard_qkv[:, cut:]),
                (shard_late[:, :units], shard_late[:, units:]),
            )
        )
    qkv = (*qkv, *map(swap, qkv))
    q_t, k_t, v_nat, v_ext, phi_q, phi_k, phi_k_nat, prefix, final = project(
        normed1, *qkv, maps, aux, kept, heads, width
    )
    if staged:
        late = gather_line(shard_late, units, where, final)
        final = after(final, late[0])
    entering = swap(final)
    att_t, att_c, denom = attend(aux, mask, phi_q, phi_k_nat, v_ext, prefix, final, entering, carry)
    if staged:
        late = gather_pair(late, "xy", where, denom)
        att_t = after(att_t, late[0])
    hidden, normed2, normed2_t = mix(spots, tokens, norms, early, units, att_t)
    feed_part = functools.partial(feed_forward, spots, normed2, normed2_t, cot, cot_t)
    early_specs = [[gathered(early, units, index, side) for index in (0, 1)] for side in (0, 1)]
    feed, grad_normed, *d_early_oth = feed_part(apart(early, early), early_specs[1], units, None)
    if staged:
        late = tuple(map(flat, gather_pair(late, "yx", where, d_early_oth[0], kind=streamed)))
        feed = after(feed, late[0])
    feed, grad_normed, *d_early_own = feed_part(
        apart(early, early), early_specs[0], units, (feed, grad_normed)
    )
    sums_early = Scatter([(*d_early_own, *d_early_oth, units)], where)
    late_oth = tuple(map(swap, late))
    feed = after(feed, sums_early.fold("xy"))
    feed, grad_normed, d_late_own, d_late_oth = feed_part(
        (*late, *late_oth), [whole(w) for w in late] * 2, units, (feed, grad_normed)
    )
    sums_early.wait_for(d_late_oth)
    hidden = after(hidden, sums_early.fold("yx"))
    mixed, grad_hidden, d_gain2, d_shift2, g_ext, leaving, d_out_own, d_out_oth = middle(
        spots, hidden, feed, grad_normed, cot, norms, early, units, att_t, att_c, denom, phi_q, aux
    )
    sums_early.wait_for(d_gain2)
    started = sums_early.spread()
    arriving = lax.ppermute(after(leaving, started), "mp", [(1, 0)])
    d_out_oth = after(d_out_oth, started)
    sums_late = Scatter([(d_late_own, d_late_oth, units), (d_out_own, d_out_oth, cut_out)], where)
    sums_late.wait_for(started)
    arriving = after(arriving, sums_late.fold("xy"))
    back = functools.partial(
        attend_back, carry=carry, kept=kept, prefix=prefix, final=final, entering=entering, q_t=q_t, k_t=k_t, maps=maps
    )
    back_inputs = (aux, mask, phi_q, phi_k, phi_k_nat, v_nat, v_ext, g_ext)
    lanes = lambda v: v.reshape(-1, feat)
    grads_oth, maps_oth = back(1, *back_inputs, arriving=arriving)
    total_early = sums_early.end(maps_oth)
    d_qkv_oth = weight_grads(normed1_t, after(grads_oth, total_early))
    sums_late.wait_for(d_qkv_oth)
    arriving = after(arriving, sums_late.fold("yx"))
    grads_own, maps_own = back(0, *back_inputs, arriving=arriving)
    sums_late.wait_for(maps_own)
    grads_own = after(grads_own, sums_late.spread())
    map_grads = lanes(maps_own + swap(maps_oth))
    d_qkv_own = weight_grads(normed1_t, grads_own)
    if staged:
        map_grads = map_grads.astype(LOW)
        for step in [4 << i for i in range(size.bit_length() - 4)]:
            moved = after(flip(map_grads, step, size), d_qkv_own)
            map_grads = (map_grads.astype(F32) + moved.astype(F32)).astype(LOW)
    sums_qkv = Scatter([(d_qkv_own, d_qkv_oth, cut)], where)
    grad_hidden = after(grad_hidden, sums_qkv.fold("xy", map_grads if staged else None))
    grad_tokens, d_gain1, d_shift1 = first_back(tokens, norms, grad_hidden, qkv, (grads_own, grads_oth))
    norm_grads = (d_gain1, d_shift1, d_gain2, d_shift2)
    if staged:
        sums_qkv.wait_for(d_gain1)
        done, (g_query, g_key, g_value, norm_grads, map_q, map_k) = finish_last(
            sums_qkv, norm_grads, map_grads, total_early, sums_late.parts, part, heads, width, where
        )
        g_fc, g_down, g_out = done
    else:
        total_late = sums_late.end()
        grad_qkv = sums_qkv.end()
        g_query, g_key, g_value = (grad_qkv[:, i * part : (i + 1) * part] for i in range(3))
        norm_grads, map_grads = lax.psum((jnp.concatenate(norm_grads, axis=0), map_grads), "dp")
        map_grads = map_grads.reshape(2, heads // 4, width, 2, width)
        map_q, map_k = map_grads.swapaxes(2, 3).reshape(2, heads // 2, width, width)
        cut_late = units + cut_out
        g_fc = jnp.concatenate([total_early[:, :units], total_late[:, :units]], axis=1)
        g_down = jnp.concatenate([total_early[:, units:], total_late[:, cut_late : cut_late + units]], axis=1)
        g_out = jnp.concatenate([total_late[:, units:cut_late], total_late[:, cut_late + units :]], axis=1)
    norm_grads = norm_grads + swap(norm_grads)
    return (
        mixed,
        grad_tokens,
        norm_grads[0],
        norm_grads[1],
        g_query,
        g_key,
        g_value,
        g_out,
        map_q,
        map_k,
        norm_grads[2],
        norm_grads[3],
        g_fc,
        g_down,
    )


def solution(mesh):
    placed = (
        P(("dp", "mp"), None),
        P(),
        P(),
        P("dp", "mp"),
        P("dp", "mp"),
        P("dp", "mp"),
        P("dp", "mp"),
        P("mp", None, None),
        P("mp", None, None),
        P(),
        P(),
        P("dp", "mp"),
        P("dp", "mp"),
        P("dp", None),
        P(("dp", "mp"), None),
    )
    return jax.shard_map(
        functools.partial(per_device, mesh.shape["dp"]),
        mesh=mesh,
        in_specs=placed,
        out_specs=(
            P(("dp", "mp"), None),
            P(("dp", "mp"), None),
            P(),
            P(),
            P("dp", "mp"),
            P("dp", "mp"),
            P("dp", "mp"),
            P("dp", "mp"),
            P("mp", None, None),
            P("mp", None, None),
            P(),
            P(),
            P("dp", "mp"),
            P("dp", "mp"),
        ),
        check_vma=False,
    )
```

```python
import functools

import jax
import jax.numpy as jnp
from jax import lax
from jax.experimental import pallas as pl
from jax.experimental.pallas import tpu as pltpu
from jax.sharding import PartitionSpec as P

EPS = 1e-05
CHUNK = 256
EXT = 80
LOW = jnp.bfloat16
F32 = jnp.float32
MIB = 1024 * 1024
PACE = 3_000_000_000
GELU_C = 0.7978845608028654
GELU_A = 0.044715


def nn(a, b):
    return lax.dot_general(a, b, (((1,), (0,)), ((), ())), preferred_element_type=F32)


def nt(a, b):
    return lax.dot_general(a, b, (((1,), (1,)), ((), ())), preferred_element_type=F32)


def tn(a, b):
    return lax.dot_general(a, b, (((0,), (0,)), ((), ())), preferred_element_type=F32)


def norm_parts(rows):
    center = rows - jnp.mean(rows, axis=-1, keepdims=True)
    spread = jnp.mean(center * center, axis=-1, keepdims=True)
    rstd = lax.rsqrt(spread + EPS)
    return center * rstd, rstd


def norm_back(grad, xhat, rstd, gain):
    e = grad * gain
    return rstd * (
        e - jnp.mean(e, axis=-1, keepdims=True) - xhat * jnp.mean(e * xhat, axis=-1, keepdims=True)
    )


def softmax_pair(logits):
    high = jnp.max(logits, axis=0, keepdims=True)
    least = jnp.min(logits, axis=0, keepdims=True)
    pos = jnp.exp(logits - high)
    neg = jnp.exp(least - logits)
    pos = pos * (1.0 / jnp.sum(pos, axis=0, keepdims=True))
    neg = neg * (1.0 / jnp.sum(neg, axis=0, keepdims=True))
    return jnp.concatenate([pos, neg], axis=0).astype(LOW)


def softmax_pair_back(phi, grad):
    width = phi.shape[0] // 2
    pos = phi[:width].astype(F32)
    neg = phi[width:].astype(F32)
    gp = grad[:width]
    gn = grad[width:]
    gp = gp - jnp.sum(pos * gp, axis=0, keepdims=True)
    gn = gn - jnp.sum(neg * gn, axis=0, keepdims=True)
    return pos * gp - neg * gn


def flat(value):
    return value.reshape(-1, value.shape[-1])


def kept_in_vmem(shape, dtype):
    return pltpu.VMEM(shape, dtype)


def streamed(shape, dtype):
    return pltpu.HBM(shape, dtype)


def apart(*arrays):
    return tuple(pltpu.with_memory_space_constraint(a, pltpu.HBM) for a in arrays)


def pinned(*arrays):
    return tuple(pltpu.with_memory_space_constraint(a, pltpu.VMEM) for a in arrays)


def whole(array):
    return pl.BlockSpec(
        array.shape, lambda *_: (0,) * array.ndim, pipeline_mode=pl.Buffered(1)
    )


def fixed(*shape):
    return pl.BlockSpec(shape, lambda *_: (0,) * len(shape))


STAYS = pl.BlockSpec(memory_space=pltpu.VMEM)


def at(step, size):
    return pl.ds(pl.multiple_of(step * size, size), size)


def call(kernel, name, grid, in_specs, out_specs, out_shape, scratch, limit, micros, args, scalars=0, alias=None):
    return pl.pallas_call(
        kernel,
        grid_spec=pltpu.PrefetchScalarGridSpec(
            num_scalar_prefetch=scalars,
            grid=grid,
            in_specs=in_specs,
            out_specs=out_specs,
            scratch_shapes=scratch,
        ),
        out_shape=out_shape,
        input_output_aliases=alias or {},
        compiler_params=pltpu.CompilerParams(vmem_limit_bytes=limit * MIB),
        cost_estimate=pl.CostEstimate(flops=micros * PACE, bytes_accessed=1024, transcendentals=0),
        name=name,
    )(*args)


def pack_kernel(groups, *refs):
    outs = refs[len(refs) - len(groups) :]
    for out, group in zip(outs, groups):
        start = 0
        for index, first, size in group:
            out[:, start : start + size] = refs[index][:, first : first + size]
            start += size


def pack(arrays, groups):
    rows = arrays[0].shape[0]
    shapes = [(rows, sum(size for unused, first, size in group)) for group in groups]
    return call(
        functools.partial(pack_kernel, groups),
        "pack",
        (1,),
        [whole(a) for a in arrays],
        [fixed(*shape) for shape in shapes],
        tuple(jax.ShapeDtypeStruct(shape, LOW) for shape in shapes),
        [],
        8,
        1,
        apart(*arrays),
    )


def prepare_kernel(
    tokens, cot, norms, fq_own, fq_oth, fk_own, fk_oth, normed, normed_t, cot_t, maps
):
    step = pl.program_id(0)
    rows = at(step, CHUNK)
    xhat, unused = norm_parts(tokens[...].astype(F32))
    low = (xhat * norms[0:1, :] + norms[1:2, :]).astype(LOW)
    normed[rows, :] = low
    normed_t[...] = low.T
    cot_t[...] = cot[...].T

    @pl.when(step == 0)
    def _():
        half, width, unused = fq_own.shape
        blank = jnp.zeros((width, width), F32)
        for kind, (own, oth) in enumerate(((fq_own, fq_oth), (fk_own, fk_oth))):
            for pair in range(half):
                source = own if pair < half // 2 else oth
                first = 2 * pair % half
                block = jnp.concatenate(
                    [
                        jnp.concatenate([source[first].astype(F32), blank], axis=1),
                        jnp.concatenate([blank, source[first + 1].astype(F32)], axis=1),
                    ],
                    axis=0,
                )
                maps[2 * kind, pair] = block.astype(LOW)
                maps[2 * kind + 1, pair] = block.T.astype(LOW)


def prepare(tokens, cot, norms, fq_own, fq_oth, fk_own, fk_oth):
    rows, dim = tokens.shape
    half, width, unused = fq_own.shape
    block = pl.BlockSpec((CHUNK, dim), lambda c: (c, 0))
    natural = kept_in_vmem((rows, dim), LOW)
    turned = streamed((dim, rows), LOW)
    column = pl.BlockSpec((dim, CHUNK), lambda c: (0, c))
    return call(
        prepare_kernel,
        "prepare",
        (rows // CHUNK,),
        [block, block] + [whole(a) for a in (norms, fq_own, fq_oth, fk_own, fk_oth)],
        [STAYS, column, column, STAYS],
        (natural, turned, turned, kept_in_vmem((4, half, 2 * width, 2 * width), LOW)),
        [],
        8,
        5,
        (*apart(tokens, cot), norms, fq_own, fq_oth, fk_own, fk_oth),
    )


def project_kernel(
    kept,
    normed,
    wa_own,
    wb_own,
    wa_oth,
    wb_oth,
    maps,
    aux,
    q_t,
    k_t,
    v_nat,
    v_ext,
    phi_q,
    phi_k,
    phi_k_nat,
    prefix,
    final,
    state,
    projected,
):
    step = pl.program_id(0)
    heads, feat, unused = phi_q.shape
    width = feat // 2
    rows = at(step, CHUNK)
    written = aux[1:2, rows].astype(LOW)
    tail = jnp.where(lax.broadcasted_iota(jnp.int32, (16, CHUNK), 0) == 0, 1.0, 0.0).astype(LOW)

    @pl.when(step == 0)
    def _():
        state[...] = jnp.zeros_like(state)
        now = normed[...]
        part = heads * width // 2
        for side, (wa, wb) in enumerate(((wa_own, wb_own), (wa_oth, wb_oth))):
            projected[side, :, : 2 * part] = nn(now, wa[...]).astype(LOW)
            projected[side, :, 2 * part :] = nn(now, wb[:, :part]).astype(LOW)

    prefix[0] = state[:heads]
    keep = kept[step]
    made = [projected[side, rows, :] for side in range(2)]
    part = made[0].shape[1] // 3
    pairs = part // feat
    for side in range(2):
        values = made[side][:, 2 * part :]
        v_nat[:, side * part : (side + 1) * part] = values
        turned = [
            [made[side][:, kind * part + p * feat : kind * part + (p + 1) * feat].T for p in range(pairs)]
            for kind in range(3)
        ]
        indices = [side * pairs + p for p in range(pairs)]
        logits = [
            [nn(maps[2 * kind + 1, index], piece) for index, piece in zip(indices, turned[kind])]
            for kind in range(2)
        ]
        for p, index in enumerate(indices):
            place = slice(index * feat, (index + 1) * feat)
            q_t[place, :] = turned[0][p]
            k_t[place, :] = turned[1][p]
            state[heads, index : index + 1, :] += jnp.sum(
                values[:, p * feat : (p + 1) * feat].astype(F32), axis=0, keepdims=True
            )
        inside = [slice(one * width, (one + 1) * width) for one in range(2)]
        feats_q = [softmax_pair(piece[lines]) for piece in logits[0] for lines in inside]
        feats_k = [softmax_pair(piece[lines]) for piece in logits[1] for lines in inside]
        extended = [jnp.concatenate([piece[lines], tail], axis=0) for piece in turned[2] for lines in inside]
        more = [nt(value, feat_k * written) for value, feat_k in zip(extended, feats_k)]
        for local in range(2 * pairs):
            head = 2 * side * pairs + local
            phi_q[head, :, rows] = feats_q[local]
            phi_k[head] = feats_k[local]
            phi_k_nat[rows, head * feat : (head + 1) * feat] = feats_k[local].T
            v_ext[head, :, rows] = extended[local]
            state[head] = keep * state[head] + more[local]
    final[...] = state[...]


def project(normed, wa_own, wb_own, wa_oth, wb_oth, maps, aux, kept, heads, width):
    rows, dim = normed.shape
    count = rows // CHUNK
    feat = 2 * width
    return call(
        project_kernel,
        "project",
        (count,),
        [STAYS] + [whole(a) for a in (wa_own, wb_own, wa_oth, wb_oth)] + [STAYS, whole(aux)],
        [
            pl.BlockSpec((heads * width, CHUNK), lambda c, *_: (0, c)),
            pl.BlockSpec((heads * width, CHUNK), lambda c, *_: (0, c)),
            pl.BlockSpec((CHUNK, heads * width), lambda c, *_: (c, 0)),
            STAYS,
            STAYS,
            pl.BlockSpec((heads, feat, CHUNK), lambda c, *_: (0, 0, c)),
            STAYS,
            pl.BlockSpec((1, heads, EXT, feat), lambda c, *_: (c, 0, 0, 0)),
            fixed(heads + 1, EXT, feat),
        ],
        (
            streamed((heads * width, rows), LOW),
            streamed((heads * width, rows), LOW),
            streamed((rows, heads * width), LOW),
            kept_in_vmem((heads, EXT, rows), LOW),
            kept_in_vmem((heads, feat, rows), LOW),
            streamed((heads, feat, rows), LOW),
            kept_in_vmem((rows, heads * feat), LOW),
            streamed((count, heads, EXT, feat), F32),
            streamed((heads + 1, EXT, feat), F32),
        ),
        [pltpu.VMEM((heads + 1, EXT, feat), F32), pltpu.VMEM((2, rows, 3 * heads * width // 2), LOW)],
        24,
        2,
        (kept, *pinned(normed), wa_own, wb_own, wa_oth, wb_oth, *pinned(maps), aux),
        scalars=1,
    )


def center_of(final, entering, pair, rows):
    heads, unused, feat = final.shape
    other = (pair + (heads - 1) // 4) % ((heads - 1) // 2)
    total = final[heads - 1, pair : pair + 1, :] + entering[heads - 1, other : other + 1, :]
    return jnp.broadcast_to(total * (1.0 / rows), (feat, feat))


def attend_kernel(
    carry,
    aux,
    mask,
    phi_q,
    phi_k_nat,
    v_ext,
    prefix,
    final,
    entering,
    att_t,
    att_c,
    denom,
):
    step = pl.program_id(0)
    heads, feat, unused = phi_q.shape
    width = feat // 2
    rows = at(step, CHUNK)
    reach = aux[0:1, rows]
    padding = aux[3:4, rows]
    keep = carry[step]
    mask_now = mask[0]
    half = heads // 2
    centers = [center_of(final, entering, pair, 2 * att_t.shape[1]).T for pair in range(half)]
    for side in range(2):
        group = range(side * half, (side + 1) * half)
        pqs = [phi_q[head, :, rows] for head in group]
        states = [(prefix[0, head] + keep * entering[(head + half) % heads]).astype(LOW) for head in group]
        scores = [
            nn(phi_k_nat[rows, head * feat : (head + 1) * feat], pq) for head, pq in zip(group, pqs)
        ]
        inter = [nn(state, pq) for state, pq in zip(states, pqs)]
        weights = [score.astype(LOW) * mask_now for score in scores]
        numers = [
            nn(v_ext[head, :, rows], weight) + reach * more
            for head, weight, more in zip(group, weights, inter)
        ]
        for head, numer in zip(group, numers):
            below = numer[width : width + 1] + padding
            denom[head : head + 1, rows] = below
            place = slice(head * width, (head + 1) * width)
            att = numer[:width] * (1.0 / below)
            att_t[place, rows] = att.astype(LOW)
            near = centers[head // 2][head % 2 * width : (head % 2 + 1) * width, :]
            att_c[place, :] = (att - jnp.concatenate([near] * (CHUNK // feat), axis=1)).astype(LOW)


def attend(aux, mask, phi_q, phi_k_nat, v_ext, prefix, final, entering, carry):
    heads, feat, rows = phi_q.shape
    width = feat // 2
    turned = kept_in_vmem((heads * width, rows), LOW)
    return call(
        attend_kernel,
        "attend",
        (rows // CHUNK,),
        [whole(aux), pl.BlockSpec((1, CHUNK, CHUNK), lambda c, *_: (c, 0, 0))]
        + [STAYS] * 3
        + [pl.BlockSpec((1, heads, EXT, feat), lambda c, *_: (c, 0, 0, 0))]
        + [whole(final), whole(entering)],
        [STAYS, pl.BlockSpec((heads * width, CHUNK), lambda c, *_: (0, c)), STAYS],
        (turned, streamed((heads * width, rows), LOW), kept_in_vmem((16, rows), F32)),
        [],
        8,
        2,
        (carry, aux, *apart(mask), *pinned(phi_q, phi_k_nat, v_ext), *apart(prefix, final, entering)),
        scalars=1,
    )


def mix_kernel(tokens, norms, w_own, w_oth, att_t, hidden, normed, normed_t):
    step = pl.program_id(0)
    rows = at(step, CHUNK)
    att = att_t[:, rows].T
    part = att.shape[1] // 2
    total = tokens[...].astype(F32)
    total = total + nt(att[:, :part], w_own[:, part:]) + nt(att[:, part:], w_oth[:, part:])
    hidden[...] = total
    xhat, unused = norm_parts(total)
    low = (xhat * norms[2:3, :] + norms[3:4, :]).astype(LOW)
    normed[...] = low
    normed_t[...] = low.T


def gathered(array, width, index, side):
    return pl.BlockSpec(
        (array.shape[0], 1, array.shape[2], width),
        lambda c, spots: (0, spots[3] if side == 0 else 1 - spots[3], 0, index),
        pipeline_mode=pl.Buffered(1),
    )


def mix(tokens, norms, w_own, w_oth, att_t):
    rows, dim = tokens.shape
    block = pl.BlockSpec((CHUNK, dim), lambda c: (c, 0))
    return call(
        mix_kernel,
        "mix",
        (rows // CHUNK,),
        [block, whole(norms), whole(w_own), whole(w_oth), STAYS],
        [block, block, pl.BlockSpec((dim, CHUNK), lambda c: (0, c))],
        (
            streamed((rows, dim), F32),
            streamed((rows, dim), LOW),
            streamed((dim, rows), LOW),
        ),
        [],
        12,
        1,
        (*apart(tokens), norms, w_own, w_oth, *pinned(att_t)),
    )


def feed_kernel(first, sides, spots, normed, normed_t, cot, cot_t, *refs):
    feed, grad_normed = refs[2 * sides :][:2] if first else refs[2 * sides + 2 :][:2]
    if first:
        for kept, source in zip(refs[2 * sides + 2 :][:4], (normed, normed_t, cot, cot_t)):
            kept[...] = source[...]
    for side in range(sides):
        fc = flat(refs[2 * side][...])
        down = flat(refs[2 * side + 1][...])
        d_weights = refs[len(refs) - sides + side]
        units = fc.shape[1]
        u = nn(normed[...], fc)
        square = u * u
        t = jnp.tanh(u * (GELU_C + (GELU_C * GELU_A) * square))
        half = 0.5 + 0.5 * t
        act = (u * half).astype(LOW)
        slope = half + (0.5 * u) * (1.0 - t * t) * (GELU_C + (3.0 * GELU_C * GELU_A) * square)
        d_weights[:, units:] = nn(cot_t[...], act).astype(LOW)
        grad = (nn(cot[...], down) * slope).astype(LOW)
        d_weights[:, :units] = nn(normed_t[...], grad).astype(LOW)
        if first and side == 0:
            feed[...] = nt(act, down)
            grad_normed[...] = nt(grad, fc)
        else:
            feed[...] += nt(act, down)
            grad_normed[...] += nt(grad, fc)


def feed_forward(spots, normed, normed_t, cot, cot_t, weights, specs, units, sums):
    rows, dim = normed.shape
    sides = len(weights) // 2
    total = kept_in_vmem((rows, dim), F32)
    shared = (normed, normed_t, cot, cot_t)
    copies = tuple(kept_in_vmem(v.shape, LOW) for v in shared) if sums is None else ()
    return call(
        functools.partial(feed_kernel, sums is None, sides),
        "feed",
        (1,),
        ([whole(v) for v in shared] if sums is None else [STAYS] * 4)
        + specs
        + ([] if sums is None else [STAYS] * 2),
        [STAYS] * (2 + len(copies)) + [fixed(dim, 2 * units)] * sides,
        (total, total, *copies) + (jax.ShapeDtypeStruct((dim, 2 * units), LOW),) * sides,
        [],
        28,
        9 * sides,
        (
            spots,
            *(apart(*shared) if sums is None else pinned(*shared)),
            *weights,
            *(() if sums is None else pinned(*sums)),
        ),
        scalars=1,
        alias=None if sums is None else {5 + 2 * sides: 0, 6 + 2 * sides: 1},
    )


def middle_kernel(
    hidden,
    feed,
    grad_normed,
    cot,
    norms,
    w_own,
    w_oth,
    att_t,
    att_c,
    denom,
    phi_q,
    aux,
    mixed,
    grad_hidden,
    d_gain,
    d_shift,
    g_ext,
    leaving,
    d_own,
    d_oth,
    branch_t,
    state,
):
    step = pl.program_id(0)
    count = pl.num_programs(0)
    heads, feat, unused = phi_q.shape
    width = feat // 2
    rows = at(step, CHUNK)
    hid = hidden[...]
    mixed[...] = (hid + feed[rows, :]).astype(LOW)
    xhat, rstd = norm_parts(hid)
    grad = grad_normed[rows, :]
    back = cot[rows, :].astype(F32) + norm_back(grad, xhat, rstd, norms[2:3, :])
    grad_hidden[...] = back

    @pl.when(step == 0)
    def _():
        d_gain[...] = jnp.zeros_like(d_gain)
        d_shift[...] = jnp.zeros_like(d_shift)
        state[...] = jnp.zeros_like(state)

    d_gain[...] += jnp.sum(grad * xhat, axis=0, keepdims=True)
    d_shift[...] += jnp.sum(grad, axis=0, keepdims=True)
    low = back.astype(LOW)
    branch_t[:, rows] = low.T
    reach = aux[2:3, rows].astype(LOW)
    first = lax.broadcasted_iota(jnp.int32, (16, CHUNK), 0) == 0
    part = heads * width // 2
    grad_att = [nn(low, weights[:, part:]) for weights in (w_own, w_oth)]
    turned = [
        piece[:, inner * feat : (inner + 1) * feat].T
        for piece in grad_att
        for inner in range(piece.shape[1] // feat)
    ]
    exts = []
    for head in range(heads):
        ga = turned[head // 2][head % 2 * width : (head % 2 + 1) * width]
        inverse = 1.0 / denom[head : head + 1, rows]
        centered = att_c[head * width : (head + 1) * width, :].astype(F32)
        gd = -jnp.sum(ga * centered, axis=0, keepdims=True) * inverse
        exts.append(
            jnp.concatenate([(ga * inverse).astype(LOW), jnp.where(first, gd, 0.0).astype(LOW)], axis=0)
        )
    more = [nt(ext * reach, phi_q[head, :, rows]) for head, ext in enumerate(exts)]
    for head in range(heads):
        g_ext[head, :, rows] = exts[head]
        state[head] += more[head]
    leaving[...] = state[...].astype(LOW)

    @pl.when(step == count - 1)
    def _():
        start = 0
        for out in (d_own, d_oth):
            size = out.shape[1]
            out[...] = nt(branch_t[...], att_t[start : start + size, :]).astype(LOW)
            start += size


def middle(hidden, feed, grad_normed, cot, norms, w_own, w_oth, att_t, att_c, denom, phi_q, aux):
    rows, dim = hidden.shape
    heads, feat, unused = phi_q.shape
    width = feat // 2
    part = heads * width // 2
    block = pl.BlockSpec((CHUNK, dim), lambda c, *_: (c, 0))
    return call(
        middle_kernel,
        "middle",
        (rows // CHUNK,),
        [block]
        + [STAYS] * 3
        + [whole(norms), whole(w_own), whole(w_oth)]
        + [STAYS, pl.BlockSpec((heads * width, CHUNK), lambda c, *_: (0, c)), STAYS, STAYS]
        + [whole(aux)],
        [block, block, fixed(1, dim), fixed(1, dim), STAYS, fixed(heads, EXT, feat)]
        + [fixed(dim, part)] * 2,
        (
            streamed((rows, dim), LOW),
            streamed((rows, dim), F32),
            jax.ShapeDtypeStruct((1, dim), F32),
            jax.ShapeDtypeStruct((1, dim), F32),
            kept_in_vmem((heads, EXT, rows), LOW),
            streamed((heads, EXT, feat), LOW),
        )
        + (jax.ShapeDtypeStruct((dim, part), LOW),) * 2,
        [pltpu.VMEM((dim, rows), LOW), pltpu.VMEM((heads, EXT, feat), F32)],
        20,
        13,
        (
            *apart(hidden),
            *pinned(feed, grad_normed, cot),
            norms,
            w_own,
            w_oth,
            *pinned(att_t),
            *apart(att_c),
            *pinned(denom, phi_q),
            aux,
        ),
    )


def attend_back_kernel(
    side,
    carry,
    kept,
    aux,
    mask,
    phi_q,
    phi_k,
    phi_k_nat,
    v_nat,
    v_ext,
    g_ext,
    prefix,
    final,
    entering,
    arriving,
    q_t,
    k_t,
    maps,
    grads,
    d_maps,
    state,
    d_fq,
    d_fk,
):
    step = pl.program_id(0)
    count = pl.num_programs(0)
    heads, feat, unused = phi_q.shape
    width = feat // 2
    part = heads * width // 2
    half = heads // 2
    chunk = count - 1 - step
    rows = at(chunk, CHUNK)
    keep_in = carry[chunk]
    keep = kept[chunk]
    reach = aux[0:1, rows].astype(LOW)
    written = aux[1:2, rows].astype(LOW)
    mask_now = mask[0]

    @pl.when(step == 0)
    def _():
        for head in range(half):
            state[head] = arriving[(1 - side) * half + head].astype(F32)
        d_fq[...] = jnp.zeros_like(d_fq)
        d_fk[...] = jnp.zeros_like(d_fk)

    locals_ = range(half)
    pairs = range(half // 2)
    centers = [center_of(final, entering, side * half // 2 + p, 2 * phi_q.shape[2]) for p in pairs]
    v_pairs = [
        (v_nat[:, p * feat : (p + 1) * feat].astype(F32) - centers[p][:1]).astype(LOW) for p in pairs
    ]
    columns = [center.T for center in centers]
    nears = [columns[n // 2][n % 2 * width : (n % 2 + 1) * width, :] for n in locals_]
    pqs = [phi_q[side * half + n, :, rows] for n in locals_]
    pks = [phi_k[n] for n in locals_]
    exts = [g_ext[side * half + n, :, rows] for n in locals_]
    scores = [
        nn(phi_k_nat[rows, (side * half + n) * feat : (side * half + n + 1) * feat], pqs[n]) for n in locals_
    ]
    blank = jnp.zeros((width, CHUNK), LOW)
    gws = []
    for n in locals_:
        numer = exts[n][:width]
        padded = jnp.concatenate([numer, blank] if n % 2 == 0 else [blank, numer], axis=0)
        gws.append(nn(v_pairs[n // 2], padded))
    weights = [score.astype(LOW) * mask_now for score in scores]
    gws = [
        (gw + ext[width : width + 1].astype(F32)).astype(LOW) * mask_now for gw, ext in zip(gws, exts)
    ]
    befores, values, afters, reached = [], [], [], []
    for n in locals_:
        before = prefix[0, n] + keep_in * entering[(1 - side) * half + n]
        befores.append(
            jnp.concatenate([before[:width] - nears[n] * before[width : width + 1], before[width:]], axis=0).astype(LOW)
        )
        value = v_ext[side * half + n, :, rows]
        near = jnp.concatenate([nears[n]] * (CHUNK // feat), axis=1)
        value = jnp.concatenate([(value[:width].astype(F32) - near).astype(LOW), value[width:]], axis=0)
        values.append(value * written)
        afters.append(state[n].astype(LOW))
        reached.append(exts[n] * reach)
    g_phi_q = [nn(pks[n], gws[n]) + tn(befores[n], reached[n]) for n in locals_]
    g_phi_k = [nt(pqs[n], gws[n]) + tn(afters[n], values[n]) for n in locals_]
    g_values = [
        nt(exts[n][:width], weights[n]) + nn(afters[n][:width], pks[n] * written) for n in locals_
    ]
    more = [nt(reached[n], pqs[n]) for n in locals_]
    grads_q = [softmax_pair_back(pqs[n], g_phi_q[n]).astype(LOW) for n in locals_]
    grads_k = [softmax_pair_back(pks[n], g_phi_k[n]).astype(LOW) for n in locals_]
    for n in locals_:
        state[n] = keep * state[n] + more[n]
    both = [[jnp.concatenate(g[2 * p : 2 * p + 2], axis=0) for p in pairs] for g in (grads_q, grads_k)]
    through = [[nn(maps[2 * kind, side * half // 2 + p], both[kind][p]) for p in pairs] for kind in range(2)]
    onto = [
        [nt(source[p * feat : (p + 1) * feat, :], both[kind][p]) for p in pairs]
        for kind, source in enumerate((q_t, k_t))
    ]
    for p in pairs:
        for kind in range(2):
            start = kind * part + p * feat
            grads[start : start + feat, rows] = through[kind][p].astype(LOW)
        start = 2 * part + p * feat
        grads[start : start + feat, rows] = jnp.concatenate(g_values[2 * p : 2 * p + 2], axis=0).astype(LOW)
        d_fq[p] += onto[0][p]
        d_fk[p] += onto[1][p]

    @pl.when(step == count - 1)
    def _():
        first = lax.broadcasted_iota(jnp.int32, (width, feat), 1) < width
        for kind, source in enumerate((d_fq, d_fk)):
            for local in range(half // 2):
                block = source[local]
                d_maps[kind, local] = jnp.where(first, block[:width], block[width:])


def attend_back(
    side, aux, mask, phi_q, phi_k, phi_k_nat, v_nat, v_ext, g_ext, prefix, final, entering, arriving, q_t, k_t, maps, carry, kept
):
    heads, feat, rows = phi_q.shape
    width = feat // 2
    half = heads // 2
    count = rows // CHUNK
    lanes = pl.BlockSpec((half * width, CHUNK), lambda c, *_: (side, count - 1 - c))
    return call(
        functools.partial(attend_back_kernel, side),
        "attend_back",
        (rows // CHUNK,),
        [
            whole(aux),
            pl.BlockSpec((1, CHUNK, CHUNK), lambda c, *_: (count - 1 - c, 0, 0)),
            STAYS,
            pl.BlockSpec((half, feat, CHUNK), lambda c, *_: (side, 0, count - 1 - c)),
            STAYS,
            pl.BlockSpec((CHUNK, half * width), lambda c, *_: (count - 1 - c, side)),
            STAYS,
            STAYS,
            pl.BlockSpec((1, half, EXT, feat), lambda c, *_: (count - 1 - c, side, 0, 0)),
            whole(final),
            whole(entering),
            whole(arriving),
            lanes,
            lanes,
            STAYS,
        ],
        [STAYS, fixed(2, half // 2, width, feat)],
        (kept_in_vmem((3 * half * width, rows), LOW), streamed((2, half // 2, width, feat), F32)),
        [pltpu.VMEM((half, EXT, feat), F32)] + [pltpu.VMEM((half // 2, feat, feat), F32)] * 2,
        10,
        14,
        (
            carry,
            kept,
            aux,
            *apart(mask),
            *pinned(phi_q),
            *apart(phi_k),
            *pinned(phi_k_nat),
            *apart(v_nat),
            *pinned(v_ext, g_ext),
            *apart(prefix, final, entering, arriving, q_t, k_t),
            *pinned(maps),
        ),
        scalars=2,
    )


def weight_kernel(normed_t, grads, out):
    out[...] = nt(normed_t[...], grads[...]).astype(LOW)


def weight_grads(normed_t, grads):
    dim, rows = normed_t.shape
    size = grads.shape[0]
    return call(
        weight_kernel,
        "weight_grads",
        (1,),
        [whole(normed_t), STAYS],
        fixed(dim, size),
        jax.ShapeDtypeStruct((dim, size), LOW),
        [],
        8,
        0,
        (*apart(normed_t), *pinned(grads)),
    )


def first_kernel(tokens, norms, grad_hidden, wa_own, wb_own, wa_oth, wb_oth, grads_own, grads_oth, out, d_gain, d_shift):
    step = pl.program_id(0)
    rows = at(step, CHUNK)
    total = None
    for wa, wb, grads in ((wa_own, wb_own, grads_own), (wa_oth, wb_oth, grads_oth)):
        cut = wa.shape[1]
        rest = grads.shape[0] - cut
        term = nn(wa[...], grads[:cut, rows]) + nn(wb[:, :rest], grads[cut:, rows])
        total = term if total is None else total + term
    grad = total.T
    xhat, rstd = norm_parts(tokens[...].astype(F32))
    out[...] = (grad_hidden[...] + norm_back(grad, xhat, rstd, norms[0:1, :])).astype(LOW)

    @pl.when(step == 0)
    def _():
        d_gain[...] = jnp.zeros_like(d_gain)
        d_shift[...] = jnp.zeros_like(d_shift)

    d_gain[...] += jnp.sum(grad * xhat, axis=0, keepdims=True)
    d_shift[...] += jnp.sum(grad, axis=0, keepdims=True)


def first_back(tokens, norms, grad_hidden, weights, grads):
    rows, dim = tokens.shape
    block = pl.BlockSpec((CHUNK, dim), lambda c: (c, 0))
    return call(
        first_kernel,
        "first_back",
        (rows // CHUNK,),
        [block, whole(norms), block] + [whole(w) for w in weights] + [STAYS] * 2,
        [block, fixed(1, dim), fixed(1, dim)],
        (
            streamed((rows, dim), LOW),
            jax.ShapeDtypeStruct((1, dim), F32),
            jax.ShapeDtypeStruct((1, dim), F32),
        ),
        [],
        16,
        9,
        (*apart(tokens), norms, *apart(grad_hidden), *weights, *pinned(*grads)),
    )


SWAP = [(0, 1), (1, 0)]


def swap(piece):
    return lax.ppermute(piece, "mp", SWAP)


def flip(piece, bit, size):
    return lax.ppermute(piece, "dp", [(i, i ^ bit) for i in range(size)])


def turn(piece, by, size):
    return lax.ppermute(piece, "dp", [(i, (i + by) % size) for i in range(size)])


def after(value, *others):
    return lax.optimization_barrier((value, *others))[0]


class Places:
    def __init__(self, size, staged):
        self.size = size
        self.deep = size // 4
        self.staged = staged
        place = lax.axis_index("dp")
        self.spots = jnp.stack([place % 2, (place // 2) % 2, place // 4, lax.axis_index("mp")])

    def flip(self, value, axis):
        return flip(value, 1 if axis == "x" else 2, self.size)


def line_kernel(cut, spots, *refs):
    deep = len(refs) - 2
    for s in range(deep):
        spot = lax.rem(spots[2] + deep - s, deep)
        refs[-2][spot] = refs[s][:, :cut]
        refs[-1][spot] = refs[s][:, cut:]


def gather_line(shard, cut, at, *others):
    pieces = [shard] + [turn(shard, 4 * s, at.size) for s in range(1, at.deep)]
    if others:
        pieces[1] = after(pieces[1], *others)
    rows, columns = shard.shape
    shapes = [(at.deep, rows, cut), (at.deep, rows, columns - cut)]
    return call(
        functools.partial(line_kernel, cut),
        "line",
        (1,),
        [whole(p) for p in pieces],
        [fixed(*shape) for shape in shapes],
        tuple(jax.ShapeDtypeStruct(shape, LOW) for shape in shapes),
        [],
        6,
        0,
        (at.spots, *pieces),
        scalars=1,
    )


def pair_kernel(axes, dims, spots, *refs):
    for index, (axis, dim) in enumerate(zip(axes, dims)):
        mine, theirs, out = refs[2 * index], refs[2 * index + 1], refs[4 + index]
        bit = spots[0 if axis == "x" else 1]
        for source, place in ((mine, bit), (theirs, 1 - bit)):
            if dim == 1:
                out[:, pl.ds(place, 1)] = source[...][:, None]
            else:
                out[:, :, pl.ds(place, 1)] = source[...][:, :, None]


def first_by(shape):
    tail = (0,) * (len(shape) - 1)
    return pl.BlockSpec((1, *shape[1:]), lambda d, *_: (jnp.minimum(d, shape[0] - 1), *tail))


def gather_pair(values, axes, at, *others, kind=jax.ShapeDtypeStruct):
    moved = [at.flip(v, axis) for v, axis in zip(values, axes)]
    if others:
        moved[0] = after(moved[0], *others)
    dims = [v.ndim - 2 if axis == "x" else 1 for v, axis in zip(values, axes)]
    shapes = [(*v.shape[:d], 2, *v.shape[d:]) for v, d in zip(values, dims)]
    return call(
        functools.partial(pair_kernel, axes, dims),
        "pair",
        (at.deep,),
        [first_by(v.shape) for v in values for unused in (0, 1)],
        [first_by(shape) for shape in shapes],
        tuple(kind(shape, LOW) for shape in shapes),
        [],
        8,
        0,
        (at.spots, values[0], moved[0], values[1], moved[1]),
        scalars=1,
    )


def first_fold_kernel(axes, cuts, deep, spots, *refs):
    outs = refs[-4:]
    step = pl.program_id(0)
    if len(refs) == 5 + 2 * len(cuts):
        rider = refs[-5]
        rows = outs[0].shape[2]

        @pl.when(step == deep)
        def _():
            for index in range(rider.shape[0] // rows):
                group, place = divmod(index, 2)
                outs[0][0, place, :, group * 128 : (group + 1) * 128] = rider[index * rows : (index + 1) * rows, :]

        @pl.when(step < deep)
        def _():
            first_fold_step(axes, cuts, spots, refs, outs)

    else:
        first_fold_step(axes, cuts, spots, refs, outs)


def first_fold_step(axes, cuts, spots, refs, outs):
    for index, axis in enumerate(axes):
        bit = spots[0 if axis == "x" else 1]
        sent, kept = outs[2 * index : 2 * index + 2]
        start = 0
        for segment, cut in enumerate(cuts):
            pair = refs[2 * segment : 2 * segment + 2]
            columns = slice(0, cut) if index == 0 else slice(cut, pair[0].shape[-1])
            size = columns.stop - columns.start
            for out, place in ((sent, 1 - bit), (kept, bit)):
                if axis == "x":
                    terms = [r[:, :, pl.ds(place, 1), :, columns].astype(F32) for r in pair]
                else:
                    terms = [r[:, pl.ds(place, 1), :, :, columns].astype(F32) for r in pair]
                total = (terms[0] + terms[1]).astype(LOW)
                out[..., start : start + size] = total.reshape(*out.shape[:-1], size)
            start += size


def fold_kernel(axes, spots, *refs):
    for index, axis in enumerate(axes):
        bit = spots[0 if axis == "x" else 1]
        sent, kept = refs[4 + 2 * index : 6 + 2 * index]
        for out, place in ((sent, 1 - bit), (kept, bit)):
            terms = [r[:, pl.ds(place, 1)].astype(F32) for r in refs[2 * index : 2 * index + 2]]
            out[...] = (terms[0] + terms[1]).astype(LOW).reshape(out.shape)


def spread_kernel(spots, a_kept, a_sent, b_kept, b_sent, *outs):
    deep = len(outs)
    cut = a_kept.shape[-1]
    for s, out in enumerate(outs):
        spot = lax.rem(spots[2] + s, deep)
        out[:, :cut] = (a_kept[spot].astype(F32) + a_sent[spot].astype(F32)).astype(LOW)
        out[:, cut:] = (b_kept[spot].astype(F32) + b_sent[spot].astype(F32)).astype(LOW)


class Scatter:
    def __init__(self, segments, at):
        self.at = at
        self.cuts = [cut for own, oth, cut in segments]
        self.cut = sum(self.cuts)
        self.terms = [[own, swap(oth)] for own, oth, cut in segments]
        if at.staged:
            split = lambda v: v.reshape(at.deep, 2, 2, v.shape[0] // at.size, v.shape[1])
            self.terms = [[split(v) for v in pair] for pair in self.terms]

    def wait_for(self, *others):
        self.terms[0][1] = after(self.terms[0][1], *others)

    def fold(self, axes, rider=None):
        at = self.at
        flats = [v for pair in self.terms for v in pair]
        if not at.staged:
            return flats[0]
        if self.cuts:
            columns = sum(pair[0].shape[-1] for pair in self.terms)
            head = flats[0].shape[:2]
            rows = flats[0].shape[3]
            lefts = [(*head, rows, self.cut), (*head, rows, columns - self.cut)]
            kernel = functools.partial(first_fold_kernel, axes, tuple(self.cuts), at.deep)
        else:
            lefts = [(v.shape[0], *v.shape[2:]) for v in flats[::2]]
            kernel = functools.partial(fold_kernel, axes)
        outs = [left for left in lefts for unused in (0, 1)]
        extra = []
        steps = at.deep
        if rider is not None:
            extra = [rider]
            steps += 1
            outs[0] = (steps, *outs[0][1:])
        a_sent, a_kept, b_sent, b_kept = call(
            kernel,
            "fold",
            (steps,),
            [first_by(v.shape) for v in flats] + [whole(v) for v in extra],
            [first_by(left) for left in outs],
            tuple(jax.ShapeDtypeStruct(left, LOW) for left in outs),
            [],
            12,
            0,
            (at.spots, *flats, *extra),
            scalars=1,
        )
        self.cuts = []
        self.terms = [[a_kept, at.flip(a_sent, axes[0])], [b_kept, at.flip(b_sent, axes[1])]]
        return a_kept

    def spread(self):
        at = self.at
        if not at.staged:
            return self.terms[0][0]
        a, b = self.terms
        shape = (a[0].shape[1], self.cut + b[0].shape[-1])
        own, *sends = call(
            spread_kernel,
            "spread",
            (1,),
            [whole(v) for v in (*a, *b)],
            [fixed(*shape)] * at.deep,
            (jax.ShapeDtypeStruct(shape, LOW),) * at.deep,
            [],
            8,
            0,
            (at.spots, *a, *b),
            scalars=1,
        )
        self.parts = [own] + [turn(p, 4 * s, at.size) for s, p in enumerate(sends, 1)]
        return own

    def end(self, *others):
        if not self.at.staged:
            sums = [own.astype(F32) + moved.astype(F32) for own, moved in self.terms]
            total = [t[:, :cut] for t, cut in zip(sums, self.cuts)] + [t[:, cut:] for t, cut in zip(sums, self.cuts)]
            total = lax.psum_scatter(jnp.concatenate(total, axis=1), "dp", scatter_dimension=0, tiled=True)
        else:
            if others:
                self.parts[1] = after(self.parts[1], *others)
            total = sum(p.astype(F32) for p in self.parts)
        return total


def ride_kernel(deep, spots, *refs):
    a_kept, a_moved, b_kept, b_moved, gain1, shift1, gain2, shift2, maps, early = refs[:10]
    late = refs[10 : 10 + deep]
    a_sent, a_left, b_sent, b_left, norm_low, maps_low, g_fc, g_down, g_out = refs[10 + deep :]
    rows = a_left.shape[1]
    units = early.shape[1] // 2
    total = late[0][...].astype(F32)
    for part in late[1:]:
        total = total + part[...].astype(F32)
    rest = total.shape[1] - 2 * units
    cut = units + (rest // 128 + 1) // 2 * 128
    g_fc[:, :units] = early[:, :units]
    g_down[:, :units] = early[:, units:]
    g_fc[:, units:] = total[:, :units]
    g_down[:, units:] = total[:, cut : cut + units]
    g_out[:, : cut - units] = total[:, units:cut]
    g_out[:, cut - units :] = total[:, cut + units :]
    blank = jnp.zeros((4, gain1.shape[1]), F32)
    norm_now = jnp.concatenate([gain1[...], shift1[...], gain2[...], shift2[...], blank], axis=0)
    norm_low[...] = jnp.concatenate([norm_now, jnp.zeros_like(norm_now)], axis=0).astype(LOW)
    for index in range(maps.shape[0] // rows):
        group, place = divmod(index, 2)
        moved = a_moved[deep, place, :, group * 128 : (group + 1) * 128].astype(F32)
        here = slice(index * rows, (index + 1) * rows)
        maps_low[here, :] = (maps[here, :].astype(F32) + moved).astype(LOW)
    for kept, moved, sent, left, bit in (
        (a_kept, a_moved, a_sent, a_left, spots[1]),
        (b_kept, b_moved, b_sent, b_left, spots[0]),
    ):
        columns = left.shape[2]
        for out, place in ((sent, 1 - bit), (left, bit)):
            terms = [r[:deep, pl.ds(place, 1)].astype(F32) for r in (kept, moved)]
            total = (terms[0] + terms[1]).astype(LOW)
            if out is left:
                out[...] = total.reshape(deep, rows, columns)
            else:
                out[: deep * rows] = total.reshape(deep * rows, columns)
        rest = norm_now[:, columns:]
        rest = jnp.concatenate([rest, jnp.zeros((8, columns - rest.shape[1]), F32)], axis=1)
        sent[deep * rows :] = jnp.concatenate([norm_now[:, :columns], rest], axis=0).astype(LOW)


def last_spread_kernel(spots, a_kept, a_moved, b_kept, b_moved, norm, norm_far, maps, maps_moved, *outs):
    *parts, maps_low = outs
    deep, rows, cut = a_kept.shape
    dim = norm.shape[1]
    maps_low[...] = (maps[...].astype(F32) + maps_moved[...].astype(F32)).astype(LOW)
    near = []
    for moved in (b_moved, a_moved):
        columns = moved.shape[1]
        tail = moved[deep * rows :].astype(F32)
        near.append(jnp.concatenate([tail[:8], tail[8:, : dim - columns]], axis=1))
    plane = (norm[...].astype(F32)[:8] + near[0]) + (near[1] + norm_far[...].astype(F32)[:8])
    tail = jnp.concatenate([plane[:, i : i + 128] for i in range(0, dim, 128)], axis=0)
    for s, out in enumerate(parts):
        spot = lax.rem(spots[2] + s, deep)
        place = pl.ds(pl.multiple_of(spot * rows, rows), rows)
        rest = out.shape[1] - 128
        out[:, :cut] = (a_kept[spot].astype(F32) + a_moved[place].astype(F32)).astype(LOW)
        out[:, cut:rest] = (b_kept[spot].astype(F32) + b_moved[place].astype(F32)).astype(LOW)
        out[:, rest:] = tail.astype(LOW)


def finish_kernel(spots, *refs):
    deep = len(refs) - 9
    parts = refs[:deep]
    maps, maps_moved, g_query, g_key, g_value, norms, map_q, map_k, held = refs[deep:]
    rows, part = g_query.shape
    total = None
    for s, ref in enumerate(parts):
        value = ref[...].astype(F32)
        held[lax.rem(spots[2] + deep - s, deep)] = value[:, 3 * part :]
        total = value if total is None else total + value
    for index, out in enumerate((g_query, g_key, g_value)):
        out[...] = total[:, index * part : (index + 1) * part]
    together = held[0]
    for spot in range(1, deep):
        together = together + held[spot]
    for index in range(rows // 8):
        norms[:, index * 128 : (index + 1) * 128] = together[index * 8 : (index + 1) * 8]
    width = map_q.shape[1]
    both = maps[...].astype(F32) + maps_moved[...].astype(F32)
    heads = map_q.shape[0]
    for kind, out in enumerate((map_q, map_k)):
        for pair in range(heads // 2):
            start = (kind * heads // 2 + pair) * width
            block = both[start : start + width]
            out[2 * pair] = block[:, :width]
            out[2 * pair + 1] = block[:, width:]


def finish_last(sums, norm, map_grads, early, late, part, heads, width, at):
    small = lambda shape, kind: jax.ShapeDtypeStruct(shape, kind)
    (a_kept, a_moved), (b_kept, b_moved) = sums.terms
    deep, unused, rows, cut = a_kept.shape
    rest = b_kept.shape[3]
    dim = norm[0].shape[1]
    units = early.shape[1]
    ins = (a_kept, a_moved, b_kept, b_moved, *norm, map_grads, early, *late)
    outs = (
        small((deep * rows + 16, cut), LOW),
        small((deep, rows, cut), LOW),
        small((deep * rows + 16, rest), LOW),
        small((deep, rows, rest), LOW),
        small((16, dim), LOW),
        small(map_grads.shape, LOW),
        small((rows, units), F32),
        small((rows, units), F32),
        small((rows, part), F32),
    )

    def run(kernel, name, ins, outs, scratch):
        return call(
            kernel,
            name,
            (1,),
            [whole(v) for v in ins],
            [fixed(*out.shape) for out in outs],
            outs,
            scratch,
            12,
            0,
            (at.spots, *ins),
            scalars=1,
        )

    kernel = functools.partial(ride_kernel, deep)
    a_sent, a_kept, b_sent, b_kept, norm_low, maps, *done = run(kernel, "ride", ins, outs, [])
    across = [(i, i ^ 3) for i in range(at.size)]
    ins = (
        a_kept,
        at.flip(a_sent, "y"),
        b_kept,
        at.flip(b_sent, "x"),
        norm_low,
        lax.ppermute(norm_low, "dp", across),
        maps,
        flip(maps, 4 << (at.size.bit_length() - 4), at.size),
    )
    ins = lax.optimization_barrier(ins)
    outs = (small((rows, cut + rest + 128), LOW),) * deep + (small(map_grads.shape, LOW),)
    own, *sends, maps = run(last_spread_kernel, "last_spread", ins, outs, [])
    ins = (own, *(turn(p, 4 * s, at.size) for s, p in enumerate(sends, 1)), maps, at.flip(maps, "y"))
    ins = lax.optimization_barrier(ins)
    outs = (
        (small((rows, part), F32),) * 3
        + (small((8, dim), F32),)
        + (small((heads // 2, width, width), F32),) * 2
    )
    return done, run(finish_kernel, "finish", ins, outs, [pltpu.VMEM((deep, rows, 128), F32)])


def add_along(value, steps, size):
    for step in steps:
        if step < size:
            value = value.astype(LOW)
            value = value.astype(F32) + flip(value, step, size).astype(F32)
    return value


def per_device(
    size,
    tokens,
    norm1_gain,
    norm1_shift,
    w_query,
    w_key,
    w_value,
    w_out,
    fmap_query,
    fmap_key,
    norm2_gain,
    norm2_shift,
    w_fc,
    w_down,
    lengths,
    cotangent,
):
    rows, dim = tokens.shape
    heads = 2 * fmap_query.shape[0]
    width = fmap_query.shape[1]
    feat = 2 * width
    part = w_query.shape[1]
    count = rows // CHUNK
    core = lax.axis_index("mp")
    staged = size % 4 == 0 and dim // size % 16 == 0
    where = Places(size, staged)
    units = w_fc.shape[1] // 2
    cut = (3 * part // feat + 1) // 2 * feat
    cut_out = (part // feat + 1) // 2 * feat
    (shard_rest,) = pack((w_fc, w_down), (((0, 0, 2 * units), (1, 0, 2 * units)),))
    (shard_qkv,) = pack(
        (w_query, w_key, w_value, after(w_out, shard_rest)), (((0, 0, part), (1, 0, part), (2, 0, part), (3, 0, part)),)
    )
    rest = lax.all_gather(shard_rest, ("dp", "mp"), axis=0)
    rest = rest.reshape(size, 2, *shard_rest.shape)
    if shard_rest.shape[0] % 16:
        rest = rest.swapaxes(0, 1).reshape(1, 2, dim, -1)
    fq_oth, fk_oth = swap(fmap_query), swap(fmap_key)
    if staged:
        qkv = gather_line(shard_qkv, 2 * part, where)
        lengths = after(lengths, qkv[0])

    ends = jnp.cumsum(lengths[0])
    places = core * rows - 1 + jnp.arange(rows + 1, dtype=jnp.int32)
    numbers = jnp.sum((ends[None, :] <= places[:, None]).astype(jnp.int32), axis=1)
    numbers = jnp.where(places < 0, -1, numbers)
    segment = numbers[1:]
    living = places[1:] < ends[-1]
    blocks = segment.reshape(count, CHUNK)
    last = blocks[:, -1]
    before = jnp.concatenate([numbers[:1], last[:-1]])
    kept = (last == before).astype(F32)
    carry = ((before == numbers[0]) & (core > 0)).astype(F32)
    reach = (blocks == before[:, None]).reshape(rows) & living
    written = (blocks == last[:, None]).reshape(rows)
    reach_in = (segment == numbers[0]) & living
    aux = jnp.stack([reach, written, reach_in, ~living] + [jnp.zeros_like(living)] * 4).astype(F32)
    order = jnp.arange(CHUNK, dtype=jnp.int32)
    mask = (
        (blocks[:, :, None] == blocks[:, None, :])
        & (order[:, None] <= order[None, :])
        & living.reshape(count, 1, CHUNK)
    ).astype(LOW)

    norms = jnp.stack([norm1_gain, norm1_shift, norm2_gain, norm2_shift])

    norms, aux, mask, kept, carry = lax.optimization_barrier((norms, aux, mask, kept, carry))
    spots = where.spots
    if staged:
        qkv = gather_pair(qkv, "xy", where)
        tokens = after(tokens, qkv[0], mask)
    normed1, normed1_t, cot_t, maps = prepare(
        tokens, cotangent, norms, fmap_query, fq_oth, fmap_key, fk_oth
    )
    if staged:
        qkv = tuple(map(flat, gather_pair(qkv, "yx", where, maps)))
    else:
        qkv = tuple(
            lax.all_gather(s, "dp", axis=0, tiled=True) for s in (shard_qkv[:, : 2 * part], shard_qkv[:, 2 * part :])
        )
    qkv = (*qkv, *map(swap, qkv))
    q_t, k_t, v_nat, v_ext, phi_q, phi_k, phi_k_nat, prefix, final = project(
        normed1, *qkv, maps, aux, kept, heads, width
    )
    entering = swap(final)
    att_t, att_c, denom = attend(aux, mask, phi_q, phi_k_nat, v_ext, prefix, final, entering, carry)
    hidden, normed2, normed2_t = mix(tokens, norms, qkv[1], qkv[3], att_t)
    specs = [[gathered(rest, units, index, side) for index in (0, 1, 2, 3)] for side in (0, 1)]
    rest = apart(rest)
    feed, grad_normed, *shared, d_early_oth = feed_forward(
        spots, normed2, normed2_t, cotangent, cot_t, rest * 2, specs[1][::2], units, None
    )
    cot = shared[2]
    feed_part = functools.partial(feed_forward, spots, *shared)
    feed, grad_normed, d_early_own = feed_part(rest * 2, specs[0][::2], units, (feed, grad_normed))
    sums_early = Scatter([(d_early_own, d_early_oth, units)], where)
    feed = after(feed, sums_early.fold("xy"))
    feed, grad_normed, d_late_own, d_late_oth = feed_part(
        rest * 4, specs[0][1::2] + specs[1][1::2], units, (feed, grad_normed)
    )
    sums_early.wait_for(d_late_oth)
    hidden = after(hidden, sums_early.fold("yx"))
    mixed, grad_hidden, d_gain2, d_shift2, g_ext, leaving, d_out_own, d_out_oth = middle(
        hidden, feed, grad_normed, cot, norms, qkv[1], qkv[3], att_t, att_c, denom, phi_q, aux
    )
    sums_early.wait_for(d_gain2)
    started = sums_early.spread()
    arriving = lax.ppermute(after(leaving, started), "mp", [(1, 0)])
    d_out_oth = after(d_out_oth, started)
    sums_late = Scatter([(d_late_own, d_late_oth, units), (d_out_own, d_out_oth, cut_out)], where)
    sums_late.wait_for(started)
    arriving = after(arriving, sums_late.fold("xy"))
    back = functools.partial(
        attend_back, carry=carry, kept=kept, prefix=prefix, final=final, entering=entering, q_t=q_t, k_t=k_t, maps=maps
    )
    back_inputs = (aux, mask, phi_q, phi_k, phi_k_nat, v_nat, v_ext, g_ext)
    lanes = lambda v: v.reshape(-1, feat)
    grads_oth, maps_oth = back(1, *back_inputs, arriving=arriving)
    total_early = sums_early.end(maps_oth)
    d_qkv_oth = weight_grads(normed1_t, after(grads_oth, total_early))
    sums_late.wait_for(d_qkv_oth)
    arriving = after(arriving, sums_late.fold("yx"))
    grads_own, maps_own = back(0, *back_inputs, arriving=arriving)
    sums_late.wait_for(maps_own)
    grads_own = after(grads_own, sums_late.spread())
    map_grads = lanes(maps_own + swap(maps_oth))
    d_qkv_own = weight_grads(normed1_t, grads_own)
    if staged:
        map_grads = map_grads.astype(LOW)
        for step in [4 << i for i in range(size.bit_length() - 4)]:
            moved = after(flip(map_grads, step, size), d_qkv_own)
            map_grads = (map_grads.astype(F32) + moved.astype(F32)).astype(LOW)
    sums_qkv = Scatter([(d_qkv_own, d_qkv_oth, cut)], where)
    grad_hidden = after(grad_hidden, sums_qkv.fold("xy", map_grads if staged else None))
    grad_tokens, d_gain1, d_shift1 = first_back(tokens, norms, grad_hidden, qkv, (grads_own, grads_oth))
    norm_grads = (d_gain1, d_shift1, d_gain2, d_shift2)
    if staged:
        sums_qkv.wait_for(d_gain1)
        done, (g_query, g_key, g_value, norm_grads, map_q, map_k) = finish_last(
            sums_qkv, norm_grads, map_grads, total_early, sums_late.parts, part, heads, width, where
        )
        g_fc, g_down, g_out = done
    else:
        total_late = sums_late.end()
        grad_qkv = sums_qkv.end()
        g_query, g_key, g_value = (grad_qkv[:, i * part : (i + 1) * part] for i in range(3))
        norm_grads, map_grads = lax.psum((jnp.concatenate(norm_grads, axis=0), map_grads), "dp")
        map_grads = map_grads.reshape(2, heads // 4, width, 2, width)
        map_q, map_k = map_grads.swapaxes(2, 3).reshape(2, heads // 2, width, width)
        cut_late = units + cut_out
        g_fc = jnp.concatenate([total_early[:, :units], total_late[:, :units]], axis=1)
        g_down = jnp.concatenate([total_early[:, units:], total_late[:, cut_late : cut_late + units]], axis=1)
        g_out = jnp.concatenate([total_late[:, units:cut_late], total_late[:, cut_late + units :]], axis=1)
    norm_grads = norm_grads + swap(norm_grads)
    return (
        mixed,
        grad_tokens,
        norm_grads[0],
        norm_grads[1],
        g_query,
        g_key,
        g_value,
        g_out,
        map_q,
        map_k,
        norm_grads[2],
        norm_grads[3],
        g_fc,
        g_down,
    )


def solution(mesh):
    placed = (
        P(("dp", "mp"), None),
        P(),
        P(),
        P("dp", "mp"),
        P("dp", "mp"),
        P("dp", "mp"),
        P("dp", "mp"),
        P("mp", None, None),
        P("mp", None, None),
        P(),
        P(),
        P("dp", "mp"),
        P("dp", "mp"),
        P("dp", None),
        P(("dp", "mp"), None),
    )
    return jax.shard_map(
        functools.partial(per_device, mesh.shape["dp"]),
        mesh=mesh,
        in_specs=placed,
        out_specs=(
            P(("dp", "mp"), None),
            P(("dp", "mp"), None),
            P(),
            P(),
            P("dp", "mp"),
            P("dp", "mp"),
            P("dp", "mp"),
            P("dp", "mp"),
            P("mp", None, None),
            P("mp", None, None),
            P(),
            P(),
            P("dp", "mp"),
            P("dp", "mp"),
        ),
        check_vma=False,
    )
```

```python
import functools

import jax
import jax.numpy as jnp
from jax import lax
from jax.experimental import pallas as pl
from jax.experimental.pallas import tpu as pltpu
from jax.sharding import PartitionSpec as P

EPS = 1e-05
CHUNK = 256
WIDE = 512
EXT = 80
LOW = jnp.bfloat16
F32 = jnp.float32
MIB = 1024 * 1024
PACE = 3_000_000_000
GELU_C = 0.7978845608028654
GELU_A = 0.044715


def nn(a, b):
    return lax.dot_general(a, b, (((1,), (0,)), ((), ())), preferred_element_type=F32)


def nt(a, b):
    return lax.dot_general(a, b, (((1,), (1,)), ((), ())), preferred_element_type=F32)


def tn(a, b):
    return lax.dot_general(a, b, (((0,), (0,)), ((), ())), preferred_element_type=F32)


def norm_parts(rows):
    center = rows - jnp.mean(rows, axis=-1, keepdims=True)
    spread = jnp.mean(center * center, axis=-1, keepdims=True)
    rstd = lax.rsqrt(spread + EPS)
    return center * rstd, rstd


def norm_back(grad, xhat, rstd, gain):
    e = grad * gain
    return rstd * (
        e - jnp.mean(e, axis=-1, keepdims=True) - xhat * jnp.mean(e * xhat, axis=-1, keepdims=True)
    )


def softmax_pair(logits):
    high = jnp.max(logits, axis=0, keepdims=True)
    least = jnp.min(logits, axis=0, keepdims=True)
    pos = jnp.exp(logits - high)
    neg = jnp.exp(least - logits)
    pos = pos * (1.0 / jnp.sum(pos, axis=0, keepdims=True))
    neg = neg * (1.0 / jnp.sum(neg, axis=0, keepdims=True))
    return jnp.concatenate([pos, neg], axis=0).astype(LOW)


def softmax_pair_back(phi, grad):
    width = phi.shape[0] // 2
    pos = phi[:width].astype(F32)
    neg = phi[width:].astype(F32)
    gp = grad[:width]
    gn = grad[width:]
    gp = gp - jnp.sum(pos * gp, axis=0, keepdims=True)
    gn = gn - jnp.sum(neg * gn, axis=0, keepdims=True)
    return pos * gp - neg * gn


def flat(value):
    return value.reshape(-1, value.shape[-1])


def kept_in_vmem(shape, dtype):
    return pltpu.VMEM(shape, dtype)


def streamed(shape, dtype):
    return pltpu.HBM(shape, dtype)


def apart(*arrays):
    return tuple(pltpu.with_memory_space_constraint(a, pltpu.HBM) for a in arrays)


def pinned(*arrays):
    return tuple(pltpu.with_memory_space_constraint(a, pltpu.VMEM) for a in arrays)


def whole(array):
    return pl.BlockSpec(
        array.shape, lambda *_: (0,) * array.ndim, pipeline_mode=pl.Buffered(1)
    )


def fixed(*shape):
    return pl.BlockSpec(shape, lambda *_: (0,) * len(shape))


STAYS = pl.BlockSpec(memory_space=pltpu.VMEM)


def at(step, size):
    return pl.ds(pl.multiple_of(step * size, size), size)


def call(kernel, name, grid, in_specs, out_specs, out_shape, scratch, limit, micros, args, scalars=0, alias=None):
    return pl.pallas_call(
        kernel,
        grid_spec=pltpu.PrefetchScalarGridSpec(
            num_scalar_prefetch=scalars,
            grid=grid,
            in_specs=in_specs,
            out_specs=out_specs,
            scratch_shapes=scratch,
        ),
        out_shape=out_shape,
        input_output_aliases=alias or {},
        compiler_params=pltpu.CompilerParams(vmem_limit_bytes=limit * MIB),
        cost_estimate=pl.CostEstimate(flops=micros * PACE, bytes_accessed=1024, transcendentals=0),
        name=name,
    )(*args)


def pack_kernel(groups, *refs):
    outs = refs[len(refs) - len(groups) :]
    for out, group in zip(outs, groups):
        start = 0
        for index, first, size in group:
            out[:, start : start + size] = refs[index][:, first : first + size]
            start += size


def pack(arrays, groups):
    rows = arrays[0].shape[0]
    shapes = [(rows, sum(size for unused, first, size in group)) for group in groups]
    return call(
        functools.partial(pack_kernel, groups),
        "pack",
        (1,),
        [whole(a) for a in arrays],
        [fixed(*shape) for shape in shapes],
        tuple(jax.ShapeDtypeStruct(shape, LOW) for shape in shapes),
        [],
        8,
        1,
        apart(*arrays),
    )


def prepare_kernel(
    tokens, cot, norms, fq_own, fq_oth, fk_own, fk_oth, normed, normed_t, cot_t, maps
):
    step = pl.program_id(0)
    rows = at(step, CHUNK)
    xhat, unused = norm_parts(tokens[...].astype(F32))
    low = (xhat * norms[0:1, :] + norms[1:2, :]).astype(LOW)
    normed[rows, :] = low
    normed_t[...] = low.T
    cot_t[...] = cot[...].T

    @pl.when(step == 0)
    def _():
        half, width, unused = fq_own.shape
        blank = jnp.zeros((width, width), F32)
        for kind, (own, oth) in enumerate(((fq_own, fq_oth), (fk_own, fk_oth))):
            for pair in range(half):
                source = own if pair < half // 2 else oth
                first = 2 * pair % half
                block = jnp.concatenate(
                    [
                        jnp.concatenate([source[first].astype(F32), blank], axis=1),
                        jnp.concatenate([blank, source[first + 1].astype(F32)], axis=1),
                    ],
                    axis=0,
                )
                maps[2 * kind, pair] = block.astype(LOW)
                maps[2 * kind + 1, pair] = block.T.astype(LOW)


def prepare(tokens, cot, norms, fq_own, fq_oth, fk_own, fk_oth):
    rows, dim = tokens.shape
    half, width, unused = fq_own.shape
    block = pl.BlockSpec((CHUNK, dim), lambda c: (c, 0))
    natural = kept_in_vmem((rows, dim), LOW)
    turned = streamed((dim, rows), LOW)
    column = pl.BlockSpec((dim, CHUNK), lambda c: (0, c))
    return call(
        prepare_kernel,
        "prepare",
        (rows // CHUNK,),
        [block, block] + [whole(a) for a in (norms, fq_own, fq_oth, fk_own, fk_oth)],
        [STAYS, column, column, STAYS],
        (natural, turned, turned, kept_in_vmem((4, half, 2 * width, 2 * width), LOW)),
        [],
        8,
        5,
        (*apart(tokens, cot), norms, fq_own, fq_oth, fk_own, fk_oth),
    )


def project_kernel(
    kept,
    normed,
    wa_own,
    wb_own,
    wa_oth,
    wb_oth,
    maps,
    aux,
    q_t,
    k_t,
    v_nat,
    v_ext,
    phi_q,
    phi_k,
    phi_k_nat,
    prefix,
    final,
    state,
    projected,
):
    step = pl.program_id(0)
    heads, feat, unused = phi_q.shape
    width = feat // 2
    rows = at(step, CHUNK)
    written = aux[1:2, rows].astype(LOW)
    tail = jnp.where(lax.broadcasted_iota(jnp.int32, (16, CHUNK), 0) == 0, 1.0, 0.0).astype(LOW)

    @pl.when(step == 0)
    def _():
        state[...] = jnp.zeros_like(state)
        now = normed[...]
        part = heads * width // 2
        for side, (wa, wb) in enumerate(((wa_own, wb_own), (wa_oth, wb_oth))):
            projected[side, :, : 2 * part] = nn(now, wa[...]).astype(LOW)
            projected[side, :, 2 * part :] = nn(now, wb[:, :part]).astype(LOW)

    prefix[0] = state[:heads]
    keep = kept[step]
    made = [projected[side, rows, :] for side in range(2)]
    part = made[0].shape[1] // 3
    pairs = part // feat
    for side in range(2):
        values = made[side][:, 2 * part :]
        v_nat[:, side * part : (side + 1) * part] = values
        turned = [
            [made[side][:, kind * part + p * feat : kind * part + (p + 1) * feat].T for p in range(pairs)]
            for kind in range(3)
        ]
        indices = [side * pairs + p for p in range(pairs)]
        logits = [
            [nn(maps[2 * kind + 1, index], piece) for index, piece in zip(indices, turned[kind])]
            for kind in range(2)
        ]
        for p, index in enumerate(indices):
            place = slice(index * feat, (index + 1) * feat)
            q_t[place, :] = turned[0][p]
            k_t[place, :] = turned[1][p]
            state[heads, index : index + 1, :] += jnp.sum(
                values[:, p * feat : (p + 1) * feat].astype(F32), axis=0, keepdims=True
            )
        inside = [slice(one * width, (one + 1) * width) for one in range(2)]
        feats_q = [softmax_pair(piece[lines]) for piece in logits[0] for lines in inside]
        feats_k = [softmax_pair(piece[lines]) for piece in logits[1] for lines in inside]
        extended = [jnp.concatenate([piece[lines], tail], axis=0) for piece in turned[2] for lines in inside]
        more = [nt(value, feat_k * written) for value, feat_k in zip(extended, feats_k)]
        for local in range(2 * pairs):
            head = 2 * side * pairs + local
            phi_q[head, :, rows] = feats_q[local]
            phi_k[head] = feats_k[local]
            phi_k_nat[rows, head * feat : (head + 1) * feat] = feats_k[local].T
            v_ext[head, :, rows] = extended[local]
            state[head] = keep * state[head] + more[local]
    final[...] = state[...]


def project(normed, wa_own, wb_own, wa_oth, wb_oth, maps, aux, kept, heads, width):
    rows, dim = normed.shape
    count = rows // CHUNK
    feat = 2 * width
    return call(
        project_kernel,
        "project",
        (count,),
        [STAYS] + [whole(a) for a in (wa_own, wb_own, wa_oth, wb_oth)] + [STAYS, whole(aux)],
        [
            pl.BlockSpec((heads * width, CHUNK), lambda c, *_: (0, c)),
            pl.BlockSpec((heads * width, CHUNK), lambda c, *_: (0, c)),
            pl.BlockSpec((CHUNK, heads * width), lambda c, *_: (c, 0)),
            STAYS,
            STAYS,
            pl.BlockSpec((heads, feat, CHUNK), lambda c, *_: (0, 0, c)),
            STAYS,
            pl.BlockSpec((1, heads, EXT, feat), lambda c, *_: (c, 0, 0, 0)),
            fixed(heads + 1, EXT, feat),
        ],
        (
            streamed((heads * width, rows), LOW),
            streamed((heads * width, rows), LOW),
            streamed((rows, heads * width), LOW),
            kept_in_vmem((heads, EXT, rows), LOW),
            kept_in_vmem((heads, feat, rows), LOW),
            streamed((heads, feat, rows), LOW),
            kept_in_vmem((rows, heads * feat), LOW),
            streamed((count, heads, EXT, feat), F32),
            streamed((heads + 1, EXT, feat), F32),
        ),
        [pltpu.VMEM((heads + 1, EXT, feat), F32), pltpu.VMEM((2, rows, 3 * heads * width // 2), LOW)],
        24,
        14,
        (kept, *pinned(normed), wa_own, wb_own, wa_oth, wb_oth, *pinned(maps), aux),
        scalars=1,
    )


def center_of(final, entering, pair, rows):
    heads, unused, feat = final.shape
    other = (pair + (heads - 1) // 4) % ((heads - 1) // 2)
    total = final[heads - 1, pair : pair + 1, :] + entering[heads - 1, other : other + 1, :]
    return jnp.broadcast_to(total * (1.0 / rows), (feat, feat))


def attend_kernel(
    carry,
    aux,
    mask,
    phi_q,
    phi_k_nat,
    v_ext,
    prefix,
    final,
    entering,
    att_t,
    att_c,
    denom,
):
    step = pl.program_id(0)
    heads, feat, unused = phi_q.shape
    width = feat // 2
    rows = at(step, CHUNK)
    reach = aux[0:1, rows]
    padding = aux[3:4, rows]
    keep = carry[step]
    mask_now = mask[0]
    half = heads // 2
    centers = [center_of(final, entering, pair, 2 * att_t.shape[1]).T for pair in range(half)]
    for side in range(2):
        group = range(side * half, (side + 1) * half)
        pqs = [phi_q[head, :, rows] for head in group]
        states = [(prefix[0, head] + keep * entering[(head + half) % heads]).astype(LOW) for head in group]
        scores = [
            nn(phi_k_nat[rows, head * feat : (head + 1) * feat], pq) for head, pq in zip(group, pqs)
        ]
        inter = [nn(state, pq) for state, pq in zip(states, pqs)]
        weights = [score.astype(LOW) * mask_now for score in scores]
        numers = [
            nn(v_ext[head, :, rows], weight) + reach * more
            for head, weight, more in zip(group, weights, inter)
        ]
        for head, numer in zip(group, numers):
            below = numer[width : width + 1] + padding
            denom[head : head + 1, rows] = below
            place = slice(head * width, (head + 1) * width)
            att = numer[:width] * (1.0 / below)
            att_t[place, rows] = att.astype(LOW)
            near = centers[head // 2][head % 2 * width : (head % 2 + 1) * width, :]
            att_c[place, :] = (att - jnp.concatenate([near] * (CHUNK // feat), axis=1)).astype(LOW)


def attend(aux, mask, phi_q, phi_k_nat, v_ext, prefix, final, entering, carry):
    heads, feat, rows = phi_q.shape
    width = feat // 2
    turned = kept_in_vmem((heads * width, rows), LOW)
    return call(
        attend_kernel,
        "attend",
        (rows // CHUNK,),
        [whole(aux), pl.BlockSpec((1, CHUNK, CHUNK), lambda c, *_: (c, 0, 0))]
        + [STAYS] * 3
        + [pl.BlockSpec((1, heads, EXT, feat), lambda c, *_: (c, 0, 0, 0))]
        + [whole(final), whole(entering)],
        [STAYS, pl.BlockSpec((heads * width, CHUNK), lambda c, *_: (0, c)), STAYS],
        (turned, streamed((heads * width, rows), LOW), kept_in_vmem((16, rows), F32)),
        [],
        8,
        1,
        (carry, aux, *apart(mask), *pinned(phi_q, phi_k_nat, v_ext), *apart(prefix, final, entering)),
        scalars=1,
    )


def mix_kernel(tokens, norms, w_own, w_oth, att_t, hidden, normed, normed_t):
    step = pl.program_id(0)
    rows = at(step, WIDE)
    att = att_t[:, rows].T
    part = att.shape[1] // 2
    total = tokens[...].astype(F32)
    total = total + nt(att[:, :part], w_own[:, part:]) + nt(att[:, part:], w_oth[:, part:])
    hidden[...] = total
    xhat, unused = norm_parts(total)
    low = (xhat * norms[2:3, :] + norms[3:4, :]).astype(LOW)
    normed[...] = low
    normed_t[...] = low.T


def mix(tokens, norms, w_own, w_oth, att_t):
    rows, dim = tokens.shape
    block = pl.BlockSpec((WIDE, dim), lambda c: (c, 0))
    return call(
        mix_kernel,
        "mix",
        (rows // WIDE,),
        [block, whole(norms), whole(w_own), whole(w_oth), STAYS],
        [block, block, pl.BlockSpec((dim, WIDE), lambda c: (0, c))],
        (
            streamed((rows, dim), F32),
            streamed((rows, dim), LOW),
            streamed((dim, rows), LOW),
        ),
        [],
        12,
        1,
        (*apart(tokens), norms, w_own, w_oth, *pinned(att_t)),
    )


def feed_kernel(first, normed, normed_t, cot, cot_t, fc_in, down_in, *refs):
    feed, grad_normed = refs[:2] if first else refs[2:4]
    d_weights = refs[-1]
    if first:
        for kept, source in zip(refs[2:6], (normed, normed_t, cot, cot_t)):
            kept[...] = source[...]
    fc = fc_in[...]
    down = down_in[...]
    units = fc.shape[1]
    u = nn(normed[...], fc)
    square = u * u
    t = jnp.tanh(u * (GELU_C + (GELU_C * GELU_A) * square))
    half = 0.5 + 0.5 * t
    act = (u * half).astype(LOW)
    slope = half + (0.5 * u) * (1.0 - t * t) * (GELU_C + (3.0 * GELU_C * GELU_A) * square)
    d_weights[:, units:] = nn(cot_t[...], act).astype(LOW)
    grad = (nn(cot[...], down) * slope).astype(LOW)
    d_weights[:, :units] = nn(normed_t[...], grad).astype(LOW)
    if first:
        feed[...] = nt(act, down)
        grad_normed[...] = nt(grad, fc)
    else:
        feed[...] += nt(act, down)
        grad_normed[...] += nt(grad, fc)


def feed_forward(normed, normed_t, cot, cot_t, weights, sums):
    rows, dim = normed.shape
    units = weights[0].shape[1]
    total = kept_in_vmem((rows, dim), F32)
    shared = (normed, normed_t, cot, cot_t)
    copies = tuple(kept_in_vmem(v.shape, LOW) for v in shared) if sums is None else ()
    return call(
        functools.partial(feed_kernel, sums is None),
        "feed",
        (1,),
        ([whole(v) for v in shared] if sums is None else [STAYS] * 4)
        + [STAYS] * 2
        + ([] if sums is None else [STAYS] * 2),
        [STAYS] * (2 + len(copies)) + [fixed(dim, 2 * units)],
        (total, total, *copies, jax.ShapeDtypeStruct((dim, 2 * units), LOW)),
        [],
        26 if sums is None else 18,
        9,
        (
            *(apart(*shared) if sums is None else pinned(*shared)),
            *pinned(*weights),
            *(() if sums is None else pinned(*sums)),
        ),
        alias=None if sums is None else {6: 0, 7: 1},
    )


def middle_kernel(
    hidden,
    feed,
    grad_normed,
    cot,
    norms,
    w_own,
    w_oth,
    att_t,
    att_c,
    denom,
    phi_q,
    aux,
    mixed,
    grad_hidden,
    d_gain,
    d_shift,
    g_ext,
    leaving,
    d_own,
    d_oth,
    branch_t,
    state,
):
    step = pl.program_id(0)
    count = pl.num_programs(0)
    heads, feat, unused = phi_q.shape
    width = feat // 2
    rows = at(step, CHUNK)
    hid = hidden[...]
    mixed[...] = (hid + feed[rows, :]).astype(LOW)
    xhat, rstd = norm_parts(hid)
    grad = grad_normed[rows, :]
    back = cot[rows, :].astype(F32) + norm_back(grad, xhat, rstd, norms[2:3, :])
    grad_hidden[...] = back

    @pl.when(step == 0)
    def _():
        d_gain[...] = jnp.zeros_like(d_gain)
        d_shift[...] = jnp.zeros_like(d_shift)
        state[...] = jnp.zeros_like(state)

    d_gain[...] += jnp.sum(grad * xhat, axis=0, keepdims=True)
    d_shift[...] += jnp.sum(grad, axis=0, keepdims=True)
    low = back.astype(LOW)
    branch_t[:, rows] = low.T
    reach = aux[2:3, rows].astype(LOW)
    first = lax.broadcasted_iota(jnp.int32, (16, CHUNK), 0) == 0
    part = heads * width // 2
    grad_att = [nn(low, weights[:, part:]) for weights in (w_own, w_oth)]
    turned = [
        piece[:, inner * feat : (inner + 1) * feat].T
        for piece in grad_att
        for inner in range(piece.shape[1] // feat)
    ]
    exts = []
    for head in range(heads):
        ga = turned[head // 2][head % 2 * width : (head % 2 + 1) * width]
        inverse = 1.0 / denom[head : head + 1, rows]
        centered = att_c[head * width : (head + 1) * width, :].astype(F32)
        gd = -jnp.sum(ga * centered, axis=0, keepdims=True) * inverse
        exts.append(
            jnp.concatenate([(ga * inverse).astype(LOW), jnp.where(first, gd, 0.0).astype(LOW)], axis=0)
        )
    more = [nt(ext * reach, phi_q[head, :, rows]) for head, ext in enumerate(exts)]
    for head in range(heads):
        g_ext[head, :, rows] = exts[head]
        state[head] += more[head]
    leaving[...] = state[...].astype(LOW)

    @pl.when(step == count - 1)
    def _():
        start = 0
        for out in (d_own, d_oth):
            size = out.shape[1]
            out[...] = nt(branch_t[...], att_t[start : start + size, :]).astype(LOW)
            start += size


def middle(hidden, feed, grad_normed, cot, norms, w_own, w_oth, att_t, att_c, denom, phi_q, aux):
    rows, dim = hidden.shape
    heads, feat, unused = phi_q.shape
    width = feat // 2
    part = heads * width // 2
    block = pl.BlockSpec((CHUNK, dim), lambda c, *_: (c, 0))
    return call(
        middle_kernel,
        "middle",
        (rows // CHUNK,),
        [block]
        + [STAYS] * 3
        + [whole(norms), whole(w_own), whole(w_oth)]
        + [STAYS, pl.BlockSpec((heads * width, CHUNK), lambda c, *_: (0, c)), STAYS, STAYS]
        + [whole(aux)],
        [block, block, fixed(1, dim), fixed(1, dim), STAYS, fixed(heads, EXT, feat)]
        + [fixed(dim, part)] * 2,
        (
            streamed((rows, dim), LOW),
            streamed((rows, dim), F32),
            jax.ShapeDtypeStruct((1, dim), F32),
            jax.ShapeDtypeStruct((1, dim), F32),
            kept_in_vmem((heads, EXT, rows), LOW),
            streamed((heads, EXT, feat), LOW),
        )
        + (jax.ShapeDtypeStruct((dim, part), LOW),) * 2,
        [pltpu.VMEM((dim, rows), LOW), pltpu.VMEM((heads, EXT, feat), F32)],
        20,
        13,
        (
            *apart(hidden),
            *pinned(feed, grad_normed, cot),
            norms,
            w_own,
            w_oth,
            *pinned(att_t),
            *apart(att_c),
            *pinned(denom, phi_q),
            aux,
        ),
    )


def attend_back_kernel(
    side,
    carry,
    kept,
    aux,
    mask,
    phi_q,
    phi_k,
    phi_k_nat,
    v_nat,
    v_ext,
    g_ext,
    prefix,
    final,
    entering,
    arriving,
    q_t,
    k_t,
    maps,
    grads,
    d_maps,
    state,
    d_fq,
    d_fk,
):
    step = pl.program_id(0)
    count = pl.num_programs(0)
    heads, feat, unused = phi_q.shape
    width = feat // 2
    part = heads * width // 2
    half = heads // 2
    chunk = count - 1 - step
    rows = at(chunk, CHUNK)
    keep_in = carry[chunk]
    keep = kept[chunk]
    reach = aux[0:1, rows].astype(LOW)
    written = aux[1:2, rows].astype(LOW)
    mask_now = mask[0]

    @pl.when(step == 0)
    def _():
        for head in range(half):
            state[head] = arriving[(1 - side) * half + head].astype(F32)
        d_fq[...] = jnp.zeros_like(d_fq)
        d_fk[...] = jnp.zeros_like(d_fk)

    locals_ = range(half)
    pairs = range(half // 2)
    centers = [center_of(final, entering, side * half // 2 + p, 2 * phi_q.shape[2]) for p in pairs]
    v_pairs = [
        (v_nat[:, p * feat : (p + 1) * feat].astype(F32) - centers[p][:1]).astype(LOW) for p in pairs
    ]
    columns = [center.T for center in centers]
    nears = [columns[n // 2][n % 2 * width : (n % 2 + 1) * width, :] for n in locals_]
    pqs = [phi_q[side * half + n, :, rows] for n in locals_]
    pks = [phi_k[n] for n in locals_]
    exts = [g_ext[side * half + n, :, rows] for n in locals_]
    scores = [
        nn(phi_k_nat[rows, (side * half + n) * feat : (side * half + n + 1) * feat], pqs[n]) for n in locals_
    ]
    blank = jnp.zeros((width, CHUNK), LOW)
    gws = []
    for n in locals_:
        numer = exts[n][:width]
        padded = jnp.concatenate([numer, blank] if n % 2 == 0 else [blank, numer], axis=0)
        gws.append(nn(v_pairs[n // 2], padded))
    weights = [score.astype(LOW) * mask_now for score in scores]
    gws = [
        (gw + ext[width : width + 1].astype(F32)).astype(LOW) * mask_now for gw, ext in zip(gws, exts)
    ]
    befores, values, afters, reached = [], [], [], []
    for n in locals_:
        before = prefix[0, n] + keep_in * entering[(1 - side) * half + n]
        befores.append(
            jnp.concatenate([before[:width] - nears[n] * before[width : width + 1], before[width:]], axis=0).astype(LOW)
        )
        value = v_ext[side * half + n, :, rows]
        near = jnp.concatenate([nears[n]] * (CHUNK // feat), axis=1)
        value = jnp.concatenate([(value[:width].astype(F32) - near).astype(LOW), value[width:]], axis=0)
        values.append(value * written)
        afters.append(state[n].astype(LOW))
        reached.append(exts[n] * reach)
    g_phi_q = [nn(pks[n], gws[n]) + tn(befores[n], reached[n]) for n in locals_]
    g_phi_k = [nt(pqs[n], gws[n]) + tn(afters[n], values[n]) for n in locals_]
    g_values = [
        nt(exts[n][:width], weights[n]) + nn(afters[n][:width], pks[n] * written) for n in locals_
    ]
    more = [nt(reached[n], pqs[n]) for n in locals_]
    grads_q = [softmax_pair_back(pqs[n], g_phi_q[n]).astype(LOW) for n in locals_]
    grads_k = [softmax_pair_back(pks[n], g_phi_k[n]).astype(LOW) for n in locals_]
    for n in locals_:
        state[n] = keep * state[n] + more[n]
    both = [[jnp.concatenate(g[2 * p : 2 * p + 2], axis=0) for p in pairs] for g in (grads_q, grads_k)]
    through = [[nn(maps[2 * kind, side * half // 2 + p], both[kind][p]) for p in pairs] for kind in range(2)]
    onto = [
        [nt(source[p * feat : (p + 1) * feat, :], both[kind][p]) for p in pairs]
        for kind, source in enumerate((q_t, k_t))
    ]
    for p in pairs:
        for kind in range(2):
            start = kind * part + p * feat
            grads[start : start + feat, rows] = through[kind][p].astype(LOW)
        start = 2 * part + p * feat
        grads[start : start + feat, rows] = jnp.concatenate(g_values[2 * p : 2 * p + 2], axis=0).astype(LOW)
        d_fq[p] += onto[0][p]
        d_fk[p] += onto[1][p]

    @pl.when(step == count - 1)
    def _():
        first = lax.broadcasted_iota(jnp.int32, (width, feat), 1) < width
        for kind, source in enumerate((d_fq, d_fk)):
            for local in range(half // 2):
                block = source[local]
                d_maps[kind, local] = jnp.where(first, block[:width], block[width:])


def attend_back(
    side, aux, mask, phi_q, phi_k, phi_k_nat, v_nat, v_ext, g_ext, prefix, final, entering, arriving, q_t, k_t, maps, carry, kept
):
    heads, feat, rows = phi_q.shape
    width = feat // 2
    half = heads // 2
    count = rows // CHUNK
    lanes = pl.BlockSpec((half * width, CHUNK), lambda c, *_: (side, count - 1 - c))
    return call(
        functools.partial(attend_back_kernel, side),
        "attend_back",
        (rows // CHUNK,),
        [
            whole(aux),
            pl.BlockSpec((1, CHUNK, CHUNK), lambda c, *_: (count - 1 - c, 0, 0)),
            STAYS,
            pl.BlockSpec((half, feat, CHUNK), lambda c, *_: (side, 0, count - 1 - c)),
            STAYS,
            pl.BlockSpec((CHUNK, half * width), lambda c, *_: (count - 1 - c, side)),
            STAYS,
            STAYS,
            pl.BlockSpec((1, half, EXT, feat), lambda c, *_: (count - 1 - c, side, 0, 0)),
            whole(final),
            whole(entering),
            whole(arriving),
            lanes,
            lanes,
            STAYS,
        ],
        [STAYS, fixed(2, half // 2, width, feat)],
        (kept_in_vmem((3 * half * width, rows), LOW), streamed((2, half // 2, width, feat), F32)),
        [pltpu.VMEM((half, EXT, feat), F32)] + [pltpu.VMEM((half // 2, feat, feat), F32)] * 2,
        10,
        14,
        (
            carry,
            kept,
            aux,
            *apart(mask),
            *pinned(phi_q),
            *apart(phi_k),
            *pinned(phi_k_nat),
            *apart(v_nat),
            *pinned(v_ext, g_ext),
            *apart(prefix, final, entering, arriving, q_t, k_t),
            *pinned(maps),
        ),
        scalars=2,
    )


def weight_kernel(normed_t, grads, out):
    out[...] = nt(normed_t[...], grads[...]).astype(LOW)


def weight_grads(normed_t, grads):
    dim, rows = normed_t.shape
    size = grads.shape[0]
    return call(
        weight_kernel,
        "weight_grads",
        (1,),
        [whole(normed_t), STAYS],
        fixed(dim, size),
        jax.ShapeDtypeStruct((dim, size), LOW),
        [],
        8,
        0,
        (*apart(normed_t), *pinned(grads)),
    )


def first_kernel(tokens, norms, grad_hidden, wa_own, wb_own, wa_oth, wb_oth, grads_own, grads_oth, out, d_gain, d_shift):
    step = pl.program_id(0)
    rows = at(step, CHUNK)
    total = None
    for wa, wb, grads in ((wa_own, wb_own, grads_own), (wa_oth, wb_oth, grads_oth)):
        cut = wa.shape[1]
        rest = grads.shape[0] - cut
        term = nn(wa[...], grads[:cut, rows]) + nn(wb[:, :rest], grads[cut:, rows])
        total = term if total is None else total + term
    grad = total.T
    xhat, rstd = norm_parts(tokens[...].astype(F32))
    out[...] = (grad_hidden[...] + norm_back(grad, xhat, rstd, norms[0:1, :])).astype(LOW)

    @pl.when(step == 0)
    def _():
        d_gain[...] = jnp.zeros_like(d_gain)
        d_shift[...] = jnp.zeros_like(d_shift)

    d_gain[...] += jnp.sum(grad * xhat, axis=0, keepdims=True)
    d_shift[...] += jnp.sum(grad, axis=0, keepdims=True)


def first_back(tokens, norms, grad_hidden, weights, grads):
    rows, dim = tokens.shape
    block = pl.BlockSpec((CHUNK, dim), lambda c: (c, 0))
    return call(
        first_kernel,
        "first_back",
        (rows // CHUNK,),
        [block, whole(norms), block] + [whole(w) for w in weights] + [STAYS] * 2,
        [block, fixed(1, dim), fixed(1, dim)],
        (
            streamed((rows, dim), LOW),
            jax.ShapeDtypeStruct((1, dim), F32),
            jax.ShapeDtypeStruct((1, dim), F32),
        ),
        [],
        16,
        9,
        (*apart(tokens), norms, *apart(grad_hidden), *weights, *pinned(*grads)),
    )


SWAP = [(0, 1), (1, 0)]


def swap(piece):
    return lax.ppermute(piece, "mp", SWAP)


def flip(piece, bit, size):
    return lax.ppermute(piece, "dp", [(i, i ^ bit) for i in range(size)])


def turn(piece, by, size):
    return lax.ppermute(piece, "dp", [(i, (i + by) % size) for i in range(size)])


def after(value, *others):
    return lax.optimization_barrier((value, *others))[0]


class Places:
    def __init__(self, size, staged):
        self.size = size
        self.deep = size // 4
        self.staged = staged
        place = lax.axis_index("dp")
        self.spots = jnp.stack([place % 2, (place // 2) % 2, place // 4, lax.axis_index("mp")])

    def flip(self, value, axis):
        return flip(value, 1 if axis == "x" else 2, self.size)


def line_kernel(cut, spots, *refs):
    deep = len(refs) - 2
    for s in range(deep):
        spot = lax.rem(spots[2] + deep - s, deep)
        refs[-2][spot] = refs[s][:, :cut]
        refs[-1][spot] = refs[s][:, cut:]


def gather_line(shard, cut, at, *others):
    return join_line(line_pieces(shard, at), cut, at, *others)


def line_pieces(shard, at):
    return [shard] + [turn(shard, 4 * s, at.size) for s in range(1, at.deep)]


def join_line(pieces, cut, at, *others):
    if others:
        pieces[1] = after(pieces[1], *others)
    rows, columns = pieces[0].shape
    shapes = [(at.deep, rows, cut), (at.deep, rows, columns - cut)]
    return call(
        functools.partial(line_kernel, cut),
        "line",
        (1,),
        [whole(p) for p in pieces],
        [fixed(*shape) for shape in shapes],
        tuple(jax.ShapeDtypeStruct(shape, LOW) for shape in shapes),
        [],
        6,
        0,
        (at.spots, *pieces),
        scalars=1,
    )


def pair_kernel(axes, dims, spots, *refs):
    for index, (axis, dim) in enumerate(zip(axes, dims)):
        mine, theirs, out = refs[2 * index], refs[2 * index + 1], refs[4 + index]
        bit = spots[0 if axis == "x" else 1]
        for source, place in ((mine, bit), (theirs, 1 - bit)):
            if dim == 1:
                out[:, pl.ds(place, 1)] = source[...][:, None]
            else:
                out[:, :, pl.ds(place, 1)] = source[...][:, :, None]


def first_by(shape):
    tail = (0,) * (len(shape) - 1)
    return pl.BlockSpec((1, *shape[1:]), lambda d, *_: (jnp.minimum(d, shape[0] - 1), *tail))


def gather_pair(values, axes, at, *others, kind=jax.ShapeDtypeStruct):
    moved = [at.flip(v, axis) for v, axis in zip(values, axes)]
    if others:
        moved[0] = after(moved[0], *others)
    dims = [v.ndim - 2 if axis == "x" else 1 for v, axis in zip(values, axes)]
    shapes = [(*v.shape[:d], 2, *v.shape[d:]) for v, d in zip(values, dims)]
    return call(
        functools.partial(pair_kernel, axes, dims),
        "pair",
        (at.deep,),
        [first_by(v.shape) for v in values for unused in (0, 1)],
        [first_by(shape) for shape in shapes],
        tuple(kind(shape, LOW) for shape in shapes),
        [],
        8,
        0,
        (at.spots, values[0], moved[0], values[1], moved[1]),
        scalars=1,
    )


def first_fold_kernel(axes, cuts, deep, spots, *refs):
    outs = refs[-4:]
    step = pl.program_id(0)
    if len(refs) == 5 + 2 * len(cuts):
        rider = refs[-5]
        rows = outs[0].shape[2]

        @pl.when(step == deep)
        def _():
            for index in range(rider.shape[0] // rows):
                group, place = divmod(index, 2)
                outs[0][0, place, :, group * 128 : (group + 1) * 128] = rider[index * rows : (index + 1) * rows, :]

        @pl.when(step < deep)
        def _():
            first_fold_step(axes, cuts, spots, refs, outs)

    else:
        first_fold_step(axes, cuts, spots, refs, outs)


def first_fold_step(axes, cuts, spots, refs, outs):
    for index, axis in enumerate(axes):
        bit = spots[0 if axis == "x" else 1]
        sent, kept = outs[2 * index : 2 * index + 2]
        start = 0
        for segment, cut in enumerate(cuts):
            pair = refs[2 * segment : 2 * segment + 2]
            columns = slice(0, cut) if index == 0 else slice(cut, pair[0].shape[-1])
            size = columns.stop - columns.start
            for out, place in ((sent, 1 - bit), (kept, bit)):
                if axis == "x":
                    terms = [r[:, :, pl.ds(place, 1), :, columns].astype(F32) for r in pair]
                else:
                    terms = [r[:, pl.ds(place, 1), :, :, columns].astype(F32) for r in pair]
                total = (terms[0] + terms[1]).astype(LOW)
                out[..., start : start + size] = total.reshape(*out.shape[:-1], size)
            start += size


def fold_kernel(axes, spots, *refs):
    for index, axis in enumerate(axes):
        bit = spots[0 if axis == "x" else 1]
        sent, kept = refs[4 + 2 * index : 6 + 2 * index]
        for out, place in ((sent, 1 - bit), (kept, bit)):
            terms = [r[:, pl.ds(place, 1)].astype(F32) for r in refs[2 * index : 2 * index + 2]]
            out[...] = (terms[0] + terms[1]).astype(LOW).reshape(out.shape)


def spread_kernel(spots, a_kept, a_sent, b_kept, b_sent, *outs):
    deep = len(outs)
    cut = a_kept.shape[-1]
    for s, out in enumerate(outs):
        spot = lax.rem(spots[2] + s, deep)
        out[:, :cut] = (a_kept[spot].astype(F32) + a_sent[spot].astype(F32)).astype(LOW)
        out[:, cut:] = (b_kept[spot].astype(F32) + b_sent[spot].astype(F32)).astype(LOW)


class Scatter:
    def __init__(self, segments, at):
        self.at = at
        self.cuts = [cut for own, oth, cut in segments]
        self.cut = sum(self.cuts)
        self.terms = [[own, swap(oth)] for own, oth, cut in segments]
        if at.staged:
            split = lambda v: v.reshape(at.deep, 2, 2, v.shape[0] // at.size, v.shape[1])
            self.terms = [[split(v) for v in pair] for pair in self.terms]

    def wait_for(self, *others):
        self.terms[0][1] = after(self.terms[0][1], *others)

    def fold(self, axes, rider=None):
        at = self.at
        flats = [v for pair in self.terms for v in pair]
        if not at.staged:
            return flats[0]
        if self.cuts:
            columns = sum(pair[0].shape[-1] for pair in self.terms)
            head = flats[0].shape[:2]
            rows = flats[0].shape[3]
            lefts = [(*head, rows, self.cut), (*head, rows, columns - self.cut)]
            kernel = functools.partial(first_fold_kernel, axes, tuple(self.cuts), at.deep)
        else:
            lefts = [(v.shape[0], *v.shape[2:]) for v in flats[::2]]
            kernel = functools.partial(fold_kernel, axes)
        outs = [left for left in lefts for unused in (0, 1)]
        extra = []
        steps = at.deep
        if rider is not None:
            extra = [rider]
            steps += 1
            outs[0] = (steps, *outs[0][1:])
        a_sent, a_kept, b_sent, b_kept = call(
            kernel,
            "fold",
            (steps,),
            [first_by(v.shape) for v in flats] + [whole(v) for v in extra],
            [first_by(left) for left in outs],
            tuple(jax.ShapeDtypeStruct(left, LOW) for left in outs),
            [],
            12,
            0,
            (at.spots, *flats, *extra),
            scalars=1,
        )
        self.cuts = []
        self.terms = [[a_kept, at.flip(a_sent, axes[0])], [b_kept, at.flip(b_sent, axes[1])]]
        return a_kept

    def spread(self):
        at = self.at
        if not at.staged:
            return self.terms[0][0]
        a, b = self.terms
        shape = (a[0].shape[1], self.cut + b[0].shape[-1])
        own, *sends = call(
            spread_kernel,
            "spread",
            (1,),
            [whole(v) for v in (*a, *b)],
            [fixed(*shape)] * at.deep,
            (jax.ShapeDtypeStruct(shape, LOW),) * at.deep,
            [],
            8,
            0,
            (at.spots, *a, *b),
            scalars=1,
        )
        self.parts = [own] + [turn(p, 4 * s, at.size) for s, p in enumerate(sends, 1)]
        return own

    def end(self, *others):
        if not self.at.staged:
            sums = [own.astype(F32) + moved.astype(F32) for own, moved in self.terms]
            total = [t[:, :cut] for t, cut in zip(sums, self.cuts)] + [t[:, cut:] for t, cut in zip(sums, self.cuts)]
            total = lax.psum_scatter(jnp.concatenate(total, axis=1), "dp", scatter_dimension=0, tiled=True)
        else:
            if others:
                self.parts[1] = after(self.parts[1], *others)
            total = sum(p.astype(F32) for p in self.parts)
        return total


def ride_kernel(deep, spots, *refs):
    a_kept, a_moved, b_kept, b_moved, gain1, shift1, gain2, shift2, maps, early = refs[:10]
    late = refs[10 : 10 + deep]
    a_sent, a_left, b_sent, b_left, norm_low, maps_low, g_fc, g_down, g_out = refs[10 + deep :]
    rows = a_left.shape[1]
    units = early.shape[1] // 2
    total = late[0][...].astype(F32)
    for part in late[1:]:
        total = total + part[...].astype(F32)
    rest = total.shape[1] - 2 * units
    cut = units + (rest // 128 + 1) // 2 * 128
    g_fc[:, :units] = early[:, :units]
    g_down[:, :units] = early[:, units:]
    g_fc[:, units:] = total[:, :units]
    g_down[:, units:] = total[:, cut : cut + units]
    g_out[:, : cut - units] = total[:, units:cut]
    g_out[:, cut - units :] = total[:, cut + units :]
    blank = jnp.zeros((4, gain1.shape[1]), F32)
    norm_now = jnp.concatenate([gain1[...], shift1[...], gain2[...], shift2[...], blank], axis=0)
    norm_low[...] = jnp.concatenate([norm_now, jnp.zeros_like(norm_now)], axis=0).astype(LOW)
    for index in range(maps.shape[0] // rows):
        group, place = divmod(index, 2)
        moved = a_moved[deep, place, :, group * 128 : (group + 1) * 128].astype(F32)
        here = slice(index * rows, (index + 1) * rows)
        maps_low[here, :] = (maps[here, :].astype(F32) + moved).astype(LOW)
    for kept, moved, sent, left, bit in (
        (a_kept, a_moved, a_sent, a_left, spots[1]),
        (b_kept, b_moved, b_sent, b_left, spots[0]),
    ):
        columns = left.shape[2]
        for out, place in ((sent, 1 - bit), (left, bit)):
            terms = [r[:deep, pl.ds(place, 1)].astype(F32) for r in (kept, moved)]
            total = (terms[0] + terms[1]).astype(LOW)
            if out is left:
                out[...] = total.reshape(deep, rows, columns)
            else:
                out[: deep * rows] = total.reshape(deep * rows, columns)
        rest = norm_now[:, columns:]
        rest = jnp.concatenate([rest, jnp.zeros((8, columns - rest.shape[1]), F32)], axis=1)
        sent[deep * rows :] = jnp.concatenate([norm_now[:, :columns], rest], axis=0).astype(LOW)


def last_spread_kernel(spots, a_kept, a_moved, b_kept, b_moved, norm, norm_far, maps, maps_moved, *outs):
    *parts, maps_low = outs
    deep, rows, cut = a_kept.shape
    dim = norm.shape[1]
    maps_low[...] = (maps[...].astype(F32) + maps_moved[...].astype(F32)).astype(LOW)
    near = []
    for moved in (b_moved, a_moved):
        columns = moved.shape[1]
        tail = moved[deep * rows :].astype(F32)
        near.append(jnp.concatenate([tail[:8], tail[8:, : dim - columns]], axis=1))
    plane = (norm[...].astype(F32)[:8] + near[0]) + (near[1] + norm_far[...].astype(F32)[:8])
    tail = jnp.concatenate([plane[:, i : i + 128] for i in range(0, dim, 128)], axis=0)
    for s, out in enumerate(parts):
        spot = lax.rem(spots[2] + s, deep)
        place = pl.ds(pl.multiple_of(spot * rows, rows), rows)
        rest = out.shape[1] - 128
        out[:, :cut] = (a_kept[spot].astype(F32) + a_moved[place].astype(F32)).astype(LOW)
        out[:, cut:rest] = (b_kept[spot].astype(F32) + b_moved[place].astype(F32)).astype(LOW)
        out[:, rest:] = tail.astype(LOW)


def finish_kernel(spots, *refs):
    deep = len(refs) - 9
    parts = refs[:deep]
    maps, maps_moved, g_query, g_key, g_value, norms, map_q, map_k, held = refs[deep:]
    rows, part = g_query.shape
    total = None
    for s, ref in enumerate(parts):
        value = ref[...].astype(F32)
        held[lax.rem(spots[2] + deep - s, deep)] = value[:, 3 * part :]
        total = value if total is None else total + value
    for index, out in enumerate((g_query, g_key, g_value)):
        out[...] = total[:, index * part : (index + 1) * part]
    together = held[0]
    for spot in range(1, deep):
        together = together + held[spot]
    for index in range(rows // 8):
        norms[:, index * 128 : (index + 1) * 128] = together[index * 8 : (index + 1) * 8]
    width = map_q.shape[1]
    both = maps[...].astype(F32) + maps_moved[...].astype(F32)
    heads = map_q.shape[0]
    for kind, out in enumerate((map_q, map_k)):
        for pair in range(heads // 2):
            start = (kind * heads // 2 + pair) * width
            block = both[start : start + width]
            out[2 * pair] = block[:, :width]
            out[2 * pair + 1] = block[:, width:]


def finish_last(sums, norm, map_grads, early, late, part, heads, width, at):
    small = lambda shape, kind: jax.ShapeDtypeStruct(shape, kind)
    (a_kept, a_moved), (b_kept, b_moved) = sums.terms
    deep, unused, rows, cut = a_kept.shape
    rest = b_kept.shape[3]
    dim = norm[0].shape[1]
    units = early.shape[1]
    ins = (a_kept, a_moved, b_kept, b_moved, *norm, map_grads, early, *late)
    outs = (
        small((deep * rows + 16, cut), LOW),
        small((deep, rows, cut), LOW),
        small((deep * rows + 16, rest), LOW),
        small((deep, rows, rest), LOW),
        small((16, dim), LOW),
        small(map_grads.shape, LOW),
        small((rows, units), F32),
        small((rows, units), F32),
        small((rows, part), F32),
    )

    def run(kernel, name, ins, outs, scratch):
        return call(
            kernel,
            name,
            (1,),
            [whole(v) for v in ins],
            [fixed(*out.shape) for out in outs],
            outs,
            scratch,
            12,
            0,
            (at.spots, *ins),
            scalars=1,
        )

    kernel = functools.partial(ride_kernel, deep)
    a_sent, a_kept, b_sent, b_kept, norm_low, maps, *done = run(kernel, "ride", ins, outs, [])
    across = [(i, i ^ 3) for i in range(at.size)]
    ins = (
        a_kept,
        at.flip(a_sent, "y"),
        b_kept,
        at.flip(b_sent, "x"),
        norm_low,
        lax.ppermute(norm_low, "dp", across),
        maps,
        flip(maps, 4 << (at.size.bit_length() - 4), at.size),
    )
    ins = lax.optimization_barrier(ins)
    outs = (small((rows, cut + rest + 128), LOW),) * deep + (small(map_grads.shape, LOW),)
    own, *sends, maps = run(last_spread_kernel, "last_spread", ins, outs, [])
    ins = (own, *(turn(p, 4 * s, at.size) for s, p in enumerate(sends, 1)), maps, at.flip(maps, "y"))
    ins = lax.optimization_barrier(ins)
    outs = (
        (small((rows, part), F32),) * 3
        + (small((8, dim), F32),)
        + (small((heads // 2, width, width), F32),) * 2
    )
    return done, run(finish_kernel, "finish", ins, outs, [pltpu.VMEM((deep, rows, 128), F32)])


def add_along(value, steps, size):
    for step in steps:
        if step < size:
            value = value.astype(LOW)
            value = value.astype(F32) + flip(value, step, size).astype(F32)
    return value


def per_device(
    size,
    tokens,
    norm1_gain,
    norm1_shift,
    w_query,
    w_key,
    w_value,
    w_out,
    fmap_query,
    fmap_key,
    norm2_gain,
    norm2_shift,
    w_fc,
    w_down,
    lengths,
    cotangent,
):
    rows, dim = tokens.shape
    heads = 2 * fmap_query.shape[0]
    width = fmap_query.shape[1]
    feat = 2 * width
    part = w_query.shape[1]
    count = rows // CHUNK
    core = lax.axis_index("mp")
    staged = size % 4 == 0 and dim // size % 16 == 0
    where = Places(size, staged)
    units = w_fc.shape[1] // 2
    cut = (3 * part // feat + 1) // 2 * feat
    cut_out = (part // feat + 1) // 2 * feat
    shard_qkv, shard_early, shard_late = pack(
        (w_query, w_key, w_value, w_out, w_fc, w_down),
        (
            ((0, 0, part), (1, 0, part), (2, 0, part), (3, 0, part)),
            ((4, 0, units), (5, 0, units)),
            ((4, units, units), (5, units, units)),
        ),
    )
    fq_oth, fk_oth = swap(fmap_query), swap(fmap_key)
    if staged:
        qkv = gather_line(shard_qkv, 2 * part, where)
        lengths = after(lengths, qkv[0])

    ends = jnp.cumsum(lengths[0])
    places = core * rows - 1 + jnp.arange(rows + 1, dtype=jnp.int32)
    numbers = jnp.sum((ends[None, :] <= places[:, None]).astype(jnp.int32), axis=1)
    numbers = jnp.where(places < 0, -1, numbers)
    segment = numbers[1:]
    living = places[1:] < ends[-1]
    blocks = segment.reshape(count, CHUNK)
    last = blocks[:, -1]
    before = jnp.concatenate([numbers[:1], last[:-1]])
    kept = (last == before).astype(F32)
    carry = ((before == numbers[0]) & (core > 0)).astype(F32)
    reach = (blocks == before[:, None]).reshape(rows) & living
    written = (blocks == last[:, None]).reshape(rows)
    reach_in = (segment == numbers[0]) & living
    aux = jnp.stack([reach, written, reach_in, ~living] + [jnp.zeros_like(living)] * 4).astype(F32)
    order = jnp.arange(CHUNK, dtype=jnp.int32)
    mask = (
        (blocks[:, :, None] == blocks[:, None, :])
        & (order[:, None] <= order[None, :])
        & living.reshape(count, 1, CHUNK)
    ).astype(LOW)

    norms = jnp.stack([norm1_gain, norm1_shift, norm2_gain, norm2_shift])

    norms, aux, mask, kept, carry = lax.optimization_barrier((norms, aux, mask, kept, carry))
    if staged:
        qkv = gather_pair(qkv, "xy", where)
        shard_early, tokens = after(shard_early, qkv[0]), after(tokens, qkv[0], mask)
    normed1, normed1_t, cot_t, maps = prepare(
        tokens, cotangent, norms, fmap_query, fq_oth, fmap_key, fk_oth
    )
    if staged:
        pieces = line_pieces(shard_early, where)
        pieces[1], maps = lax.optimization_barrier((pieces[1], maps))
        qkv = gather_pair(qkv, "yx", where, *pieces[1:], maps)
        early = join_line(pieces, units, where, qkv[0])
        qkv = tuple(map(flat, qkv))
        normed1, shard_late = after(normed1, early[0]), after(shard_late, early[0])
    else:
        qkv, early, late = (
            tuple(lax.all_gather(s, "dp", axis=0, tiled=True) for s in (shard[:, :at_], shard[:, at_:]))
            for shard, at_ in ((shard_qkv, 2 * part), (shard_early, units), (shard_late, units))
        )
    qkv = (*qkv, *map(swap, qkv))
    q_t, k_t, v_nat, v_ext, phi_q, phi_k, phi_k_nat, prefix, final = project(
        normed1, *qkv, maps, aux, kept, heads, width
    )
    if staged:
        early = gather_pair(early, "xy", where, final)
        final = after(final, early[0])
    entering = swap(final)
    att_t, att_c, denom = attend(aux, mask, phi_q, phi_k_nat, v_ext, prefix, final, entering, carry)
    if staged:
        late = gather_line(shard_late, units, where, denom)
        att_t = after(att_t, late[0])
    hidden, normed2, normed2_t = mix(tokens, norms, qkv[1], qkv[3], att_t)
    if staged:
        early = tuple(map(flat, gather_pair(early, "yx", where, normed2_t)))
    early_oth = tuple(map(swap, early))
    feed, grad_normed, *shared, d_early_oth = feed_forward(normed2, normed2_t, cotangent, cot_t, early_oth, None)
    cot = shared[2]
    if staged:
        late = gather_pair(late, "xy", where, d_early_oth)
        feed = after(feed, late[0])
    feed, grad_normed, d_early_own = feed_forward(*shared, early, (feed, grad_normed))
    sums_early = Scatter([(d_early_own, d_early_oth, units)], where)
    if staged:
        late = tuple(map(flat, gather_pair(late, "yx", where, d_early_own)))
    late_oth = tuple(map(swap, late))
    feed = after(feed, sums_early.fold("xy"))
    feed, grad_normed, d_late_own = feed_forward(*shared, late, (feed, grad_normed))
    feed, grad_normed, d_late_oth = feed_forward(*shared, late_oth, (feed, grad_normed))
    sums_early.wait_for(d_late_oth)
    hidden = after(hidden, sums_early.fold("yx"))
    mixed, grad_hidden, d_gain2, d_shift2, g_ext, leaving, d_out_own, d_out_oth = middle(
        hidden, feed, grad_normed, cot, norms, qkv[1], qkv[3], att_t, att_c, denom, phi_q, aux
    )
    sums_early.wait_for(d_gain2)
    started = sums_early.spread()
    arriving = lax.ppermute(after(leaving, started), "mp", [(1, 0)])
    d_out_oth = after(d_out_oth, started)
    sums_late = Scatter([(d_late_own, d_late_oth, units), (d_out_own, d_out_oth, cut_out)], where)
    sums_late.wait_for(started)
    arriving = after(arriving, sums_late.fold("xy"))
    back = functools.partial(
        attend_back, carry=carry, kept=kept, prefix=prefix, final=final, entering=entering, q_t=q_t, k_t=k_t, maps=maps
    )
    back_inputs = (aux, mask, phi_q, phi_k, phi_k_nat, v_nat, v_ext, g_ext)
    lanes = lambda v: v.reshape(-1, feat)
    grads_oth, maps_oth = back(1, *back_inputs, arriving=arriving)
    total_early = sums_early.end(maps_oth)
    d_qkv_oth = weight_grads(normed1_t, after(grads_oth, total_early))
    sums_late.wait_for(d_qkv_oth)
    arriving = after(arriving, sums_late.fold("yx"))
    grads_own, maps_own = back(0, *back_inputs, arriving=arriving)
    sums_late.wait_for(maps_own)
    grads_own = after(grads_own, sums_late.spread())
    map_grads = lanes(maps_own + swap(maps_oth))
    d_qkv_own = weight_grads(normed1_t, grads_own)
    if staged:
        map_grads = map_grads.astype(LOW)
        for step in [4 << i for i in range(size.bit_length() - 4)]:
            moved = after(flip(map_grads, step, size), d_qkv_own)
            map_grads = (map_grads.astype(F32) + moved.astype(F32)).astype(LOW)
    sums_qkv = Scatter([(d_qkv_own, d_qkv_oth, cut)], where)
    grad_hidden = after(grad_hidden, sums_qkv.fold("xy", map_grads if staged else None))
    grad_tokens, d_gain1, d_shift1 = first_back(tokens, norms, grad_hidden, qkv, (grads_own, grads_oth))
    norm_grads = (d_gain1, d_shift1, d_gain2, d_shift2)
    if staged:
        sums_qkv.wait_for(d_gain1)
        done, (g_query, g_key, g_value, norm_grads, map_q, map_k) = finish_last(
            sums_qkv, norm_grads, map_grads, total_early, sums_late.parts, part, heads, width, where
        )
        g_fc, g_down, g_out = done
    else:
        total_late = sums_late.end()
        grad_qkv = sums_qkv.end()
        g_query, g_key, g_value = (grad_qkv[:, i * part : (i + 1) * part] for i in range(3))
        norm_grads, map_grads = lax.psum((jnp.concatenate(norm_grads, axis=0), map_grads), "dp")
        map_grads = map_grads.reshape(2, heads // 4, width, 2, width)
        map_q, map_k = map_grads.swapaxes(2, 3).reshape(2, heads // 2, width, width)
        cut_late = units + cut_out
        g_fc = jnp.concatenate([total_early[:, :units], total_late[:, :units]], axis=1)
        g_down = jnp.concatenate([total_early[:, units:], total_late[:, cut_late : cut_late + units]], axis=1)
        g_out = jnp.concatenate([total_late[:, units:cut_late], total_late[:, cut_late + units :]], axis=1)
    norm_grads = norm_grads + swap(norm_grads)
    return (
        mixed,
        grad_tokens,
        norm_grads[0],
        norm_grads[1],
        g_query,
        g_key,
        g_value,
        g_out,
        map_q,
        map_k,
        norm_grads[2],
        norm_grads[3],
        g_fc,
        g_down,
    )


def solution(mesh):
    placed = (
        P(("dp", "mp"), None),
        P(),
        P(),
        P("dp", "mp"),
        P("dp", "mp"),
        P("dp", "mp"),
        P("dp", "mp"),
        P("mp", None, None),
        P("mp", None, None),
        P(),
        P(),
        P("dp", "mp"),
        P("dp", "mp"),
        P("dp", None),
        P(("dp", "mp"), None),
    )
    return jax.shard_map(
        functools.partial(per_device, mesh.shape["dp"]),
        mesh=mesh,
        in_specs=placed,
        out_specs=(
            P(("dp", "mp"), None),
            P(("dp", "mp"), None),
            P(),
            P(),
            P("dp", "mp"),
            P("dp", "mp"),
            P("dp", "mp"),
            P("dp", "mp"),
            P("mp", None, None),
            P("mp", None, None),
            P(),
            P(),
            P("dp", "mp"),
            P("dp", "mp"),
        ),
        check_vma=False,
    )
```

```python
import functools

import jax
import jax.numpy as jnp
from jax import lax
from jax.experimental import pallas as pl
from jax.experimental.pallas import tpu as pltpu
from jax.sharding import PartitionSpec as P

EPS = 1e-05
CHUNK = 256
WIDE = 512
EXT = 80
LOW = jnp.bfloat16
F32 = jnp.float32
MIB = 1024 * 1024
PACE = 3_000_000_000
GELU_C = 0.7978845608028654
GELU_A = 0.044715


def nn(a, b):
    return lax.dot_general(a, b, (((1,), (0,)), ((), ())), preferred_element_type=F32)


def nt(a, b):
    return lax.dot_general(a, b, (((1,), (1,)), ((), ())), preferred_element_type=F32)


def tn(a, b):
    return lax.dot_general(a, b, (((0,), (0,)), ((), ())), preferred_element_type=F32)


def norm_parts(rows):
    center = rows - jnp.mean(rows, axis=-1, keepdims=True)
    spread = jnp.mean(center * center, axis=-1, keepdims=True)
    rstd = lax.rsqrt(spread + EPS)
    return center * rstd, rstd


def norm_back(grad, xhat, rstd, gain):
    e = grad * gain
    return rstd * (
        e - jnp.mean(e, axis=-1, keepdims=True) - xhat * jnp.mean(e * xhat, axis=-1, keepdims=True)
    )


def softmax_pair(logits):
    high = jnp.max(logits, axis=0, keepdims=True)
    least = jnp.min(logits, axis=0, keepdims=True)
    pos = jnp.exp(logits - high)
    neg = jnp.exp(least - logits)
    pos = pos * (1.0 / jnp.sum(pos, axis=0, keepdims=True))
    neg = neg * (1.0 / jnp.sum(neg, axis=0, keepdims=True))
    return jnp.concatenate([pos, neg], axis=0).astype(LOW)


def softmax_pair_back(phi, grad):
    width = phi.shape[0] // 2
    pos = phi[:width].astype(F32)
    neg = phi[width:].astype(F32)
    gp = grad[:width]
    gn = grad[width:]
    gp = gp - jnp.sum(pos * gp, axis=0, keepdims=True)
    gn = gn - jnp.sum(neg * gn, axis=0, keepdims=True)
    return pos * gp - neg * gn


def flat(value):
    return value.reshape(-1, value.shape[-1])


def kept_in_vmem(shape, dtype):
    return pltpu.VMEM(shape, dtype)


def streamed(shape, dtype):
    return pltpu.HBM(shape, dtype)


def apart(*arrays):
    return tuple(pltpu.with_memory_space_constraint(a, pltpu.HBM) for a in arrays)


def pinned(*arrays):
    return tuple(pltpu.with_memory_space_constraint(a, pltpu.VMEM) for a in arrays)


def whole(array):
    return pl.BlockSpec(
        array.shape, lambda *_: (0,) * array.ndim, pipeline_mode=pl.Buffered(1)
    )


def fixed(*shape):
    return pl.BlockSpec(shape, lambda *_: (0,) * len(shape))


STAYS = pl.BlockSpec(memory_space=pltpu.VMEM)


def at(step, size):
    return pl.ds(pl.multiple_of(step * size, size), size)


def call(kernel, name, grid, in_specs, out_specs, out_shape, scratch, limit, micros, args, scalars=0, alias=None):
    return pl.pallas_call(
        kernel,
        grid_spec=pltpu.PrefetchScalarGridSpec(
            num_scalar_prefetch=scalars,
            grid=grid,
            in_specs=in_specs,
            out_specs=out_specs,
            scratch_shapes=scratch,
        ),
        out_shape=out_shape,
        input_output_aliases=alias or {},
        compiler_params=pltpu.CompilerParams(vmem_limit_bytes=limit * MIB),
        cost_estimate=pl.CostEstimate(flops=micros * PACE, bytes_accessed=1024, transcendentals=0),
        name=name,
    )(*args)


def pack_kernel(groups, *refs):
    outs = refs[len(refs) - len(groups) :]
    for out, group in zip(outs, groups):
        start = 0
        for index, first, size in group:
            out[:, start : start + size] = refs[index][:, first : first + size]
            start += size


def pack(arrays, groups):
    rows = arrays[0].shape[0]
    shapes = [(rows, sum(size for unused, first, size in group)) for group in groups]
    return call(
        functools.partial(pack_kernel, groups),
        "pack",
        (1,),
        [whole(a) for a in arrays],
        [fixed(*shape) for shape in shapes],
        tuple(jax.ShapeDtypeStruct(shape, LOW) for shape in shapes),
        [],
        8,
        1,
        apart(*arrays),
    )


def prepare_kernel(
    tokens, cot, norms, fq_own, fq_oth, fk_own, fk_oth, normed, normed_t, cot_t, maps
):
    step = pl.program_id(0)
    rows = at(step, CHUNK)
    xhat, unused = norm_parts(tokens[...].astype(F32))
    low = (xhat * norms[0:1, :] + norms[1:2, :]).astype(LOW)
    normed[rows, :] = low
    normed_t[...] = low.T
    cot_t[...] = cot[...].T

    @pl.when(step == 0)
    def _():
        half, width, unused = fq_own.shape
        blank = jnp.zeros((width, width), F32)
        for kind, (own, oth) in enumerate(((fq_own, fq_oth), (fk_own, fk_oth))):
            for pair in range(half):
                source = own if pair < half // 2 else oth
                first = 2 * pair % half
                block = jnp.concatenate(
                    [
                        jnp.concatenate([source[first].astype(F32), blank], axis=1),
                        jnp.concatenate([blank, source[first + 1].astype(F32)], axis=1),
                    ],
                    axis=0,
                )
                maps[2 * kind, pair] = block.astype(LOW)
                maps[2 * kind + 1, pair] = block.T.astype(LOW)


def prepare(tokens, cot, norms, fq_own, fq_oth, fk_own, fk_oth):
    rows, dim = tokens.shape
    half, width, unused = fq_own.shape
    block = pl.BlockSpec((CHUNK, dim), lambda c: (c, 0))
    natural = kept_in_vmem((rows, dim), LOW)
    turned = streamed((dim, rows), LOW)
    column = pl.BlockSpec((dim, CHUNK), lambda c: (0, c))
    return call(
        prepare_kernel,
        "prepare",
        (rows // CHUNK,),
        [block, block] + [whole(a) for a in (norms, fq_own, fq_oth, fk_own, fk_oth)],
        [STAYS, column, column, STAYS],
        (natural, turned, turned, kept_in_vmem((4, half, 2 * width, 2 * width), LOW)),
        [],
        8,
        5,
        (*apart(tokens, cot), norms, fq_own, fq_oth, fk_own, fk_oth),
    )


def project_kernel(
    kept,
    normed,
    wa_own,
    wb_own,
    wa_oth,
    wb_oth,
    maps,
    aux,
    q_t,
    k_t,
    v_nat,
    v_ext,
    phi_q,
    phi_k,
    phi_k_nat,
    prefix,
    final,
    state,
    projected,
):
    step = pl.program_id(0)
    heads, feat, unused = phi_q.shape
    width = feat // 2
    rows = at(step, CHUNK)
    written = aux[1:2, rows].astype(LOW)
    tail = jnp.where(lax.broadcasted_iota(jnp.int32, (16, CHUNK), 0) == 0, 1.0, 0.0).astype(LOW)

    @pl.when(step == 0)
    def _():
        state[...] = jnp.zeros_like(state)
        now = normed[...]
        part = heads * width // 2
        for side, (wa, wb) in enumerate(((wa_own, wb_own), (wa_oth, wb_oth))):
            projected[side, :, : 2 * part] = nn(now, wa[...]).astype(LOW)
            projected[side, :, 2 * part :] = nn(now, wb[:, :part]).astype(LOW)

    prefix[0] = state[:heads]
    keep = kept[step]
    made = [projected[side, rows, :] for side in range(2)]
    part = made[0].shape[1] // 3
    pairs = part // feat
    for side in range(2):
        values = made[side][:, 2 * part :]
        v_nat[:, side * part : (side + 1) * part] = values
        turned = [
            [made[side][:, kind * part + p * feat : kind * part + (p + 1) * feat].T for p in range(pairs)]
            for kind in range(3)
        ]
        indices = [side * pairs + p for p in range(pairs)]
        logits = [
            [nn(maps[2 * kind + 1, index], piece) for index, piece in zip(indices, turned[kind])]
            for kind in range(2)
        ]
        for p, index in enumerate(indices):
            place = slice(index * feat, (index + 1) * feat)
            q_t[place, :] = turned[0][p]
            k_t[place, :] = turned[1][p]
            state[heads, index : index + 1, :] += jnp.sum(
                values[:, p * feat : (p + 1) * feat].astype(F32), axis=0, keepdims=True
            )
        inside = [slice(one * width, (one + 1) * width) for one in range(2)]
        feats_q = [softmax_pair(piece[lines]) for piece in logits[0] for lines in inside]
        feats_k = [softmax_pair(piece[lines]) for piece in logits[1] for lines in inside]
        extended = [jnp.concatenate([piece[lines], tail], axis=0) for piece in turned[2] for lines in inside]
        more = [nt(value, feat_k * written) for value, feat_k in zip(extended, feats_k)]
        for local in range(2 * pairs):
            head = 2 * side * pairs + local
            phi_q[head, :, rows] = feats_q[local]
            phi_k[head] = feats_k[local]
            phi_k_nat[rows, head * feat : (head + 1) * feat] = feats_k[local].T
            v_ext[head, :, rows] = extended[local]
            state[head] = keep * state[head] + more[local]
    final[...] = state[...]


def project(normed, wa_own, wb_own, wa_oth, wb_oth, maps, aux, kept, heads, width):
    rows, dim = normed.shape
    count = rows // CHUNK
    feat = 2 * width
    return call(
        project_kernel,
        "project",
        (count,),
        [STAYS] + [whole(a) for a in (wa_own, wb_own, wa_oth, wb_oth)] + [STAYS, whole(aux)],
        [
            pl.BlockSpec((heads * width, CHUNK), lambda c, *_: (0, c)),
            pl.BlockSpec((heads * width, CHUNK), lambda c, *_: (0, c)),
            pl.BlockSpec((CHUNK, heads * width), lambda c, *_: (c, 0)),
            STAYS,
            STAYS,
            pl.BlockSpec((heads, feat, CHUNK), lambda c, *_: (0, 0, c)),
            STAYS,
            pl.BlockSpec((1, heads, EXT, feat), lambda c, *_: (c, 0, 0, 0)),
            fixed(heads + 1, EXT, feat),
        ],
        (
            streamed((heads * width, rows), LOW),
            streamed((heads * width, rows), LOW),
            streamed((rows, heads * width), LOW),
            kept_in_vmem((heads, EXT, rows), LOW),
            kept_in_vmem((heads, feat, rows), LOW),
            streamed((heads, feat, rows), LOW),
            kept_in_vmem((rows, heads * feat), LOW),
            streamed((count, heads, EXT, feat), F32),
            streamed((heads + 1, EXT, feat), F32),
        ),
        [pltpu.VMEM((heads + 1, EXT, feat), F32), pltpu.VMEM((2, rows, 3 * heads * width // 2), LOW)],
        24,
        14,
        (kept, *pinned(normed), wa_own, wb_own, wa_oth, wb_oth, *pinned(maps), aux),
        scalars=1,
    )


def center_of(final, entering, pair, rows):
    heads, unused, feat = final.shape
    other = (pair + (heads - 1) // 4) % ((heads - 1) // 2)
    total = final[heads - 1, pair : pair + 1, :] + entering[heads - 1, other : other + 1, :]
    return jnp.broadcast_to(total * (1.0 / rows), (feat, feat))


def attend_kernel(
    carry,
    aux,
    mask,
    phi_q,
    phi_k_nat,
    v_ext,
    prefix,
    final,
    entering,
    att_t,
    att_c,
    denom,
):
    step = pl.program_id(0)
    heads, feat, unused = phi_q.shape
    width = feat // 2
    rows = at(step, CHUNK)
    reach = aux[0:1, rows]
    padding = aux[3:4, rows]
    keep = carry[step]
    mask_now = mask[0]
    half = heads // 2
    centers = [center_of(final, entering, pair, 2 * att_t.shape[1]).T for pair in range(half)]
    for side in range(2):
        group = range(side * half, (side + 1) * half)
        pqs = [phi_q[head, :, rows] for head in group]
        states = [(prefix[0, head] + keep * entering[(head + half) % heads]).astype(LOW) for head in group]
        scores = [
            nn(phi_k_nat[rows, head * feat : (head + 1) * feat], pq) for head, pq in zip(group, pqs)
        ]
        inter = [nn(state, pq) for state, pq in zip(states, pqs)]
        weights = [score.astype(LOW) * mask_now for score in scores]
        numers = [
            nn(v_ext[head, :, rows], weight) + reach * more
            for head, weight, more in zip(group, weights, inter)
        ]
        for head, numer in zip(group, numers):
            below = numer[width : width + 1] + padding
            denom[head : head + 1, rows] = below
            place = slice(head * width, (head + 1) * width)
            att = numer[:width] * (1.0 / below)
            att_t[place, rows] = att.astype(LOW)
            near = centers[head // 2][head % 2 * width : (head % 2 + 1) * width, :]
            att_c[place, :] = (att - jnp.concatenate([near] * (CHUNK // feat), axis=1)).astype(LOW)


def attend(aux, mask, phi_q, phi_k_nat, v_ext, prefix, final, entering, carry):
    heads, feat, rows = phi_q.shape
    width = feat // 2
    turned = kept_in_vmem((heads * width, rows), LOW)
    return call(
        attend_kernel,
        "attend",
        (rows // CHUNK,),
        [whole(aux), pl.BlockSpec((1, CHUNK, CHUNK), lambda c, *_: (c, 0, 0))]
        + [STAYS] * 3
        + [pl.BlockSpec((1, heads, EXT, feat), lambda c, *_: (c, 0, 0, 0))]
        + [whole(final), whole(entering)],
        [STAYS, pl.BlockSpec((heads * width, CHUNK), lambda c, *_: (0, c)), STAYS],
        (turned, streamed((heads * width, rows), LOW), kept_in_vmem((16, rows), F32)),
        [],
        8,
        1,
        (carry, aux, *apart(mask), *pinned(phi_q, phi_k_nat, v_ext), *apart(prefix, final, entering)),
        scalars=1,
    )


def mix_kernel(tokens, norms, w_own, w_oth, att_t, hidden, normed, normed_t):
    step = pl.program_id(0)
    rows = at(step, WIDE)
    att = att_t[:, rows].T
    part = att.shape[1] // 2
    total = tokens[...].astype(F32)
    total = total + nt(att[:, :part], w_own[:, part:]) + nt(att[:, part:], w_oth[:, part:])
    hidden[...] = total
    xhat, unused = norm_parts(total)
    low = (xhat * norms[2:3, :] + norms[3:4, :]).astype(LOW)
    normed[rows, :] = low
    normed_t[:, rows] = low.T


def mix(tokens, norms, w_own, w_oth, att_t):
    rows, dim = tokens.shape
    block = pl.BlockSpec((WIDE, dim), lambda c: (c, 0))
    return call(
        mix_kernel,
        "mix",
        (rows // WIDE,),
        [block, whole(norms), whole(w_own), whole(w_oth), STAYS],
        [block, STAYS, STAYS],
        (
            streamed((rows, dim), F32),
            kept_in_vmem((rows, dim), LOW),
            kept_in_vmem((dim, rows), LOW),
        ),
        [],
        12,
        1,
        (*apart(tokens), norms, w_own, w_oth, *pinned(att_t)),
    )


def feed_kernel(first, normed, normed_t, cot, cot_t, fc_in, down_in, *refs):
    feed, grad_normed = refs[:2] if first else refs[2:4]
    d_weights = refs[-1]
    fc = fc_in[...]
    down = down_in[...]
    units = fc.shape[1]
    u = nn(normed[...], fc)
    square = u * u
    t = jnp.tanh(u * (GELU_C + (GELU_C * GELU_A) * square))
    half = 0.5 + 0.5 * t
    act = (u * half).astype(LOW)
    slope = half + (0.5 * u) * (1.0 - t * t) * (GELU_C + (3.0 * GELU_C * GELU_A) * square)
    d_weights[:, units:] = nn(cot_t[...], act).astype(LOW)
    grad = (nn(cot[...], down) * slope).astype(LOW)
    d_weights[:, :units] = nn(normed_t[...], grad).astype(LOW)
    if first:
        feed[...] = nt(act, down)
        grad_normed[...] = nt(grad, fc)
    else:
        feed[...] += nt(act, down)
        grad_normed[...] += nt(grad, fc)


def feed_forward(normed, normed_t, cot, cot_t, weights, sums):
    rows, dim = normed.shape
    units = weights[0].shape[1]
    total = kept_in_vmem((rows, dim), F32)
    shared = (normed, normed_t, cot, cot_t)
    return call(
        functools.partial(feed_kernel, sums is None),
        "feed",
        (1,),
        [STAYS] * 6
        + ([] if sums is None else [STAYS] * 2),
        [STAYS] * 2 + [fixed(dim, 2 * units)],
        (total, total, jax.ShapeDtypeStruct((dim, 2 * units), LOW)),
        [],
        18,
        9,
        (
            *pinned(*shared),
            *pinned(*weights),
            *(() if sums is None else pinned(*sums)),
        ),
        alias=None if sums is None else {6: 0, 7: 1},
    )


def middle_kernel(
    hidden,
    feed,
    grad_normed,
    cot,
    norms,
    w_own,
    w_oth,
    att_t,
    att_c,
    denom,
    phi_q,
    aux,
    mixed,
    grad_hidden,
    d_gain,
    d_shift,
    g_ext,
    leaving,
    d_own,
    d_oth,
    branch_t,
    state,
):
    step = pl.program_id(0)
    count = pl.num_programs(0)
    heads, feat, unused = phi_q.shape
    width = feat // 2
    rows = at(step, CHUNK)
    hid = hidden[...]
    mixed[...] = (hid + feed[rows, :]).astype(LOW)
    xhat, rstd = norm_parts(hid)
    grad = grad_normed[rows, :]
    back = cot[rows, :].astype(F32) + norm_back(grad, xhat, rstd, norms[2:3, :])
    grad_hidden[...] = back

    @pl.when(step == 0)
    def _():
        d_gain[...] = jnp.zeros_like(d_gain)
        d_shift[...] = jnp.zeros_like(d_shift)
        state[...] = jnp.zeros_like(state)

    d_gain[...] += jnp.sum(grad * xhat, axis=0, keepdims=True)
    d_shift[...] += jnp.sum(grad, axis=0, keepdims=True)
    low = back.astype(LOW)
    branch_t[:, rows] = low.T
    reach = aux[2:3, rows].astype(LOW)
    first = lax.broadcasted_iota(jnp.int32, (16, CHUNK), 0) == 0
    part = heads * width // 2
    grad_att = [nn(low, weights[:, part:]) for weights in (w_own, w_oth)]
    turned = [
        piece[:, inner * feat : (inner + 1) * feat].T
        for piece in grad_att
        for inner in range(piece.shape[1] // feat)
    ]
    exts = []
    for head in range(heads):
        ga = turned[head // 2][head % 2 * width : (head % 2 + 1) * width]
        inverse = 1.0 / denom[head : head + 1, rows]
        centered = att_c[head * width : (head + 1) * width, :].astype(F32)
        gd = -jnp.sum(ga * centered, axis=0, keepdims=True) * inverse
        exts.append(
            jnp.concatenate([(ga * inverse).astype(LOW), jnp.where(first, gd, 0.0).astype(LOW)], axis=0)
        )
    more = [nt(ext * reach, phi_q[head, :, rows]) for head, ext in enumerate(exts)]
    for head in range(heads):
        g_ext[head, :, rows] = exts[head]
        state[head] += more[head]
    leaving[...] = state[...].astype(LOW)

    @pl.when(step == count - 1)
    def _():
        start = 0
        for out in (d_own, d_oth):
            size = out.shape[1]
            out[...] = nt(branch_t[...], att_t[start : start + size, :]).astype(LOW)
            start += size


def middle(hidden, feed, grad_normed, cot, norms, w_own, w_oth, att_t, att_c, denom, phi_q, aux):
    rows, dim = hidden.shape
    heads, feat, unused = phi_q.shape
    width = feat // 2
    part = heads * width // 2
    block = pl.BlockSpec((CHUNK, dim), lambda c, *_: (c, 0))
    return call(
        middle_kernel,
        "middle",
        (rows // CHUNK,),
        [block]
        + [STAYS] * 3
        + [whole(norms), whole(w_own), whole(w_oth)]
        + [STAYS, pl.BlockSpec((heads * width, CHUNK), lambda c, *_: (0, c)), STAYS, STAYS]
        + [whole(aux)],
        [block, block, fixed(1, dim), fixed(1, dim), STAYS, fixed(heads, EXT, feat)]
        + [fixed(dim, part)] * 2,
        (
            streamed((rows, dim), LOW),
            streamed((rows, dim), F32),
            jax.ShapeDtypeStruct((1, dim), F32),
            jax.ShapeDtypeStruct((1, dim), F32),
            kept_in_vmem((heads, EXT, rows), LOW),
            streamed((heads, EXT, feat), LOW),
        )
        + (jax.ShapeDtypeStruct((dim, part), LOW),) * 2,
        [pltpu.VMEM((dim, rows), LOW), pltpu.VMEM((heads, EXT, feat), F32)],
        20,
        13,
        (
            *apart(hidden),
            *pinned(feed, grad_normed, cot),
            norms,
            w_own,
            w_oth,
            *pinned(att_t),
            *apart(att_c),
            *pinned(denom, phi_q),
            aux,
        ),
    )


def attend_back_kernel(
    side,
    carry,
    kept,
    aux,
    mask,
    phi_q,
    phi_k,
    phi_k_nat,
    v_nat,
    v_ext,
    g_ext,
    prefix,
    final,
    entering,
    arriving,
    q_t,
    k_t,
    maps,
    grads,
    d_maps,
    state,
    d_fq,
    d_fk,
):
    step = pl.program_id(0)
    count = pl.num_programs(0)
    heads, feat, unused = phi_q.shape
    width = feat // 2
    part = heads * width // 2
    half = heads // 2
    chunk = count - 1 - step
    rows = at(chunk, CHUNK)
    keep_in = carry[chunk]
    keep = kept[chunk]
    reach = aux[0:1, rows].astype(LOW)
    written = aux[1:2, rows].astype(LOW)
    mask_now = mask[0]

    @pl.when(step == 0)
    def _():
        for head in range(half):
            state[head] = arriving[(1 - side) * half + head].astype(F32)
        d_fq[...] = jnp.zeros_like(d_fq)
        d_fk[...] = jnp.zeros_like(d_fk)

    locals_ = range(half)
    pairs = range(half // 2)
    centers = [center_of(final, entering, side * half // 2 + p, 2 * phi_q.shape[2]) for p in pairs]
    v_pairs = [
        (v_nat[:, p * feat : (p + 1) * feat].astype(F32) - centers[p][:1]).astype(LOW) for p in pairs
    ]
    columns = [center.T for center in centers]
    nears = [columns[n // 2][n % 2 * width : (n % 2 + 1) * width, :] for n in locals_]
    pqs = [phi_q[side * half + n, :, rows] for n in locals_]
    pks = [phi_k[n] for n in locals_]
    exts = [g_ext[side * half + n, :, rows] for n in locals_]
    scores = [
        nn(phi_k_nat[rows, (side * half + n) * feat : (side * half + n + 1) * feat], pqs[n]) for n in locals_
    ]
    blank = jnp.zeros((width, CHUNK), LOW)
    gws = []
    for n in locals_:
        numer = exts[n][:width]
        padded = jnp.concatenate([numer, blank] if n % 2 == 0 else [blank, numer], axis=0)
        gws.append(nn(v_pairs[n // 2], padded))
    weights = [score.astype(LOW) * mask_now for score in scores]
    gws = [
        (gw + ext[width : width + 1].astype(F32)).astype(LOW) * mask_now for gw, ext in zip(gws, exts)
    ]
    befores, values, afters, reached = [], [], [], []
    for n in locals_:
        before = prefix[0, n] + keep_in * entering[(1 - side) * half + n]
        befores.append(
            jnp.concatenate([before[:width] - nears[n] * before[width : width + 1], before[width:]], axis=0).astype(LOW)
        )
        value = v_ext[side * half + n, :, rows]
        near = jnp.concatenate([nears[n]] * (CHUNK // feat), axis=1)
        value = jnp.concatenate([(value[:width].astype(F32) - near).astype(LOW), value[width:]], axis=0)
        values.append(value * written)
        afters.append(state[n].astype(LOW))
        reached.append(exts[n] * reach)
    g_phi_q = [nn(pks[n], gws[n]) + tn(befores[n], reached[n]) for n in locals_]
    g_phi_k = [nt(pqs[n], gws[n]) + tn(afters[n], values[n]) for n in locals_]
    g_values = [
        nt(exts[n][:width], weights[n]) + nn(afters[n][:width], pks[n] * written) for n in locals_
    ]
    more = [nt(reached[n], pqs[n]) for n in locals_]
    grads_q = [softmax_pair_back(pqs[n], g_phi_q[n]).astype(LOW) for n in locals_]
    grads_k = [softmax_pair_back(pks[n], g_phi_k[n]).astype(LOW) for n in locals_]
    for n in locals_:
        state[n] = keep * state[n] + more[n]
    both = [[jnp.concatenate(g[2 * p : 2 * p + 2], axis=0) for p in pairs] for g in (grads_q, grads_k)]
    through = [[nn(maps[2 * kind, side * half // 2 + p], both[kind][p]) for p in pairs] for kind in range(2)]
    onto = [
        [nt(source[p * feat : (p + 1) * feat, :], both[kind][p]) for p in pairs]
        for kind, source in enumerate((q_t, k_t))
    ]
    for p in pairs:
        for kind in range(2):
            start = kind * part + p * feat
            grads[start : start + feat, rows] = through[kind][p].astype(LOW)
        start = 2 * part + p * feat
        grads[start : start + feat, rows] = jnp.concatenate(g_values[2 * p : 2 * p + 2], axis=0).astype(LOW)
        d_fq[p] += onto[0][p]
        d_fk[p] += onto[1][p]

    @pl.when(step == count - 1)
    def _():
        first = lax.broadcasted_iota(jnp.int32, (width, feat), 1) < width
        for kind, source in enumerate((d_fq, d_fk)):
            for local in range(half // 2):
                block = source[local]
                d_maps[kind, local] = jnp.where(first, block[:width], block[width:])


def attend_back(
    side, aux, mask, phi_q, phi_k, phi_k_nat, v_nat, v_ext, g_ext, prefix, final, entering, arriving, q_t, k_t, maps, carry, kept
):
    heads, feat, rows = phi_q.shape
    width = feat // 2
    half = heads // 2
    count = rows // CHUNK
    lanes = pl.BlockSpec((half * width, CHUNK), lambda c, *_: (side, count - 1 - c))
    return call(
        functools.partial(attend_back_kernel, side),
        "attend_back",
        (rows // CHUNK,),
        [
            whole(aux),
            pl.BlockSpec((1, CHUNK, CHUNK), lambda c, *_: (count - 1 - c, 0, 0)),
            STAYS,
            pl.BlockSpec((half, feat, CHUNK), lambda c, *_: (side, 0, count - 1 - c)),
            STAYS,
            pl.BlockSpec((CHUNK, half * width), lambda c, *_: (count - 1 - c, side)),
            STAYS,
            STAYS,
            pl.BlockSpec((1, half, EXT, feat), lambda c, *_: (count - 1 - c, side, 0, 0)),
            whole(final),
            whole(entering),
            whole(arriving),
            lanes,
            lanes,
            STAYS,
        ],
        [STAYS, fixed(2, half // 2, width, feat)],
        (kept_in_vmem((3 * half * width, rows), LOW), streamed((2, half // 2, width, feat), F32)),
        [pltpu.VMEM((half, EXT, feat), F32)] + [pltpu.VMEM((half // 2, feat, feat), F32)] * 2,
        10,
        14,
        (
            carry,
            kept,
            aux,
            *apart(mask),
            *pinned(phi_q),
            *apart(phi_k),
            *pinned(phi_k_nat),
            *apart(v_nat),
            *pinned(v_ext, g_ext),
            *apart(prefix, final, entering, arriving, q_t, k_t),
            *pinned(maps),
        ),
        scalars=2,
    )


def weight_kernel(normed_t, grads, out):
    out[...] = nt(normed_t[...], grads[...]).astype(LOW)


def weight_grads(normed_t, grads):
    dim, rows = normed_t.shape
    size = grads.shape[0]
    return call(
        weight_kernel,
        "weight_grads",
        (1,),
        [whole(normed_t), STAYS],
        fixed(dim, size),
        jax.ShapeDtypeStruct((dim, size), LOW),
        [],
        8,
        0,
        (*apart(normed_t), *pinned(grads)),
    )


def first_kernel(tokens, norms, grad_hidden, wa_own, wb_own, wa_oth, wb_oth, grads_own, grads_oth, out, d_gain, d_shift):
    step = pl.program_id(0)
    rows = at(step, CHUNK)
    total = None
    for wa, wb, grads in ((wa_own, wb_own, grads_own), (wa_oth, wb_oth, grads_oth)):
        cut = wa.shape[1]
        rest = grads.shape[0] - cut
        term = nn(wa[...], grads[:cut, rows]) + nn(wb[:, :rest], grads[cut:, rows])
        total = term if total is None else total + term
    grad = total.T
    xhat, rstd = norm_parts(tokens[...].astype(F32))
    out[...] = (grad_hidden[...] + norm_back(grad, xhat, rstd, norms[0:1, :])).astype(LOW)

    @pl.when(step == 0)
    def _():
        d_gain[...] = jnp.zeros_like(d_gain)
        d_shift[...] = jnp.zeros_like(d_shift)

    d_gain[...] += jnp.sum(grad * xhat, axis=0, keepdims=True)
    d_shift[...] += jnp.sum(grad, axis=0, keepdims=True)


def first_back(tokens, norms, grad_hidden, weights, grads):
    rows, dim = tokens.shape
    block = pl.BlockSpec((CHUNK, dim), lambda c: (c, 0))
    return call(
        first_kernel,
        "first_back",
        (rows // CHUNK,),
        [block, whole(norms), block] + [whole(w) for w in weights] + [STAYS] * 2,
        [block, fixed(1, dim), fixed(1, dim)],
        (
            streamed((rows, dim), LOW),
            jax.ShapeDtypeStruct((1, dim), F32),
            jax.ShapeDtypeStruct((1, dim), F32),
        ),
        [],
        16,
        9,
        (*apart(tokens), norms, *apart(grad_hidden), *weights, *pinned(*grads)),
    )


SWAP = [(0, 1), (1, 0)]


def swap(piece):
    return lax.ppermute(piece, "mp", SWAP)


def flip(piece, bit, size):
    return lax.ppermute(piece, "dp", [(i, i ^ bit) for i in range(size)])


def turn(piece, by, size):
    return lax.ppermute(piece, "dp", [(i, (i + by) % size) for i in range(size)])


def after(value, *others):
    return lax.optimization_barrier((value, *others))[0]


class Places:
    def __init__(self, size, staged):
        self.size = size
        self.deep = size // 4
        self.staged = staged
        place = lax.axis_index("dp")
        self.spots = jnp.stack([place % 2, (place // 2) % 2, place // 4, lax.axis_index("mp")])

    def flip(self, value, axis):
        return flip(value, 1 if axis == "x" else 2, self.size)


def line_kernel(cut, spots, *refs):
    deep = len(refs) - 2
    for s in range(deep):
        spot = lax.rem(spots[2] + deep - s, deep)
        refs[-2][spot] = refs[s][:, :cut]
        refs[-1][spot] = refs[s][:, cut:]


def gather_line(shard, cut, at, *others):
    return join_line(line_pieces(shard, at), cut, at, *others)


def line_pieces(shard, at):
    return [shard] + [turn(shard, 4 * s, at.size) for s in range(1, at.deep)]


def join_line(pieces, cut, at, *others):
    if others:
        pieces[1] = after(pieces[1], *others)
    rows, columns = pieces[0].shape
    shapes = [(at.deep, rows, cut), (at.deep, rows, columns - cut)]
    return call(
        functools.partial(line_kernel, cut),
        "line",
        (1,),
        [whole(p) for p in pieces],
        [fixed(*shape) for shape in shapes],
        tuple(jax.ShapeDtypeStruct(shape, LOW) for shape in shapes),
        [],
        6,
        0,
        (at.spots, *pieces),
        scalars=1,
    )


def pair_kernel(axes, dims, spots, *refs):
    for index, (axis, dim) in enumerate(zip(axes, dims)):
        mine, theirs, out = refs[2 * index], refs[2 * index + 1], refs[4 + index]
        bit = spots[0 if axis == "x" else 1]
        for source, place in ((mine, bit), (theirs, 1 - bit)):
            if dim == 1:
                out[:, pl.ds(place, 1)] = source[...][:, None]
            else:
                out[:, :, pl.ds(place, 1)] = source[...][:, :, None]


def first_by(shape):
    tail = (0,) * (len(shape) - 1)
    return pl.BlockSpec((1, *shape[1:]), lambda d, *_: (jnp.minimum(d, shape[0] - 1), *tail))


def gather_pair(values, axes, at, *others, kind=jax.ShapeDtypeStruct):
    moved = [at.flip(v, axis) for v, axis in zip(values, axes)]
    if others:
        moved[0] = after(moved[0], *others)
    dims = [v.ndim - 2 if axis == "x" else 1 for v, axis in zip(values, axes)]
    shapes = [(*v.shape[:d], 2, *v.shape[d:]) for v, d in zip(values, dims)]
    return call(
        functools.partial(pair_kernel, axes, dims),
        "pair",
        (at.deep,),
        [first_by(v.shape) for v in values for unused in (0, 1)],
        [first_by(shape) for shape in shapes],
        tuple(kind(shape, LOW) for shape in shapes),
        [],
        8,
        0,
        (at.spots, values[0], moved[0], values[1], moved[1]),
        scalars=1,
    )


def first_fold_kernel(axes, cuts, deep, spots, *refs):
    outs = refs[-4:]
    step = pl.program_id(0)
    if len(refs) == 5 + 2 * len(cuts):
        rider = refs[-5]
        rows = outs[0].shape[2]

        @pl.when(step == deep)
        def _():
            for index in range(rider.shape[0] // rows):
                group, place = divmod(index, 2)
                outs[0][0, place, :, group * 128 : (group + 1) * 128] = rider[index * rows : (index + 1) * rows, :]

        @pl.when(step < deep)
        def _():
            first_fold_step(axes, cuts, spots, refs, outs)

    else:
        first_fold_step(axes, cuts, spots, refs, outs)


def first_fold_step(axes, cuts, spots, refs, outs):
    for index, axis in enumerate(axes):
        bit = spots[0 if axis == "x" else 1]
        sent, kept = outs[2 * index : 2 * index + 2]
        start = 0
        for segment, cut in enumerate(cuts):
            pair = refs[2 * segment : 2 * segment + 2]
            columns = slice(0, cut) if index == 0 else slice(cut, pair[0].shape[-1])
            size = columns.stop - columns.start
            for out, place in ((sent, 1 - bit), (kept, bit)):
                if axis == "x":
                    terms = [r[:, :, pl.ds(place, 1), :, columns].astype(F32) for r in pair]
                else:
                    terms = [r[:, pl.ds(place, 1), :, :, columns].astype(F32) for r in pair]
                total = (terms[0] + terms[1]).astype(LOW)
                out[..., start : start + size] = total.reshape(*out.shape[:-1], size)
            start += size


def fold_kernel(axes, spots, *refs):
    for index, axis in enumerate(axes):
        bit = spots[0 if axis == "x" else 1]
        sent, kept = refs[4 + 2 * index : 6 + 2 * index]
        for out, place in ((sent, 1 - bit), (kept, bit)):
            terms = [r[:, pl.ds(place, 1)].astype(F32) for r in refs[2 * index : 2 * index + 2]]
            out[...] = (terms[0] + terms[1]).astype(LOW).reshape(out.shape)


def spread_kernel(spots, a_kept, a_sent, b_kept, b_sent, *outs):
    deep = len(outs)
    cut = a_kept.shape[-1]
    for s, out in enumerate(outs):
        spot = lax.rem(spots[2] + s, deep)
        out[:, :cut] = (a_kept[spot].astype(F32) + a_sent[spot].astype(F32)).astype(LOW)
        out[:, cut:] = (b_kept[spot].astype(F32) + b_sent[spot].astype(F32)).astype(LOW)


class Scatter:
    def __init__(self, segments, at):
        self.at = at
        self.cuts = [cut for own, oth, cut in segments]
        self.cut = sum(self.cuts)
        self.terms = [[own, swap(oth)] for own, oth, cut in segments]
        if at.staged:
            split = lambda v: v.reshape(at.deep, 2, 2, v.shape[0] // at.size, v.shape[1])
            self.terms = [[split(v) for v in pair] for pair in self.terms]

    def wait_for(self, *others):
        self.terms[0][1] = after(self.terms[0][1], *others)

    def fold(self, axes, rider=None):
        at = self.at
        flats = [v for pair in self.terms for v in pair]
        if not at.staged:
            return flats[0]
        if self.cuts:
            columns = sum(pair[0].shape[-1] for pair in self.terms)
            head = flats[0].shape[:2]
            rows = flats[0].shape[3]
            lefts = [(*head, rows, self.cut), (*head, rows, columns - self.cut)]
            kernel = functools.partial(first_fold_kernel, axes, tuple(self.cuts), at.deep)
        else:
            lefts = [(v.shape[0], *v.shape[2:]) for v in flats[::2]]
            kernel = functools.partial(fold_kernel, axes)
        outs = [left for left in lefts for unused in (0, 1)]
        extra = []
        steps = at.deep
        if rider is not None:
            extra = [rider]
            steps += 1
            outs[0] = (steps, *outs[0][1:])
        a_sent, a_kept, b_sent, b_kept = call(
            kernel,
            "fold",
            (steps,),
            [first_by(v.shape) for v in flats] + [whole(v) for v in extra],
            [first_by(left) for left in outs],
            tuple(jax.ShapeDtypeStruct(left, LOW) for left in outs),
            [],
            12,
            0,
            (at.spots, *flats, *extra),
            scalars=1,
        )
        self.cuts = []
        self.terms = [[a_kept, at.flip(a_sent, axes[0])], [b_kept, at.flip(b_sent, axes[1])]]
        return a_kept

    def spread(self):
        at = self.at
        if not at.staged:
            return self.terms[0][0]
        a, b = self.terms
        shape = (a[0].shape[1], self.cut + b[0].shape[-1])
        own, *sends = call(
            spread_kernel,
            "spread",
            (1,),
            [whole(v) for v in (*a, *b)],
            [fixed(*shape)] * at.deep,
            (jax.ShapeDtypeStruct(shape, LOW),) * at.deep,
            [],
            8,
            0,
            (at.spots, *a, *b),
            scalars=1,
        )
        self.parts = [own] + [turn(p, 4 * s, at.size) for s, p in enumerate(sends, 1)]
        return own

    def end(self, *others):
        if not self.at.staged:
            sums = [own.astype(F32) + moved.astype(F32) for own, moved in self.terms]
            total = [t[:, :cut] for t, cut in zip(sums, self.cuts)] + [t[:, cut:] for t, cut in zip(sums, self.cuts)]
            total = lax.psum_scatter(jnp.concatenate(total, axis=1), "dp", scatter_dimension=0, tiled=True)
        else:
            if others:
                self.parts[1] = after(self.parts[1], *others)
            total = sum(p.astype(F32) for p in self.parts)
        return total


def ride_kernel(deep, spots, *refs):
    a_kept, a_moved, b_kept, b_moved, gain1, shift1, gain2, shift2, maps, early = refs[:10]
    late = refs[10 : 10 + deep]
    a_sent, a_left, b_sent, b_left, norm_low, maps_low, g_fc, g_down, g_out = refs[10 + deep :]
    rows = a_left.shape[1]
    units = early.shape[1] // 2
    total = late[0][...].astype(F32)
    for part in late[1:]:
        total = total + part[...].astype(F32)
    rest = total.shape[1] - 2 * units
    cut = units + (rest // 128 + 1) // 2 * 128
    g_fc[:, :units] = early[:, :units]
    g_down[:, :units] = early[:, units:]
    g_fc[:, units:] = total[:, :units]
    g_down[:, units:] = total[:, cut : cut + units]
    g_out[:, : cut - units] = total[:, units:cut]
    g_out[:, cut - units :] = total[:, cut + units :]
    blank = jnp.zeros((4, gain1.shape[1]), F32)
    norm_now = jnp.concatenate([gain1[...], shift1[...], gain2[...], shift2[...], blank], axis=0)
    norm_low[...] = jnp.concatenate([norm_now, jnp.zeros_like(norm_now)], axis=0).astype(LOW)
    for index in range(maps.shape[0] // rows):
        group, place = divmod(index, 2)
        moved = a_moved[deep, place, :, group * 128 : (group + 1) * 128].astype(F32)
        here = slice(index * rows, (index + 1) * rows)
        maps_low[here, :] = (maps[here, :].astype(F32) + moved).astype(LOW)
    for kept, moved, sent, left, bit in (
        (a_kept, a_moved, a_sent, a_left, spots[1]),
        (b_kept, b_moved, b_sent, b_left, spots[0]),
    ):
        columns = left.shape[2]
        for out, place in ((sent, 1 - bit), (left, bit)):
            terms = [r[:deep, pl.ds(place, 1)].astype(F32) for r in (kept, moved)]
            total = (terms[0] + terms[1]).astype(LOW)
            if out is left:
                out[...] = total.reshape(deep, rows, columns)
            else:
                out[: deep * rows] = total.reshape(deep * rows, columns)
        rest = norm_now[:, columns:]
        rest = jnp.concatenate([rest, jnp.zeros((8, columns - rest.shape[1]), F32)], axis=1)
        sent[deep * rows :] = jnp.concatenate([norm_now[:, :columns], rest], axis=0).astype(LOW)


def last_spread_kernel(spots, a_kept, a_moved, b_kept, b_moved, norm, norm_far, maps, maps_moved, *outs):
    *parts, maps_low = outs
    deep, rows, cut = a_kept.shape
    dim = norm.shape[1]
    maps_low[...] = (maps[...].astype(F32) + maps_moved[...].astype(F32)).astype(LOW)
    near = []
    for moved in (b_moved, a_moved):
        columns = moved.shape[1]
        tail = moved[deep * rows :].astype(F32)
        near.append(jnp.concatenate([tail[:8], tail[8:, : dim - columns]], axis=1))
    plane = (norm[...].astype(F32)[:8] + near[0]) + (near[1] + norm_far[...].astype(F32)[:8])
    tail = jnp.concatenate([plane[:, i : i + 128] for i in range(0, dim, 128)], axis=0)
    for s, out in enumerate(parts):
        spot = lax.rem(spots[2] + s, deep)
        place = pl.ds(pl.multiple_of(spot * rows, rows), rows)
        rest = out.shape[1] - 128
        out[:, :cut] = (a_kept[spot].astype(F32) + a_moved[place].astype(F32)).astype(LOW)
        out[:, cut:rest] = (b_kept[spot].astype(F32) + b_moved[place].astype(F32)).astype(LOW)
        out[:, rest:] = tail.astype(LOW)


def finish_kernel(spots, *refs):
    deep = len(refs) - 9
    parts = refs[:deep]
    maps, maps_moved, g_query, g_key, g_value, norms, map_q, map_k, held = refs[deep:]
    rows, part = g_query.shape
    total = None
    for s, ref in enumerate(parts):
        value = ref[...].astype(F32)
        held[lax.rem(spots[2] + deep - s, deep)] = value[:, 3 * part :]
        total = value if total is None else total + value
    for index, out in enumerate((g_query, g_key, g_value)):
        out[...] = total[:, index * part : (index + 1) * part]
    together = held[0]
    for spot in range(1, deep):
        together = together + held[spot]
    for index in range(rows // 8):
        norms[:, index * 128 : (index + 1) * 128] = together[index * 8 : (index + 1) * 8]
    width = map_q.shape[1]
    both = maps[...].astype(F32) + maps_moved[...].astype(F32)
    heads = map_q.shape[0]
    for kind, out in enumerate((map_q, map_k)):
        for pair in range(heads // 2):
            start = (kind * heads // 2 + pair) * width
            block = both[start : start + width]
            out[2 * pair] = block[:, :width]
            out[2 * pair + 1] = block[:, width:]


def finish_last(sums, norm, map_grads, early, late, part, heads, width, at):
    small = lambda shape, kind: jax.ShapeDtypeStruct(shape, kind)
    (a_kept, a_moved), (b_kept, b_moved) = sums.terms
    deep, unused, rows, cut = a_kept.shape
    rest = b_kept.shape[3]
    dim = norm[0].shape[1]
    units = early.shape[1]
    ins = (a_kept, a_moved, b_kept, b_moved, *norm, map_grads, early, *late)
    outs = (
        small((deep * rows + 16, cut), LOW),
        small((deep, rows, cut), LOW),
        small((deep * rows + 16, rest), LOW),
        small((deep, rows, rest), LOW),
        small((16, dim), LOW),
        small(map_grads.shape, LOW),
        small((rows, units), F32),
        small((rows, units), F32),
        small((rows, part), F32),
    )

    def run(kernel, name, ins, outs, scratch):
        return call(
            kernel,
            name,
            (1,),
            [whole(v) for v in ins],
            [fixed(*out.shape) for out in outs],
            outs,
            scratch,
            12,
            0,
            (at.spots, *ins),
            scalars=1,
        )

    kernel = functools.partial(ride_kernel, deep)
    a_sent, a_kept, b_sent, b_kept, norm_low, maps, *done = run(kernel, "ride", ins, outs, [])
    across = [(i, i ^ 3) for i in range(at.size)]
    ins = (
        a_kept,
        at.flip(a_sent, "y"),
        b_kept,
        at.flip(b_sent, "x"),
        norm_low,
        lax.ppermute(norm_low, "dp", across),
        maps,
        flip(maps, 4 << (at.size.bit_length() - 4), at.size),
    )
    ins = lax.optimization_barrier(ins)
    outs = (small((rows, cut + rest + 128), LOW),) * deep + (small(map_grads.shape, LOW),)
    own, *sends, maps = run(last_spread_kernel, "last_spread", ins, outs, [])
    ins = (own, *(turn(p, 4 * s, at.size) for s, p in enumerate(sends, 1)), maps, at.flip(maps, "y"))
    ins = lax.optimization_barrier(ins)
    outs = (
        (small((rows, part), F32),) * 3
        + (small((8, dim), F32),)
        + (small((heads // 2, width, width), F32),) * 2
    )
    return done, run(finish_kernel, "finish", ins, outs, [pltpu.VMEM((deep, rows, 128), F32)])


def add_along(value, steps, size):
    for step in steps:
        if step < size:
            value = value.astype(LOW)
            value = value.astype(F32) + flip(value, step, size).astype(F32)
    return value


def per_device(
    size,
    tokens,
    norm1_gain,
    norm1_shift,
    w_query,
    w_key,
    w_value,
    w_out,
    fmap_query,
    fmap_key,
    norm2_gain,
    norm2_shift,
    w_fc,
    w_down,
    lengths,
    cotangent,
):
    rows, dim = tokens.shape
    heads = 2 * fmap_query.shape[0]
    width = fmap_query.shape[1]
    feat = 2 * width
    part = w_query.shape[1]
    count = rows // CHUNK
    core = lax.axis_index("mp")
    staged = size % 4 == 0 and dim // size % 16 == 0
    where = Places(size, staged)
    units = w_fc.shape[1] // 2
    cut = (3 * part // feat + 1) // 2 * feat
    cut_out = (part // feat + 1) // 2 * feat
    shard_qkv, shard_early, shard_late = pack(
        (w_query, w_key, w_value, w_out, w_fc, w_down),
        (
            ((0, 0, part), (1, 0, part), (2, 0, part), (3, 0, part)),
            ((4, 0, units), (5, 0, units)),
            ((4, units, units), (5, units, units)),
        ),
    )
    fq_oth, fk_oth = swap(fmap_query), swap(fmap_key)
    if staged:
        qkv = gather_line(shard_qkv, 2 * part, where)
        lengths = after(lengths, qkv[0])

    ends = jnp.cumsum(lengths[0])
    places = core * rows - 1 + jnp.arange(rows + 1, dtype=jnp.int32)
    numbers = jnp.sum((ends[None, :] <= places[:, None]).astype(jnp.int32), axis=1)
    numbers = jnp.where(places < 0, -1, numbers)
    segment = numbers[1:]
    living = places[1:] < ends[-1]
    blocks = segment.reshape(count, CHUNK)
    last = blocks[:, -1]
    before = jnp.concatenate([numbers[:1], last[:-1]])
    kept = (last == before).astype(F32)
    carry = ((before == numbers[0]) & (core > 0)).astype(F32)
    reach = (blocks == before[:, None]).reshape(rows) & living
    written = (blocks == last[:, None]).reshape(rows)
    reach_in = (segment == numbers[0]) & living
    aux = jnp.stack([reach, written, reach_in, ~living] + [jnp.zeros_like(living)] * 4).astype(F32)
    order = jnp.arange(CHUNK, dtype=jnp.int32)
    mask = (
        (blocks[:, :, None] == blocks[:, None, :])
        & (order[:, None] <= order[None, :])
        & living.reshape(count, 1, CHUNK)
    ).astype(LOW)

    norms = jnp.stack([norm1_gain, norm1_shift, norm2_gain, norm2_shift])

    norms, aux, mask, kept, carry = lax.optimization_barrier((norms, aux, mask, kept, carry))
    if staged:
        qkv = gather_pair(qkv, "xy", where)
        shard_early, tokens = after(shard_early, qkv[0]), after(tokens, qkv[0], mask)
    normed1, normed1_t, cot_t, maps = prepare(
        tokens, cotangent, norms, fmap_query, fq_oth, fmap_key, fk_oth
    )
    if staged:
        pieces = line_pieces(shard_early, where)
        pieces[1], maps = lax.optimization_barrier((pieces[1], maps))
        qkv = gather_pair(qkv, "yx", where, *pieces[1:], maps)
        early = join_line(pieces, units, where, qkv[0])
        qkv = tuple(map(flat, qkv))
        normed1, shard_late = after(normed1, early[0]), after(shard_late, early[0])
    else:
        qkv, early, late = (
            tuple(lax.all_gather(s, "dp", axis=0, tiled=True) for s in (shard[:, :at_], shard[:, at_:]))
            for shard, at_ in ((shard_qkv, 2 * part), (shard_early, units), (shard_late, units))
        )
    qkv = (*qkv, *map(swap, qkv))
    q_t, k_t, v_nat, v_ext, phi_q, phi_k, phi_k_nat, prefix, final = project(
        normed1, *qkv, maps, aux, kept, heads, width
    )
    if staged:
        early = gather_pair(early, "xy", where, final)
        final = after(final, early[0])
    entering = swap(final)
    att_t, att_c, denom = attend(aux, mask, phi_q, phi_k_nat, v_ext, prefix, final, entering, carry)
    if staged:
        late = gather_line(shard_late, units, where, denom)
        att_t = after(att_t, late[0])
    hidden, normed2, normed2_t = mix(tokens, norms, qkv[1], qkv[3], att_t)
    if staged:
        early = tuple(map(flat, gather_pair(early, "yx", where, normed2_t)))
    early_oth = tuple(map(swap, early))
    shared = (normed2, normed2_t, cotangent, cot_t)
    cot = cotangent
    feed, grad_normed, d_early_oth = feed_forward(*shared, early_oth, None)
    if staged:
        late = gather_pair(late, "xy", where, d_early_oth)
        feed = after(feed, late[0])
    feed, grad_normed, d_early_own = feed_forward(*shared, early, (feed, grad_normed))
    sums_early = Scatter([(d_early_own, d_early_oth, units)], where)
    if staged:
        late = tuple(map(flat, gather_pair(late, "yx", where, d_early_own)))
    late_oth = tuple(map(swap, late))
    feed = after(feed, sums_early.fold("xy"))
    feed, grad_normed, d_late_own = feed_forward(*shared, late, (feed, grad_normed))
    feed, grad_normed, d_late_oth = feed_forward(*shared, late_oth, (feed, grad_normed))
    sums_early.wait_for(d_late_oth)
    hidden = after(hidden, sums_early.fold("yx"))
    mixed, grad_hidden, d_gain2, d_shift2, g_ext, leaving, d_out_own, d_out_oth = middle(
        hidden, feed, grad_normed, cot, norms, qkv[1], qkv[3], att_t, att_c, denom, phi_q, aux
    )
    sums_early.wait_for(d_gain2)
    started = sums_early.spread()
    arriving = lax.ppermute(after(leaving, started), "mp", [(1, 0)])
    d_out_oth = after(d_out_oth, started)
    sums_late = Scatter([(d_late_own, d_late_oth, units), (d_out_own, d_out_oth, cut_out)], where)
    sums_late.wait_for(started)
    arriving = after(arriving, sums_late.fold("xy"))
    back = functools.partial(
        attend_back, carry=carry, kept=kept, prefix=prefix, final=final, entering=entering, q_t=q_t, k_t=k_t, maps=maps
    )
    back_inputs = (aux, mask, phi_q, phi_k, phi_k_nat, v_nat, v_ext, g_ext)
    lanes = lambda v: v.reshape(-1, feat)
    grads_oth, maps_oth = back(1, *back_inputs, arriving=arriving)
    total_early = sums_early.end(maps_oth)
    d_qkv_oth = weight_grads(normed1_t, after(grads_oth, total_early))
    sums_late.wait_for(d_qkv_oth)
    arriving = after(arriving, sums_late.fold("yx"))
    grads_own, maps_own = back(0, *back_inputs, arriving=arriving)
    sums_late.wait_for(maps_own)
    grads_own = after(grads_own, sums_late.spread())
    map_grads = lanes(maps_own + swap(maps_oth))
    d_qkv_own = weight_grads(normed1_t, grads_own)
    if staged:
        map_grads = map_grads.astype(LOW)
        for step in [4 << i for i in range(size.bit_length() - 4)]:
            moved = after(flip(map_grads, step, size), d_qkv_own)
            map_grads = (map_grads.astype(F32) + moved.astype(F32)).astype(LOW)
    sums_qkv = Scatter([(d_qkv_own, d_qkv_oth, cut)], where)
    grad_hidden = after(grad_hidden, sums_qkv.fold("xy", map_grads if staged else None))
    grad_tokens, d_gain1, d_shift1 = first_back(tokens, norms, grad_hidden, qkv, (grads_own, grads_oth))
    norm_grads = (d_gain1, d_shift1, d_gain2, d_shift2)
    if staged:
        sums_qkv.wait_for(d_gain1)
        done, (g_query, g_key, g_value, norm_grads, map_q, map_k) = finish_last(
            sums_qkv, norm_grads, map_grads, total_early, sums_late.parts, part, heads, width, where
        )
        g_fc, g_down, g_out = done
    else:
        total_late = sums_late.end()
        grad_qkv = sums_qkv.end()
        g_query, g_key, g_value = (grad_qkv[:, i * part : (i + 1) * part] for i in range(3))
        norm_grads, map_grads = lax.psum((jnp.concatenate(norm_grads, axis=0), map_grads), "dp")
        map_grads = map_grads.reshape(2, heads // 4, width, 2, width)
        map_q, map_k = map_grads.swapaxes(2, 3).reshape(2, heads // 2, width, width)
        cut_late = units + cut_out
        g_fc = jnp.concatenate([total_early[:, :units], total_late[:, :units]], axis=1)
        g_down = jnp.concatenate([total_early[:, units:], total_late[:, cut_late : cut_late + units]], axis=1)
        g_out = jnp.concatenate([total_late[:, units:cut_late], total_late[:, cut_late + units :]], axis=1)
    norm_grads = norm_grads + swap(norm_grads)
    return (
        mixed,
        grad_tokens,
        norm_grads[0],
        norm_grads[1],
        g_query,
        g_key,
        g_value,
        g_out,
        map_q,
        map_k,
        norm_grads[2],
        norm_grads[3],
        g_fc,
        g_down,
    )


def solution(mesh):
    placed = (
        P(("dp", "mp"), None),
        P(),
        P(),
        P("dp", "mp"),
        P("dp", "mp"),
        P("dp", "mp"),
        P("dp", "mp"),
        P("mp", None, None),
        P("mp", None, None),
        P(),
        P(),
        P("dp", "mp"),
        P("dp", "mp"),
        P("dp", None),
        P(("dp", "mp"), None),
    )
    return jax.shard_map(
        functools.partial(per_device, mesh.shape["dp"]),
        mesh=mesh,
        in_specs=placed,
        out_specs=(
            P(("dp", "mp"), None),
            P(("dp", "mp"), None),
            P(),
            P(),
            P("dp", "mp"),
            P("dp", "mp"),
            P("dp", "mp"),
            P("dp", "mp"),
            P("mp", None, None),
            P("mp", None, None),
            P(),
            P(),
            P("dp", "mp"),
            P("dp", "mp"),
        ),
        check_vma=False,
    )
```
